32 devices in a mesh: dp: 8 (over y, x, core), tensor: 4 (over z).
Axes of the slice: x: 2, y: 2, z: 4, core: 2. Of those that a mesh axis runs over, the one named last changes fastest.
Arguments:
- raw_series: bfloat16 [2, 32, 1024, 144], P(None, ('dp', 'tensor')), may hold values from -6 to 6
- median_code: int32 [2, 32], P(None, ('dp', 'tensor')), may hold values from -20 to 20
- scale_code: int32 [2, 32], P(None, ('dp', 'tensor')), may hold values from 2 to 8
- qkv_weight: bfloat16 [144, 432], replicated, may hold values from -0.5 to 0.5
- out_weight: bfloat16 [144, 144], replicated, may hold values from -2 to 2
- attn_gain: float32 [144], replicated, may hold values from 0.5 to 1.5
- gate_weight: bfloat16 [144, 512], P(None, 'tensor'), may hold values from -0.5 to 0.5
- up_weight: bfloat16 [144, 512], P(None, 'tensor'), may hold values from -0.5 to 0.5
- down_weight: bfloat16 [512, 144], P('tensor'), may hold values from -0.25 to 0.25
- mlp_gain: float32 [144], replicated, may hold values from 0.5 to 1.5
- cotangent: bfloat16 [2, 32, 1024, 144], P(None, ('dp', 'tensor')), may hold values from -6 to 6
Outputs:
- result: bfloat16 [2, 32, 1024, 144], P(None, ('dp', 'tensor'))
- input_grad: float32 [2, 32, 1024, 144], P(None, ('dp', 'tensor'))
- qkv_grad: float32 [144, 432], replicated
- out_grad: float32 [144, 144], replicated
- attn_gain_grad: float32 [144], replicated
- gate_grad: float32 [144, 512], P(None, 'tensor')
- up_grad: float32 [144, 512], P(None, 'tensor')
- down_grad: float32 [512, 144], P('tensor')
- mlp_gain_grad: float32 [144], replicated
The draws below stay inside these ranges and needn't reach their ends.
All inputs are finite; a program needn't handle non-finite values.
Results may differ from the reference program's by a relative error of at most 0.009.
Values may be sent and summed in bfloat16 or wider, within the bound.
A program may use at most 128 MiB of HBM per device.

```python
import jax
import jax.numpy as jnp
from jax import lax

D = 144
HEADS = 9
HEAD_DIM = 16
FF = 512
LEN = 1024
MB = 2
SERIES = 32


def place_ends(entries, stream_key, smallest, high):
    longest = entries.shape.index(max(entries.shape))
    spots = []
    for shift in (0, 1):
        where = [jax.random.randint(jax.random.fold_in(stream_key, axis), (), 0, length) for axis, length in enumerate(entries.shape)]
        where[longest] = (where[longest] + shift) % entries.shape[longest]
        spots.append(tuple(where))
    return entries.at[spots[0]].set(smallest).at[spots[1]].set(high)


def block_levels(rng, dims, shards, smallest, top_value):
    def one(dim, blocks):
        draws = jax.random.uniform(jax.random.fold_in(jax.random.fold_in(rng, 6), dim), (blocks,), jnp.float32, smallest / len(shards), top_value / len(shards))
        return jnp.repeat(jnp.exp(draws), dims[dim] // blocks).reshape((-1,) + (1,) * (len(dims) - dim - 1))

    loudness = one(*shards[0])
    for cut in shards[1:]:
        loudness = loudness * one(*cut)
    return loudness


def scatter_about(own_key, extent, spread, limit, split=(), kind=jnp.bfloat16):
    loudness = block_levels(own_key, extent, split, -0.22, 0.18) if split else 1.0
    entries = jax.random.normal(own_key, extent, jnp.float32) * spread * loudness
    return jnp.minimum(jnp.maximum(entries, -limit), limit).astype(kind)


def setup_inputs(seed: int = 0) -> dict:
    key_list = jax.random.split(jax.random.key(seed), 12)
    raw_series = scatter_about(key_list[0], (MB, SERIES, LEN, D), 1.0, 6.0, ((1, 32),))
    median_code = place_ends(jax.random.randint(key_list[1], (MB, SERIES), -20, 21), jax.random.fold_in(key_list[1], 1), -20, 20).astype(jnp.int32)
    scale_code = place_ends(jax.random.randint(key_list[2], (MB, SERIES), 2, 9), jax.random.fold_in(key_list[2], 1), 2, 8).astype(jnp.int32)
    qkv_weight = scatter_about(key_list[3], (D, 3 * D), D ** -0.5, 0.5)
    out_weight = scatter_about(key_list[4], (D, D), (D // 16) ** -0.5, 2.0)
    attn_gain = jnp.clip(1.0 + 0.1 * jax.random.normal(key_list[5], (D,), jnp.float32), 0.5, 1.5)
    gate_weight = scatter_about(key_list[6], (D, FF), D ** -0.5, 0.5, ((1, 4),))
    up_weight = scatter_about(key_list[7], (D, FF), D ** -0.5, 0.5, ((1, 4),))
    down_weight = scatter_about(key_list[8], (FF, D), FF ** -0.5, 0.25, ((0, 4),))
    mlp_gain = jnp.clip(1.0 + 0.1 * jax.random.normal(key_list[9], (D,), jnp.float32), 0.5, 1.5)
    cotangent = scatter_about(key_list[10], (MB, SERIES, LEN, D), 1.0, 6.0, ((1, 32),))
    return dict(raw_series=raw_series, median_code=median_code, scale_code=scale_code, qkv_weight=qkv_weight, out_weight=out_weight, attn_gain=attn_gain, gate_weight=gate_weight, up_weight=up_weight, down_weight=down_weight, mlp_gain=mlp_gain, cotangent=cotangent)


@jax.custom_vjp
def low(v):
    return lax.optimization_barrier(v.astype(jnp.bfloat16)).astype(jnp.float32)

@jax.custom_vjp
def low_back(v):
    return v

def low_keep(v):
    return (low(v), None)

def low_pass(kept, grad):
    return (grad,)

def back_keep(v):
    return (v, None)

def back_low(kept, grad):
    return (low(grad),)
low.defvjp(low_keep, low_pass)
low_back.defvjp(back_keep, back_low)
highest = lax.Precision.HIGHEST
epsilon = 1e-05
masked_value = -1e+30

def rope_tables(length, head_width):
    half_width = head_width // 2
    frequency = 10000.0 ** (-(jnp.arange(half_width, dtype=jnp.float32) * 2.0 / head_width))
    angles = jnp.arange(length, dtype=jnp.float32)[:, None] * frequency[None, :]
    return (jnp.cos(angles), jnp.sin(angles))

def rotate(values, cosine, sine_table):
    half_width = values.shape[-1] // 2
    first_half = values[..., :half_width]
    second_half = values[..., half_width:]
    return jnp.concatenate([first_half * cosine - second_half * sine_table, first_half * sine_table + second_half * cosine], axis=-1)

def norm_apply(inputs, gain):
    return inputs * lax.rsqrt(lax.optimization_barrier(jnp.mean(inputs * inputs, axis=-1, keepdims=True)) + epsilon) * gain

def attend_series(operands):
    queries, keys_rot, values_in = operands
    length = queries.shape[1]
    scores = low_back(jnp.einsum('hqd,hkd->hqk', queries, keys_rot, precision=highest) * HEAD_DIM ** (-0.5))
    query_pos = lax.broadcasted_iota(jnp.int32, (length, length), 0)
    key_pos = lax.broadcasted_iota(jnp.int32, (length, length), 1)
    masked = jnp.where(key_pos <= query_pos, scores, masked_value)
    largest = lax.optimization_barrier(jnp.max(masked, axis=-1, keepdims=True))
    weights = jnp.exp(masked - largest)
    probs = low(weights / lax.optimization_barrier(jnp.sum(weights, axis=-1, keepdims=True)))
    return jnp.einsum('hqk,hkd->hqd', probs, values_in, precision=highest)

def layer_forward(raw_rows, shifts, spreads, params):
    qkv_weight, out_weight, attn_gain, gate_weight, up_weight, down_weight, mlp_gain = params
    groups, length, model_width = raw_rows.shape
    scaled_series = (raw_rows - shifts[:, None, None]) / spreads[:, None, None]
    attn_rows = low(norm_apply(scaled_series, attn_gain))
    projected = jnp.dot(attn_rows.reshape(-1, model_width), qkv_weight, precision=highest, preferred_element_type=jnp.float32)
    projected = projected.reshape(groups, length, 3, HEADS, HEAD_DIM).transpose(2, 0, 3, 1, 4)
    cosine, sine_table = rope_tables(length, HEAD_DIM)
    queries = low(rotate(low_back(projected[0]), cosine, sine_table))
    keys_rot = low(rotate(low_back(projected[1]), cosine, sine_table))
    values_in = low(low_back(projected[2]))
    attended = lax.map(jax.checkpoint(attend_series), (queries, keys_rot, values_in))
    attended = low(low_back(attended))
    attended_flat = attended.transpose(0, 2, 1, 3).reshape(-1, model_width)
    attn_branch = low_back(jnp.dot(attended_flat, out_weight, precision=highest, preferred_element_type=jnp.float32))
    hidden = scaled_series + attn_branch.reshape(groups, length, model_width)
    mlp_rows = low(norm_apply(hidden, mlp_gain)).reshape(-1, model_width)
    gate = low_back(jnp.dot(mlp_rows, gate_weight, precision=highest, preferred_element_type=jnp.float32))
    upper = low_back(jnp.dot(mlp_rows, up_weight, precision=highest, preferred_element_type=jnp.float32))
    inner = low(gate * (1.0 / (1.0 + jnp.exp(-gate))) * upper)
    mlp_branch = low_back(jnp.dot(inner, down_weight, precision=highest, preferred_element_type=jnp.float32))
    return hidden + mlp_branch.reshape(groups, length, model_width)

def reference(raw_series, median_code, scale_code, qkv_weight, out_weight, attn_gain, gate_weight, up_weight, down_weight, mlp_gain, cotangent):
    group_size = 4
    full_shape = raw_series.shape
    length = full_shape[2]
    model_width = full_shape[3]
    raw_groups = raw_series.astype(jnp.float32).reshape(-1, group_size, length, model_width)
    shift_groups = (median_code.astype(jnp.float32) * 0.05).reshape(-1, group_size)
    spread_groups = (scale_code.astype(jnp.float32) * 0.25).reshape(-1, group_size)
    cotan_groups = cotangent.astype(jnp.float32).reshape(-1, group_size, length, model_width)
    params = tuple((weight.astype(jnp.float32) for weight in (qkv_weight, out_weight, attn_gain, gate_weight, up_weight, down_weight, mlp_gain)))

    def one_group(totals, operands):
        raw_rows, shifts, spreads, upstream = operands

        def forward(raw_input, weights):
            return layer_forward(raw_input, shifts, spreads, weights)
        outputs, pullback = jax.vjp(forward, raw_rows, params)
        input_grad, param_grads = pullback(upstream)
        totals = jax.tree.map(lambda running, addend: running + addend, totals, param_grads)
        return (totals, (outputs.astype(jnp.bfloat16), input_grad))
    initial = tuple((jnp.zeros(weight.shape, jnp.float32) for weight in params))
    totals, (results, input_grads) = lax.scan(one_group, initial, (raw_groups, shift_groups, spread_groups, cotan_groups))
    return (results.reshape(full_shape), input_grads.reshape(full_shape), totals[0], totals[1], totals[2], totals[3], totals[4], totals[5], totals[6])
```

```python
import functools

import jax
import jax.numpy as jnp
import numpy as np
from jax import lax
from jax.experimental import pallas as pl
from jax.experimental.pallas import tpu as pltpu
from jax.sharding import PartitionSpec as P

BF = jnp.bfloat16
F32 = jnp.float32
HEADS = 9
HEAD_DIM = 16
D = HEADS * HEAD_DIM
BLK = 256
EPS = 1e-05
MASKED = -1e30
LOG2E_SCALED = 0.25 * 1.4426950408889634


def mm(a, b):
    return lax.dot_general(a, b, (((1,), (0,)), ((), ())), preferred_element_type=F32)


def mm_tn(a, b):
    return lax.dot_general(a, b, (((0,), (0,)), ((), ())), preferred_element_type=F32)


def mm_nt(a, b):
    return lax.dot_general(a, b, (((1,), (1,)), ((), ())), preferred_element_type=F32)


def eye(n, dtype):
    same = lax.broadcasted_iota(jnp.int32, (n, n), 0) == lax.broadcasted_iota(jnp.int32, (n, n), 1)
    return jnp.where(same, 1.0, 0.0).astype(dtype)


def to_column(row):
    n = row.shape[1]
    return jnp.sum(eye(n, F32) * row, axis=1, keepdims=True)


def to_row(column):
    n = column.shape[0]
    return jnp.sum(eye(n, F32) * column, axis=0, keepdims=True)


def norm_stats(rows):
    r = lax.rsqrt(jnp.mean(rows * rows, axis=0, keepdims=True) + EPS)
    return rows * r, r


def norm_backward(e, n, r, gain):
    weighted = e * gain
    mean = jnp.mean(weighted * n, axis=0, keepdims=True)
    return r * (weighted - n * mean), jnp.sum(e * n, axis=1, keepdims=True)


def rope(x, cosine, sine, sign):
    length = x.shape[1]
    x = x.reshape(HEADS, 2, 8, length)
    a, b = x[:, 0], x[:, 1]
    s = sine * sign
    first = a * cosine - b * s
    second = a * s + b * cosine
    return jnp.concatenate([first[:, None], second[:, None]], axis=1).reshape(HEADS, HEAD_DIM, length)


def kernel(
    median_ref, scale_ref, raw_ref, cot_ref, qkv_ref, out_ref, again_ref, gu_ref, down_ref, mgain_ref, cos_ref, sin_ref,
    result_ref, igrad_ref, qkvg_ref, outg_ref, againg_ref, gug_ref, downg_ref, mgaing_ref,
    e_ref, ds_ref, qa_ref, q_ref, k_ref, v_ref, o_ref, linv_ref, att_ref, datt_ref, dproj_ref, rows_ref, scaled_ref, dh_ref,
):
    length = raw_ref.shape[2]
    series = raw_ref.shape[0]
    slots = gu_ref.shape[0]
    nblk = length // BLK
    cosine, sine = cos_ref[...], sin_ref[...]
    again, mgain = to_column(again_ref[...]), to_column(mgain_ref[...])

    def spread_inverse(s):
        return 1.0 / jnp.full((1, length), scale_ref[s, 0].astype(F32) * 0.25, F32)

    ident = eye(D, BF)
    tail_rows = lax.broadcasted_iota(jnp.int32, (HEAD_DIM, length), 0)

    @pl.loop(0, series)
    def _(s):
        shift = median_ref[s, 0].astype(F32) * 0.05
        scaled = (mm_nt(ident, raw_ref[s, 0]) - shift) * spread_inverse(s)
        scaled_ref[s] = scaled
        n, _ = norm_stats(scaled)
        rows = (n * again).astype(BF)
        rows_ref[s] = rows
        projected = mm_tn(qkv_ref[...], rows)
        queries = rope(projected[:D], cosine, sine, 1.0).astype(BF)
        keys = rope(projected[D : 2 * D], cosine, sine, 1.0).astype(BF)
        values = projected[2 * D :].reshape(HEADS, HEAD_DIM, length).astype(BF)
        q_ref[s] = queries
        k_ref[s] = keys
        wide = queries.astype(F32) * LOG2E_SCALED
        high = wide.astype(BF)
        qa_ref[s, :, :HEAD_DIM] = high
        qa_ref[s, :, HEAD_DIM:] = (wide - high.astype(F32)).astype(BF)
        v_ref[s, :, :HEAD_DIM] = values
        ones = jnp.where(tail_rows < 2, 1.0, 0.0).astype(BF)
        v_ref[s, :, HEAD_DIM:] = jnp.broadcast_to(ones[None], (HEADS, HEAD_DIM, length))

    causal = lax.broadcasted_iota(jnp.int32, (BLK, BLK), 0) <= lax.broadcasted_iota(jnp.int32, (BLK, BLK), 1)

    def offset(j):
        return BLK * (j * (j + 1) // 2)

    @pl.loop(0, series)
    def _(s):
        @pl.loop(0, HEADS)
        def _(h):
            keys = k_ref[s, h]
            keys2 = jnp.concatenate([keys, keys], axis=0)
            for j in range(nblk):
                lo, hi = j * BLK, (j + 1) * BLK
                scores = mm_tn(keys2[:, :hi], qa_ref[s, h, :, lo:hi])
                diagonal = jnp.where(causal, scores[lo:], MASKED)
                scores = jnp.concatenate([scores[:lo], diagonal], axis=0) if j else diagonal
                largest = jnp.max(scores, axis=0, keepdims=True)
                e_ref[s * HEADS + h, offset(j) : offset(j) + hi] = jnp.exp2(scores - largest).astype(BF)
            for j in range(nblk):
                lo, hi = j * BLK, (j + 1) * BLK
                mixed = mm(v_ref[s, h, :, :hi], e_ref[s * HEADS + h, offset(j) : offset(j) + hi])
                inverse = 1.0 / mixed[HEAD_DIM : HEAD_DIM + 1]
                attended = mixed[:HEAD_DIM] * inverse
                linv_ref[s, h, :, lo:hi] = inverse
                o_ref[s, h, :, lo:hi] = attended
                att_ref[s, h, :, lo:hi] = attended.astype(BF)

    @pl.loop(0, series)
    def _(s):
        attended = att_ref[s].reshape(D, length)
        hidden = scaled_ref[s] + mm_tn(out_ref[...], attended)
        n, r = norm_stats(hidden)
        rows = (n * mgain).astype(BF)
        top = mm_nt(ident, cot_ref[s, 0])
        low = top.astype(BF)
        result = hidden
        grad_rows = jnp.zeros((D, length), F32)
        for t in range(slots):
            gu = gu_ref[t]
            both = mm_tn(gu, rows)
            half = both.shape[0] // 2
            gate, up = both[:half], both[half:]
            grad_inner = mm(down_ref[t], low)
            sigma = 1.0 / (1.0 + jnp.exp(-gate))
            act = gate * sigma
            inner = (act * up).astype(BF)
            grad_gate = (grad_inner * up * (sigma + act * (1.0 - sigma))).astype(BF)
            grad_up = (grad_inner * act).astype(BF)
            grad_both = jnp.concatenate([grad_gate, grad_up], axis=0)
            result = result + mm_tn(down_ref[t], inner)
            grad_rows = grad_rows + mm(gu, grad_both)
            gu_piece = mm_nt(rows, grad_both)
            down_piece = mm_nt(inner, low)

            @pl.when(s == 0)
            def _():
                gug_ref[t] = gu_piece
                downg_ref[t] = down_piece

            @pl.when(s != 0)
            def _():
                gug_ref[t] += gu_piece
                downg_ref[t] += down_piece

        result_ref[s, 0] = result.T.astype(BF)
        part, gain_part = norm_backward(grad_rows, n, r, mgain)
        grad_hidden = top + part
        dh_ref[s] = grad_hidden
        branch = grad_hidden.astype(BF)
        out_piece = mm_nt(attended, branch)
        gain_row = to_row(gain_part)
        datt_ref[s] = mm(out_ref[...], branch).astype(BF).reshape(HEADS, HEAD_DIM, length)

        @pl.when(s == 0)
        def _():
            outg_ref[...] = out_piece
            mgaing_ref[...] = gain_row

        @pl.when(s != 0)
        def _():
            outg_ref[...] += out_piece
            mgaing_ref[...] += gain_row

    @pl.loop(0, series)
    def _(s):
        @pl.loop(0, HEADS)
        def _(h):
            grad = (datt_ref[s, h].astype(F32) * linv_ref[s, h]).astype(BF)
            delta = -jnp.sum(grad.astype(F32) * o_ref[s, h], axis=0, keepdims=True)
            high = delta.astype(BF).astype(F32)
            tail = jnp.where(tail_rows == 0, high, jnp.where(tail_rows == 1, delta - high, 0.0))
            grad_all = jnp.concatenate([grad, tail.astype(BF)], axis=0)
            values = v_ref[s, h]
            queries, keys = q_ref[s, h], k_ref[s, h]
            for j in range(nblk):
                lo, hi = j * BLK, (j + 1) * BLK
                weights = e_ref[s * HEADS + h, offset(j) : offset(j) + hi]
                centred = mm_tn(values[:, :hi], grad_all[:, lo:hi])
                ds_ref[offset(j) : offset(j) + hi] = centred.astype(BF) * weights
            value_grads, key_grads, query_grads = [], [], []
            for j in range(nblk):
                lo, hi = j * BLK, (j + 1) * BLK
                query_grads.append(mm(keys[:, :hi], ds_ref[offset(j) : offset(j) + hi]))
            for i in range(nblk):
                value_grad = key_grad = None
                for j in range(i, nblk):
                    at = offset(j) + i * BLK
                    cols = slice(j * BLK, (j + 1) * BLK)
                    piece = mm_nt(grad[:, cols], e_ref[s * HEADS + h, at : at + BLK])
                    value_grad = piece if value_grad is None else value_grad + piece
                    piece = mm_nt(queries[:, cols], ds_ref[at : at + BLK])
                    key_grad = piece if key_grad is None else key_grad + piece
                value_grads.append(value_grad)
                key_grads.append(key_grad)

            def unrotate(g):
                a, b = g[:8], g[8:]
                return jnp.concatenate([a * cosine + b * sine, b * cosine - a * sine], axis=0)

            query_grad = jnp.concatenate(query_grads, axis=1) * 0.25
            key_grad = jnp.concatenate(key_grads, axis=1) * 0.25
            dproj_ref[s, h] = unrotate(query_grad).astype(BF)
            dproj_ref[s, HEADS + h] = unrotate(key_grad).astype(BF)
            dproj_ref[s, 2 * HEADS + h] = jnp.concatenate(value_grads, axis=1).astype(BF)

    @pl.loop(0, series)
    def _(s):
        grad = dproj_ref[s].reshape(3 * D, length)
        qkv_piece = mm_nt(rows_ref[s], grad)
        grad_rows = mm(qkv_ref[...], grad)
        n, r = norm_stats(scaled_ref[s])
        part, gain_part = norm_backward(grad_rows, n, r, again)
        igrad_ref[s, 0] = ((dh_ref[s] + part) * spread_inverse(s)).T
        gain_row = to_row(gain_part)

        @pl.when(s == 0)
        def _():
            qkvg_ref[...] = qkv_piece
            againg_ref[...] = gain_row

        @pl.when(s != 0)
        def _():
            qkvg_ref[...] += qkv_piece
            againg_ref[...] += gain_row


def rope_tables(length):
    half = HEAD_DIM // 2
    frequency = np.float32(10000.0) ** (-(np.arange(half, dtype=np.float32) * np.float32(2.0) / np.float32(HEAD_DIM)))
    angles = np.arange(length, dtype=np.float32)[None, :] * frequency.astype(np.float32)[:, None]
    return np.cos(angles).astype(np.float32), np.sin(angles).astype(np.float32)


def layer(median_code, scale_code, raw, cot, qkv, out, again, gu, down, mgain):
    series, _, length, width = raw.shape
    slots, _, pair = gu.shape
    cosine, sine = rope_tables(length)
    packed = BLK * (length // BLK) * (length // BLK + 1) // 2
    vmem = pl.BlockSpec(memory_space=pltpu.VMEM)
    smem = pl.BlockSpec(memory_space=pltpu.SMEM)
    per_head = (series, HEADS, HEAD_DIM, length)
    return pl.pallas_call(
        kernel,
        out_shape=[
            jax.ShapeDtypeStruct(raw.shape, BF),
            jax.ShapeDtypeStruct(raw.shape, F32),
            jax.ShapeDtypeStruct((width, 3 * width), F32),
            jax.ShapeDtypeStruct((width, width), F32),
            jax.ShapeDtypeStruct((1, width), F32),
            jax.ShapeDtypeStruct((slots, width, pair), F32),
            jax.ShapeDtypeStruct((slots, pair // 2, width), F32),
            jax.ShapeDtypeStruct((1, width), F32),
        ],
        in_specs=[smem, smem] + [vmem] * 10,
        out_specs=[vmem] * 8,
        scratch_shapes=[
            pltpu.VMEM((series * HEADS, packed, BLK), BF),
            pltpu.VMEM((packed, BLK), BF),
            pltpu.VMEM((series, HEADS, 2 * HEAD_DIM, length), BF),
            pltpu.VMEM(per_head, BF),
            pltpu.VMEM(per_head, BF),
            pltpu.VMEM((series, HEADS, 2 * HEAD_DIM, length), BF),
            pltpu.VMEM(per_head, F32),
            pltpu.VMEM((series, HEADS, 1, length), F32),
            pltpu.VMEM(per_head, BF),
            pltpu.VMEM(per_head, BF),
            pltpu.VMEM((series, 3 * HEADS, HEAD_DIM, length), BF),
            pltpu.VMEM((series, width, length), BF),
            pltpu.VMEM((series, width, length), F32),
            pltpu.VMEM((series, width, length), F32),
        ],
        compiler_params=pltpu.CompilerParams(vmem_limit_bytes=60 * 2**20),
    )(median_code, scale_code, raw, cot, qkv, out, again.reshape(1, -1), gu, down, mgain.reshape(1, -1), cosine, sine)


def local(raw_series, median_code, scale_code, qkv_weight, out_weight, attn_gain, gate_weight, up_weight, down_weight, mlp_gain, cotangent):
    gu = lax.all_gather(jnp.concatenate([gate_weight, up_weight], axis=1), "tensor")
    down = lax.all_gather(down_weight, "tensor")
    result, input_grad, qkv_grad, out_grad, again_grad, gu_grad, down_grad, mgain_grad = layer(
        median_code, scale_code, raw_series, cotangent, qkv_weight, out_weight, attn_gain, gu, down, mlp_gain
    )
    qkv_grad, out_grad, again_grad, mgain_grad = lax.psum((qkv_grad, out_grad, again_grad, mgain_grad), ("dp", "tensor"))
    gu_grad = lax.psum_scatter(gu_grad, "tensor", scatter_dimension=0, tiled=False)
    down_grad = lax.psum_scatter(down_grad, "tensor", scatter_dimension=0, tiled=False)
    gu_grad, down_grad = lax.psum((gu_grad, down_grad), "dp")
    half = gu_grad.shape[1] // 2
    return (
        result, input_grad, qkv_grad, out_grad, again_grad[0], gu_grad[:, :half], gu_grad[:, half:], down_grad, mgain_grad[0],
    )


def solution(mesh):
    placed = (
        P(None, ("dp", "tensor"), None, None), P(None, ("dp", "tensor")), P(None, ("dp", "tensor")), P(), P(), P(),
        P(None, "tensor"), P(None, "tensor"), P("tensor", None), P(), P(None, ("dp", "tensor"), None, None),
    )
    return jax.shard_map(
        local, mesh=mesh, in_specs=placed,
        out_specs=(
            P(None, ("dp", "tensor"), None, None), P(None, ("dp", "tensor"), None, None), P(), P(), P(),
            P(None, "tensor"), P(None, "tensor"), P("tensor", None), P(),
        ),
        check_vma=False,
    )
```

```python
import functools

import jax
import jax.numpy as jnp
import numpy as np
from jax import lax
from jax.experimental import pallas as pl
from jax.experimental.pallas import tpu as pltpu
from jax.sharding import PartitionSpec as P

BF = jnp.bfloat16
F32 = jnp.float32
HEADS = 9
HEAD_DIM = 16
D = HEADS * HEAD_DIM
BLK = 256
EPS = 1e-05
MASKED = -1e30
EARLY = 7
FF_AT = 4
MESH = pl.DeviceIdType.MESH
LOG2E_SCALED = 0.25 * 1.4426950408889634


def mm(a, b):
    return lax.dot_general(a, b, (((1,), (0,)), ((), ())), preferred_element_type=F32)


def mm_tn(a, b):
    return lax.dot_general(a, b, (((0,), (0,)), ((), ())), preferred_element_type=F32)


def mm_nt(a, b):
    return lax.dot_general(a, b, (((1,), (1,)), ((), ())), preferred_element_type=F32)


def eye(n, dtype):
    same = lax.broadcasted_iota(jnp.int32, (n, n), 0) == lax.broadcasted_iota(jnp.int32, (n, n), 1)
    return jnp.where(same, 1.0, 0.0).astype(dtype)


def to_column(row):
    n = row.shape[1]
    return jnp.sum(eye(n, F32) * row, axis=1, keepdims=True)


def to_row(column):
    n = column.shape[0]
    return jnp.sum(eye(n, F32) * column, axis=0, keepdims=True)


def norm_stats(rows):
    r = lax.rsqrt(jnp.mean(rows * rows, axis=0, keepdims=True) + EPS)
    return rows * r, r


def norm_backward(e, n, r, gain):
    weighted = e * gain
    mean = jnp.mean(weighted * n, axis=0, keepdims=True)
    return r * (weighted - n * mean), jnp.sum(e * n, axis=1, keepdims=True)


def rope(x, cosine, sine, sign):
    length = x.shape[1]
    x = x.reshape(HEADS, 2, 8, length)
    a, b = x[:, 0], x[:, 1]
    s = sine * sign
    first = a * cosine - b * s
    second = a * s + b * cosine
    return jnp.concatenate([first[:, None], second[:, None]], axis=1).reshape(HEADS, HEAD_DIM, length)


def group_owner_reduce(index, count, stage, recv, out, send_sem, recv_sem, spread_sem, gather_sem, to):
    groups = stage.shape[0]

    def part(owner):
        return pltpu.make_async_remote_copy(
            src_ref=stage.at[owner], dst_ref=recv.at[lax.rem(owner - index + count, count) - 1],
            send_sem=send_sem.at[owner], recv_sem=recv_sem, device_id=to(owner), device_id_type=MESH,
        )

    def whole(k):
        return pltpu.make_async_remote_copy(
            src_ref=out.at[index], dst_ref=out.at[index], send_sem=spread_sem, recv_sem=gather_sem.at[index],
            device_id=to(lax.rem(index + k, count)), device_id_type=MESH,
        )

    def each_other_owner(body):
        @pl.loop(0, groups)
        def _(owner):
            @pl.when(owner != index)
            def _():
                body(owner)

    def send():
        each_other_owner(lambda owner: part(owner).start())

    def reduce():
        @pl.when(index < groups)
        def _():
            pltpu.make_async_remote_copy(
                src_ref=recv, dst_ref=recv, send_sem=spread_sem, recv_sem=recv_sem, device_id=to(index), device_id_type=MESH,
            ).wait_recv()
            total = stage[index].astype(F32) + jnp.sum(recv[...].astype(F32), axis=0)
            out[index] = total.astype(BF)

            @pl.loop(1, count)
            def _(k):
                whole(k).start()

    def finish():
        def landed(owner):
            pltpu.make_async_remote_copy(
                src_ref=out.at[owner], dst_ref=out.at[owner], send_sem=spread_sem, recv_sem=gather_sem.at[owner],
                device_id=to(owner), device_id_type=MESH,
            ).wait_recv()

        each_other_owner(landed)
        each_other_owner(lambda owner: part(owner).wait_send())

        @pl.when(index < groups)
        def _():
            pltpu.make_async_remote_copy(
                src_ref=recv, dst_ref=recv, send_sem=spread_sem, recv_sem=recv_sem, device_id=to(index), device_id_type=MESH,
            ).wait_send()

    return send, reduce, finish


def kernel(
    n_dp, n_t,
    median_ref, scale_ref, raw_ref, cot_ref, qkv_ref, out_ref, again_ref, gate_ref, up_ref, down_ref, mgain_ref, cos_ref, sin_ref,
    result_ref, igrad_ref, qkvg_ref, outg_ref, againg_ref, gateg_ref, upg_ref, downg_ref, mgaing_ref,
    e_ref, ds_ref, qa_ref, q_ref, k_ref, v_ref, o_ref, linv_ref, att_ref, datt_ref, dproj_ref, rows_ref, scaled_ref, dh_ref,
    w_ref, ffacc_ref, ffstage_ref, ffrecv_ref, ffout_ref, outacc_ref,
    estage_ref, erecv_ref, eout_ref, lstage_ref, lrecv_ref, lout_ref, gains_ref,
    w_send, w_recv, ff_send, ff_recv, ff_spread, ff_gather,
    e_send, e_recv, e_spread, e_gather, l_send, l_recv, l_spread, l_gather,
):
    length = raw_ref.shape[3]
    series = raw_ref.shape[0]
    nblk = length // BLK
    hidden_local = gate_ref.shape[1]
    count = n_dp * n_t
    my_dp, my_t = lax.axis_index("dp"), lax.axis_index("tensor")
    index = my_dp * n_t + my_t

    def to(device):
        return (device // n_t, lax.rem(device, n_t))

    barrier = pltpu.get_barrier_semaphore()

    @pl.loop(1, count)
    def _(k):
        pl.semaphore_signal(barrier, inc=1, device_id=to(lax.rem(index + k, count)), device_id_type=MESH)

    cosine, sine = cos_ref[...], sin_ref[...]
    again, mgain = to_column(again_ref[...]), to_column(mgain_ref[...])

    def spread_inverse(s):
        return 1.0 / jnp.full((1, length), scale_ref[0, s].astype(F32) * 0.25, F32)

    tail_rows = lax.broadcasted_iota(jnp.int32, (HEAD_DIM, length), 0)

    @pl.loop(0, series)
    def _(s):
        shift = median_ref[0, s].astype(F32) * 0.05
        scaled = (raw_ref[s, 0].astype(F32) - shift) * spread_inverse(s)
        scaled_ref[s] = scaled
        n, _ = norm_stats(scaled)
        rows = (n * again).astype(BF)
        rows_ref[s] = rows
        projected = mm_tn(qkv_ref[...], rows)
        queries = rope(projected[:D], cosine, sine, 1.0).astype(BF)
        keys = rope(projected[D : 2 * D], cosine, sine, 1.0).astype(BF)
        values = projected[2 * D :].reshape(HEADS, HEAD_DIM, length).astype(BF)
        q_ref[s] = queries
        k_ref[s] = keys
        wide = queries.astype(F32) * LOG2E_SCALED
        high = wide.astype(BF)
        qa_ref[s, :, :HEAD_DIM] = high
        qa_ref[s, :, HEAD_DIM:] = (wide - high.astype(F32)).astype(BF)
        v_ref[s, :, :HEAD_DIM] = values
        ones = jnp.where(tail_rows < 2, 1.0, 0.0).astype(BF)
        v_ref[s, :, HEAD_DIM:] = jnp.broadcast_to(ones[None], (HEADS, HEAD_DIM, length))

    w_ref[0, :, :hidden_local] = gate_ref[...]
    w_ref[0, :, hidden_local : 2 * hidden_local] = up_ref[...]
    w_ref[0, :, 2 * hidden_local :] = down_ref[...]
    pl.semaphore_wait(barrier, count - 1)

    def weights(k):
        return pltpu.make_async_remote_copy(
            src_ref=w_ref.at[0], dst_ref=w_ref.at[k], send_sem=w_send.at[k], recv_sem=w_recv.at[k],
            device_id=(my_dp, lax.rem(my_t + k, n_t)), device_id_type=MESH,
        )

    for k in range(1, n_t):
        weights(k).start()

    causal = lax.broadcasted_iota(jnp.int32, (BLK, BLK), 0) <= lax.broadcasted_iota(jnp.int32, (BLK, BLK), 1)

    def offset(j):
        return BLK * (j * (j + 1) // 2)

    @pl.loop(0, series)
    def _(s):
        @pl.loop(0, HEADS)
        def _(h):
            keys = k_ref[s, h]
            keys2 = jnp.concatenate([keys, keys], axis=0)
            for j in range(nblk):
                lo, hi = j * BLK, (j + 1) * BLK
                scores = mm_tn(keys2[:, :hi], qa_ref[s, h, :, lo:hi])
                diagonal = jnp.where(causal, scores[lo:], MASKED)
                scores = jnp.concatenate([scores[:lo], diagonal], axis=0) if j else diagonal
                largest = jnp.max(scores, axis=0, keepdims=True)
                e_ref[s * HEADS + h, offset(j) : offset(j) + hi] = jnp.exp2(scores - largest).astype(BF)
            for j in range(nblk):
                lo, hi = j * BLK, (j + 1) * BLK
                mixed = mm(v_ref[s, h, :, :hi], e_ref[s * HEADS + h, offset(j) : offset(j) + hi])
                inverse = 1.0 / mixed[HEAD_DIM : HEAD_DIM + 1]
                attended = mixed[:HEAD_DIM] * inverse
                linv_ref[s, h, :, lo:hi] = inverse
                o_ref[s, h, :, lo:hi] = attended
                att_ref[s, h, :, lo:hi] = attended.astype(BF)

    for k in range(1, n_t):
        weights(k).wait()

    ffacc_ref[...] = jnp.zeros_like(ffacc_ref)
    outacc_ref[...] = jnp.zeros_like(outacc_ref)
    gains_ref[...] = jnp.zeros_like(gains_ref)

    @pl.loop(0, series)
    def _(s):
        attended = att_ref[s].reshape(D, length)
        hidden = scaled_ref[s] + mm_tn(out_ref[...], attended)
        n, r = norm_stats(hidden)
        rows = (n * mgain).astype(BF)
        low = cot_ref[s, 0]
        top = low.astype(F32)
        result = hidden
        grad_rows = jnp.zeros((D, length), F32)
        for t in range(n_t):
            gu = w_ref[t, :, : 2 * hidden_local]
            down = w_ref[t, :, 2 * hidden_local :]
            both = mm_tn(gu, rows)
            gate, up = both[:hidden_local], both[hidden_local:]
            grad_inner = mm_tn(down, low)
            sigma = 1.0 / (1.0 + jnp.exp(-gate))
            act = gate * sigma
            inner = (act * up).astype(BF)
            grad_gate = (grad_inner * up * (sigma + act * (1.0 - sigma))).astype(BF)
            grad_up = (grad_inner * act).astype(BF)
            grad_both = jnp.concatenate([grad_gate, grad_up], axis=0)
            result = result + mm(down, inner)
            grad_rows = grad_rows + mm(gu, grad_both)
            gu_piece = mm_nt(rows, grad_both)
            ffacc_ref[t, :D] += gu_piece[:, :hidden_local]
            ffacc_ref[t, D : 2 * D] += gu_piece[:, hidden_local:]
            ffacc_ref[t, 2 * D : 3 * D] += mm_nt(low, inner)

        result_ref[s, 0] = result.astype(BF)
        part, gain_part = norm_backward(grad_rows, n, r, mgain)
        grad_hidden = top + part
        dh_ref[s] = grad_hidden
        branch = grad_hidden.astype(BF)
        outacc_ref[...] += mm_nt(attended, branch)
        gains_ref[0:1] += to_row(gain_part)
        datt_ref[s] = mm(out_ref[...], branch).astype(BF).reshape(HEADS, HEAD_DIM, length)

    ffstage_ref[...] = ffacc_ref[...].astype(BF).reshape(ffstage_ref.shape)

    def ff_part(k):
        peer = lax.rem(index + k, count)
        peer_dp, peer_t = peer // n_t, lax.rem(peer, n_t)
        return pltpu.make_async_remote_copy(
            src_ref=ffstage_ref.at[lax.rem(my_t - peer_t + n_t, n_t), peer_dp], dst_ref=ffrecv_ref.at[k - 1],
            send_sem=ff_send.at[k - 1], recv_sem=ff_recv, device_id=(peer_dp, peer_t), device_id_type=MESH,
        )

    def ff_whole(k):
        return pltpu.make_async_remote_copy(
            src_ref=ffout_ref.at[my_dp], dst_ref=ffout_ref.at[my_dp], send_sem=ff_spread.at[k - 1], recv_sem=ff_gather,
            device_id=(lax.rem(my_dp + k, n_dp), my_t), device_id_type=MESH,
        )

    @pl.loop(1, count)
    def _(k):
        ff_part(k).start()

    def ff_reduce():
        pltpu.make_async_remote_copy(
            src_ref=ffrecv_ref, dst_ref=ffrecv_ref, send_sem=ff_spread.at[0], recv_sem=ff_recv, device_id=to(index),
            device_id_type=MESH,
        ).wait_recv()
        total = ffstage_ref[0, my_dp].astype(F32) + jnp.sum(ffrecv_ref[...].astype(F32), axis=0)
        ffout_ref[my_dp] = total.astype(BF)

        @pl.loop(1, n_dp)
        def _(k):
            ff_whole(k).start()

    def ff_finish():
        others = ffout_ref.at[pl.ds(0, n_dp - 1)]
        pltpu.make_async_remote_copy(
            src_ref=others, dst_ref=others, send_sem=ff_spread.at[0], recv_sem=ff_gather, device_id=to(index),
            device_id_type=MESH,
        ).wait_recv()

        @pl.loop(1, count)
        def _(k):
            ff_part(k).wait_send()

        @pl.loop(1, n_dp)
        def _(k):
            ff_whole(k).wait_send()

    e_go, e_reduce, e_finish = group_owner_reduce(
        index, count, estage_ref, erecv_ref, eout_ref, e_send, e_recv, e_spread, e_gather, to
    )
    l_go, l_reduce, l_finish = group_owner_reduce(
        index, count, lstage_ref, lrecv_ref, lout_ref, l_send, l_recv, l_spread, l_gather, to
    )

    def head_grads(first, last):
        total = None
        for s in range(series):
            parts = [dproj_ref[s, c * HEADS + first : c * HEADS + last] for c in range(3)]
            grads = jnp.concatenate(parts, axis=0).reshape(3 * (last - first) * HEAD_DIM, length)
            piece = mm_nt(grads, rows_ref[s])
            total = piece if total is None else total + piece
        return total.astype(BF).reshape(3 * (last - first), HEAD_DIM, D)

    def gain_group(row):
        first = lax.broadcasted_iota(jnp.int32, (HEAD_DIM, D), 0) == 0
        return jnp.where(first, jnp.broadcast_to(row, (HEAD_DIM, D)), 0.0).astype(BF)

    @pl.loop(0, HEADS)
    def _(h):
        @pl.loop(0, series)
        def _(s):
            grad = (datt_ref[s, h].astype(F32) * linv_ref[s, h]).astype(BF)
            delta = -jnp.sum(grad.astype(F32) * o_ref[s, h], axis=0, keepdims=True)
            high = delta.astype(BF).astype(F32)
            tail = jnp.where(tail_rows == 0, high, jnp.where(tail_rows == 1, delta - high, 0.0))
            grad_all = jnp.concatenate([grad, tail.astype(BF)], axis=0)
            values = v_ref[s, h]
            queries, keys = q_ref[s, h], k_ref[s, h]
            for j in range(nblk):
                lo, hi = j * BLK, (j + 1) * BLK
                weights = e_ref[s * HEADS + h, offset(j) : offset(j) + hi]
                centred = mm_tn(values[:, :hi], grad_all[:, lo:hi])
                ds_ref[offset(j) : offset(j) + hi] = centred.astype(BF) * weights
            value_grads, key_grads, query_grads = [], [], []
            for j in range(nblk):
                lo, hi = j * BLK, (j + 1) * BLK
                query_grads.append(mm(keys[:, :hi], ds_ref[offset(j) : offset(j) + hi]))
            for i in range(nblk):
                value_grad = key_grad = None
                for j in range(i, nblk):
                    at = offset(j) + i * BLK
                    cols = slice(j * BLK, (j + 1) * BLK)
                    piece = mm_nt(grad[:, cols], e_ref[s * HEADS + h, at : at + BLK])
                    value_grad = piece if value_grad is None else value_grad + piece
                    piece = mm_nt(queries[:, cols], ds_ref[at : at + BLK])
                    key_grad = piece if key_grad is None else key_grad + piece
                value_grads.append(value_grad)
                key_grads.append(key_grad)

            def unrotate(g):
                a, b = g[:8], g[8:]
                return jnp.concatenate([a * cosine + b * sine, b * cosine - a * sine], axis=0)

            query_grad = jnp.concatenate(query_grads, axis=1) * 0.25
            key_grad = jnp.concatenate(key_grads, axis=1) * 0.25
            dproj_ref[s, h] = unrotate(query_grad).astype(BF)
            dproj_ref[s, HEADS + h] = unrotate(key_grad).astype(BF)
            dproj_ref[s, 2 * HEADS + h] = jnp.concatenate(value_grads, axis=1).astype(BF)

        @pl.when(h == FF_AT)
        def _():
            ff_reduce()

        @pl.when(h == EARLY - 1)
        def _():
            estage_ref[0 : 3 * EARLY] = head_grads(0, EARLY)
            estage_ref[3 * EARLY : 3 * EARLY + HEADS] = outacc_ref[...].astype(BF).reshape(HEADS, HEAD_DIM, D)
            estage_ref[3 * EARLY + HEADS] = gain_group(gains_ref[0:1])
            e_go()

    late = 3 * (HEADS - EARLY)
    lstage_ref[0:late] = head_grads(EARLY, HEADS)

    @pl.loop(0, series)
    def _(s):
        grad = dproj_ref[s].reshape(3 * D, length)
        grad_rows = mm(qkv_ref[...], grad)
        n, r = norm_stats(scaled_ref[s])
        part, gain_part = norm_backward(grad_rows, n, r, again)
        igrad_ref[s, 0] = (dh_ref[s] + part) * spread_inverse(s)
        gains_ref[8:9] += to_row(gain_part)

    lstage_ref[late] = gain_group(gains_ref[8:9])
    l_go()
    e_reduce()
    l_reduce()
    ff_finish()
    ffout = ffout_ref[...].astype(F32).reshape(-1, hidden_local)
    gateg_ref[...] = ffout[:D]
    upg_ref[...] = ffout[D : 2 * D]
    downg_ref[...] = ffout[2 * D : 3 * D]
    e_finish()
    outg_ref[...] = eout_ref[3 * EARLY : 3 * EARLY + HEADS].reshape(D, D).astype(F32)
    mgaing_ref[...] = eout_ref[3 * EARLY + HEADS].astype(F32)[0:1]
    l_finish()
    againg_ref[...] = lout_ref[late].astype(F32)[0:1]
    parts = []
    for c in range(3):
        parts.append(eout_ref[c * EARLY : (c + 1) * EARLY].reshape(EARLY * HEAD_DIM, D))
        parts.append(lout_ref[c * (HEADS - EARLY) : (c + 1) * (HEADS - EARLY)].reshape((HEADS - EARLY) * HEAD_DIM, D))
    qkvg_ref[...] = jnp.concatenate(parts, axis=0).astype(F32).T


def rope_tables(length):
    half = HEAD_DIM // 2
    frequency = np.float32(10000.0) ** (-(np.arange(half, dtype=np.float32) * np.float32(2.0) / np.float32(HEAD_DIM)))
    angles = np.arange(length, dtype=np.float32)[None, :] * frequency.astype(np.float32)[:, None]
    return np.cos(angles).astype(np.float32), np.sin(angles).astype(np.float32)


def layer(n_dp, n_t, median_code, scale_code, raw, cot, qkv, out, again, gate, up, down, mgain):
    series, _, width, length = raw.shape
    cosine, sine = rope_tables(length)
    blocks = length // BLK
    packed = BLK * blocks * (blocks + 1) // 2
    vmem = pl.BlockSpec(memory_space=pltpu.VMEM)
    smem = pl.BlockSpec(memory_space=pltpu.SMEM)
    per_head = (series, HEADS, HEAD_DIM, length)
    count = n_dp * n_t
    hidden = gate.shape[1]
    share = -(-3 * width // (16 * n_dp)) * 16
    early = 3 * EARLY + HEADS + 1
    late = 3 * (HEADS - EARLY) + 1
    dma = pltpu.SemaphoreType.DMA
    group = (HEAD_DIM, width)
    return pl.pallas_call(
        functools.partial(kernel, n_dp, n_t),
        out_shape=[
            jax.ShapeDtypeStruct(raw.shape, BF),
            jax.ShapeDtypeStruct(raw.shape, F32),
            jax.ShapeDtypeStruct((width, 3 * width), F32),
            jax.ShapeDtypeStruct((width, width), F32),
            jax.ShapeDtypeStruct((1, width), F32),
            jax.ShapeDtypeStruct((width, hidden), F32),
            jax.ShapeDtypeStruct((width, hidden), F32),
            jax.ShapeDtypeStruct((width, hidden), F32),
            jax.ShapeDtypeStruct((1, width), F32),
        ],
        in_specs=[smem, smem] + [vmem] * 11,
        out_specs=[vmem] * 9,
        scratch_shapes=[
            pltpu.VMEM((series * HEADS, packed, BLK), BF),
            pltpu.VMEM((packed, BLK), BF),
            pltpu.VMEM((series, HEADS, 2 * HEAD_DIM, length), BF),
            pltpu.VMEM(per_head, BF),
            pltpu.VMEM(per_head, BF),
            pltpu.VMEM((series, HEADS, 2 * HEAD_DIM, length), BF),
            pltpu.VMEM(per_head, F32),
            pltpu.VMEM((series, HEADS, 1, length), F32),
            pltpu.VMEM(per_head, BF),
            pltpu.VMEM(per_head, BF),
            pltpu.VMEM((series, 3 * HEADS, HEAD_DIM, length), BF),
            pltpu.VMEM((series, width, length), BF),
            pltpu.VMEM((series, width, length), F32),
            pltpu.VMEM((series, width, length), F32),
            pltpu.VMEM((n_t, width, 3 * hidden), BF),
            pltpu.VMEM((n_t, n_dp * share, hidden), F32),
            pltpu.VMEM((n_t, n_dp, share, hidden), BF),
            pltpu.VMEM((count - 1, share, hidden), BF),
            pltpu.VMEM((n_dp, share, hidden), BF),
            pltpu.VMEM((width, width), F32),
            pltpu.VMEM((early,) + group, BF),
            pltpu.VMEM((count - 1,) + group, BF),
            pltpu.VMEM((early,) + group, BF),
            pltpu.VMEM((late,) + group, BF),
            pltpu.VMEM((count - 1,) + group, BF),
            pltpu.VMEM((late,) + group, BF),
            pltpu.VMEM((16, width), F32),
            dma((n_t,)), dma((n_t,)), dma((count - 1,)), dma, dma((max(n_dp - 1, 1),)), dma,
            dma((early,)), dma, dma, dma((early,)),
            dma((late,)), dma, dma, dma((late,)),
        ],
        compiler_params=pltpu.CompilerParams(vmem_limit_bytes=60 * 2**20, collective_id=0, has_side_effects=True),
    )(median_code, scale_code, raw, cot, qkv, out, again.reshape(1, -1), gate, up, down, mgain.reshape(1, -1), cosine, sine)


def local(
    n_dp, n_t, raw_series, median_code, scale_code, qkv_weight, out_weight, attn_gain, gate_weight, up_weight, down_weight,
    mlp_gain, cotangent,
):
    result, input_grad, qkv_grad, out_grad, again_grad, gate_grad, up_grad, down_grad, mgain_grad = layer(
        n_dp, n_t, median_code.T, scale_code.T, raw_series.transpose(0, 1, 3, 2), cotangent.transpose(0, 1, 3, 2), qkv_weight,
        out_weight, attn_gain, gate_weight, up_weight, down_weight.T, mlp_gain,
    )
    return (
        result.transpose(0, 1, 3, 2), input_grad.transpose(0, 1, 3, 2), qkv_grad, out_grad, again_grad[0], gate_grad, up_grad,
        down_grad.T, mgain_grad[0],
    )


def solution(mesh):
    placed = (
        P(None, ("dp", "tensor"), None, None), P(None, ("dp", "tensor")), P(None, ("dp", "tensor")), P(), P(), P(),
        P(None, "tensor"), P(None, "tensor"), P("tensor", None), P(), P(None, ("dp", "tensor"), None, None),
    )
    return jax.shard_map(
        functools.partial(local, mesh.shape["dp"], mesh.shape["tensor"]), mesh=mesh, in_specs=placed,
        out_specs=(
            P(None, ("dp", "tensor"), None, None), P(None, ("dp", "tensor"), None, None), P(), P(), P(),
            P(None, "tensor"), P(None, "tensor"), P("tensor", None), P(),
        ),
        check_vma=False,
    )
```

```python
import functools

import jax
import jax.numpy as jnp
import numpy as np
from jax import lax
from jax.experimental import pallas as pl
from jax.experimental.pallas import tpu as pltpu
from jax.sharding import PartitionSpec as P

BF = jnp.bfloat16
F32 = jnp.float32
MESH = pl.DeviceIdType.MESH
HEADS = 9
HEAD_DIM = 16
D = HEADS * HEAD_DIM
LANES = 128
GROUPS = D // 16
BLK = 256
EPS = 1e-05
MASKED = -1e30
LOG2E_SCALED = 0.25 * 1.4426950408889634

STAGE1 = [(c, h) for c in range(3) for h in range(5)]
STAGE2 = [(c, h) for c in range(3) for h in range(5, 8)][:8]
STAGE3 = [(2, 7), (0, 8), (1, 8), (2, 8)]
TILES = (3, 1, 1)
OUT_AT = 16 * len(STAGE1)
GAIN_AT = 16 * len(STAGE3)


def mm(a, b):
    return lax.dot_general(a, b, (((1,), (0,)), ((), ())), preferred_element_type=F32)


def mm_tn(a, b):
    return lax.dot_general(a, b, (((0,), (0,)), ((), ())), preferred_element_type=F32)


def mm_nt(a, b):
    return lax.dot_general(a, b, (((1,), (1,)), ((), ())), preferred_element_type=F32)


def eye(n):
    same = lax.broadcasted_iota(jnp.int32, (n, n), 0) == lax.broadcasted_iota(jnp.int32, (n, n), 1)
    return jnp.where(same, 1.0, 0.0)


def to_column(row):
    return jnp.sum(eye(row.shape[1]) * row, axis=1, keepdims=True)


def to_row(column):
    return jnp.sum(eye(column.shape[0]) * column, axis=0, keepdims=True)


def norm_stats(rows):
    r = lax.rsqrt(jnp.mean(rows * rows, axis=0, keepdims=True) + EPS)
    return rows * r, r


def norm_backward(e, n, r, gain):
    weighted = e * gain
    mean = jnp.mean(weighted * n, axis=0, keepdims=True)
    return r * (weighted - n * mean), jnp.sum(e * n, axis=1, keepdims=True)


def rope(x, cosine, sine):
    length = x.shape[1]
    x = x.reshape(HEADS, 2, 8, length)
    a, b = x[:, 0], x[:, 1]
    first = a * cosine - b * sine
    second = a * sine + b * cosine
    return jnp.concatenate([first[:, None], second[:, None]], axis=1).reshape(HEADS, HEAD_DIM, length)


def each(first, last, body):
    if last - first <= 40:
        for k in range(first, last):
            body(k)
    else:
        pl.loop(first, last)(body)


def remote(src, dst, send_sem, recv_sem, device):
    return pltpu.make_async_remote_copy(
        src_ref=src, dst_ref=dst, send_sem=send_sem, recv_sem=recv_sem, device_id=device, device_id_type=MESH
    )


class GroupSum:
    def __init__(self, index, count, to, stage, recv, out, sems):
        self.index, self.count, self.to = index, count, to
        self.stage, self.recv, self.out = stage, recv, out
        self.send, self.land, self.spread, self.gather = (sems.at[i] for i in range(4))
        self.groups = stage.shape[0]
        self.stride = max(count // self.groups, 1)
        self.mine = index // self.stride
        self.owner = (lax.rem(index, self.stride) == 0) & (self.mine < self.groups)

    def go(self):
        def part(g):
            owner = g * self.stride

            @pl.when(owner != self.index)
            def _():
                slot = lax.rem(owner - self.index + self.count, self.count) - 1
                remote(self.stage.at[g], self.recv.at[slot], self.send, self.land, self.to(owner)).start()

        each(0, self.groups, part)

    def _all_parts(self):
        return remote(self.recv, self.recv, self.spread, self.land, self.to(self.index))

    def reduce(self):
        @pl.when(self.owner)
        def _():
            self._all_parts().wait_recv()
            total = self.stage[self.mine].astype(F32) + jnp.sum(self.recv[...].astype(F32), axis=0)
            self.out[self.mine] = total.astype(BF)

            def whole(k):
                device = self.to(lax.rem(self.index + k, self.count))
                remote(self.out.at[self.mine], self.out.at[self.mine], self.spread, self.gather, device).start()

            each(1, self.count, whole)

    def finish(self):
        def landed(n):
            stage, out = self.stage.at[pl.ds(0, n)], self.out.at[pl.ds(0, n)]
            both = remote(stage, out, self.send, self.gather, self.to(self.index))
            both.wait_recv()
            both.wait_send()

        @pl.when(self.owner)
        def _():
            if self.groups > 1:
                landed(self.groups - 1)
            self._all_parts().wait_send()

        @pl.when(jnp.logical_not(self.owner))
        def _():
            landed(self.groups)


def kernel(
    n_dp, n_t,
    median_ref, scale_ref, raw_hbm, cot_hbm, qkv_ref, out_ref, again_ref, gate_ref, up_ref, down_ref, mgain_ref, cos_ref, sin_ref,
    source_ref,
    result_hbm, igrad_hbm, qkvg_ref, outg_ref, againg_ref, gateg_ref, upg_ref, downg_ref, mgaing_ref,
    raw_ref, cot_ref, result_ref, igrad_ref,
    e_ref, ds_ref, qa_ref, q_ref, k_ref, v_ref, o_ref, linv_ref, att_ref, datt_ref, dproj_ref, rows_ref, scaled_ref, dh_ref,
    w_ref, ffacc_ref, ffstage_ref, ffpair_ref, ffhalf_ref, ffrecv_ref, ffout_ref, outacc_ref, gains_ref,
    stage1, recv1, out1, stage2, recv2, out2, stage3, recv3, out3,
    local_sem, w_send, w_recv, w_send2, w_recv2, ff_sem, sems1, sems2, sems3,
):
    series, _, _, length = raw_hbm.shape
    nblk = length // BLK
    hidden_local = gate_ref.shape[1]
    count = n_dp * n_t
    my_dp, my_t = lax.axis_index("dp"), lax.axis_index("tensor")
    index = my_dp * n_t + my_t
    core = lax.rem(my_dp, 2)
    pair = my_dp // 2
    partner = (my_dp + 1 - 2 * core, my_t)
    pairs = n_dp // 2

    def to(device):
        return (device // n_t, lax.rem(device, n_t))

    loads = [pltpu.make_async_copy(raw_hbm.at[s, 0], raw_ref.at[s], local_sem.at[s]) for s in range(series)]
    loads += [pltpu.make_async_copy(cot_hbm.at[s, 0], cot_ref.at[s], local_sem.at[series + s]) for s in range(series)]
    for copy in loads:
        copy.start()

    barrier = pltpu.get_barrier_semaphore()

    def greet(k):
        pl.semaphore_signal(barrier, inc=1, device_id=to(lax.rem(index + k, count)), device_id_type=MESH)

    each(1, count, greet)

    cosine, sine = cos_ref[...], sin_ref[...]
    again, mgain = to_column(again_ref[...]), to_column(mgain_ref[...])

    def spread_inverse(s):
        return 1.0 / jnp.full((1, length), scale_ref[0, s].astype(F32) * 0.25, F32)

    tail_rows = lax.broadcasted_iota(jnp.int32, (HEAD_DIM, length), 0)
    w_ref[0, :, :hidden_local] = gate_ref[...]
    w_ref[0, :, hidden_local : 2 * hidden_local] = up_ref[...]
    w_ref[0, :, 2 * hidden_local :] = down_ref[...]
    for copy in loads:
        copy.wait()

    @pl.loop(0, series)
    def _(s):
        shift = median_ref[0, s].astype(F32) * 0.05
        scaled = (raw_ref[s].astype(F32) - shift) * spread_inverse(s)
        scaled_ref[s] = scaled
        n, _ = norm_stats(scaled)
        rows = (n * again).astype(BF)
        rows_ref[s] = rows
        projected = mm_tn(qkv_ref[...], rows)
        queries = rope(projected[:D], cosine, sine).astype(BF)
        keys = rope(projected[D : 2 * D], cosine, sine).astype(BF)
        values = projected[2 * D :].reshape(HEADS, HEAD_DIM, length).astype(BF)
        q_ref[s] = queries
        k_ref[s] = keys
        wide = queries.astype(F32) * LOG2E_SCALED
        high = wide.astype(BF)
        qa_ref[s, :, :HEAD_DIM] = high
        qa_ref[s, :, HEAD_DIM:] = (wide - high.astype(F32)).astype(BF)
        v_ref[s, :, :HEAD_DIM] = values
        ones = jnp.where(tail_rows < 2, 1.0, 0.0).astype(BF)
        v_ref[s, :, HEAD_DIM:] = jnp.broadcast_to(ones[None], (HEADS, HEAD_DIM, length))

    cut = 16 * ((GROUPS + 1) // 2)

    def half_rows(which, body):
        for c, (lo, hi) in enumerate(((0, cut), (cut, D))):
            @pl.when(core == (c if which == 0 else 1 - c))
            def _():
                body(pl.ds(lo, hi - lo))

    def over_links(k, rows):
        device = (my_dp, lax.rem(my_t + k, n_t))
        return remote(w_ref.at[0, rows], w_ref.at[k, rows], w_send.at[k], w_recv.at[k], device)

    def within_pair(k, rows):
        return remote(w_ref.at[k, rows], w_ref.at[k, rows], w_send2.at[k], w_recv2.at[k], partner)

    def send_weights():
        pl.semaphore_wait(barrier, count - 1)

        def start(rows):
            for k in range(1, n_t):
                over_links(k, rows).start()

        half_rows(0, start)

    def exchange_weights():
        def forward(rows):
            for k in range(1, n_t):
                over_links(k, rows).wait()
                within_pair(k, rows).start()

        half_rows(0, forward)

    def finish_weights():
        def sent(rows):
            for k in range(1, n_t):
                within_pair(k, rows).wait_send()

        def landed(rows):
            for k in range(1, n_t):
                within_pair(k, rows).wait_recv()

        half_rows(0, sent)
        half_rows(1, landed)

    causal = lax.broadcasted_iota(jnp.int32, (BLK, BLK), 0) <= lax.broadcasted_iota(jnp.int32, (BLK, BLK), 1)

    def offset(j):
        return BLK * (j * (j + 1) // 2)

    @pl.loop(0, series)
    def _(s):
        @pl.loop(0, HEADS)
        def _(h):
            keys = k_ref[s, h]
            keys2 = jnp.concatenate([keys, keys], axis=0)
            for j in range(nblk):
                lo, hi = j * BLK, (j + 1) * BLK
                scores = mm_tn(keys2[:, :hi], qa_ref[s, h, :, lo:hi])
                diagonal = jnp.where(causal, scores[lo:], MASKED)
                scores = jnp.concatenate([scores[:lo], diagonal], axis=0) if j else diagonal
                largest = jnp.max(scores, axis=0, keepdims=True)
                e_ref[s * HEADS + h, offset(j) : offset(j) + hi] = jnp.exp2(scores - largest).astype(BF)
            for j in range(nblk):
                lo, hi = j * BLK, (j + 1) * BLK
                mixed = mm(v_ref[s, h, :, :hi], e_ref[s * HEADS + h, offset(j) : offset(j) + hi])
                inverse = 1.0 / mixed[HEAD_DIM : HEAD_DIM + 1]
                attended = mixed[:HEAD_DIM] * inverse
                linv_ref[s, h, :, lo:hi] = inverse
                o_ref[s, h, :, lo:hi] = attended
                att_ref[s, h, :, lo:hi] = attended.astype(BF)

            @pl.when((s == 0) & (h == 5))
            def _():
                send_weights()

            @pl.when((s == series - 1) & (h == 5))
            def _():
                exchange_weights()

    finish_weights()

    ffacc_ref[...] = jnp.zeros_like(ffacc_ref)
    outacc_ref[...] = jnp.zeros_like(outacc_ref)
    gains_ref[...] = jnp.zeros_like(gains_ref)

    @pl.loop(0, series)
    def _(s):
        attended = att_ref[s].reshape(D, length)
        hidden = scaled_ref[s] + mm_tn(out_ref[...], attended)
        n, r = norm_stats(hidden)
        rows = (n * mgain).astype(BF)
        low = cot_ref[s]
        top = low.astype(F32)
        result = hidden
        grad_rows = jnp.zeros((D, length), F32)
        for t in range(n_t):
            gu = w_ref[t, :, : 2 * hidden_local]
            down = w_ref[t, :, 2 * hidden_local :]
            both = mm_tn(gu, rows)
            gate, up = both[:hidden_local], both[hidden_local:]
            grad_inner = mm_tn(down, low)
            sigma = 1.0 / (1.0 + jnp.exp(-gate))
            act = gate * sigma
            inner = (act * up).astype(BF)
            grad_gate = (grad_inner * up * (sigma + act * (1.0 - sigma))).astype(BF)
            grad_up = (grad_inner * act).astype(BF)
            grad_both = jnp.concatenate([grad_gate, grad_up], axis=0)
            result = result + mm(down, inner)
            grad_rows = grad_rows + mm(gu, grad_both)
            gu_piece = mm_nt(rows, grad_both)
            ffacc_ref[t, :D] += gu_piece[:, :hidden_local]
            ffacc_ref[t, D : 2 * D] += gu_piece[:, hidden_local:]
            ffacc_ref[t, 2 * D : 3 * D] += mm_nt(low, inner)

        result_ref[s] = result.astype(BF)
        part, gain_part = norm_backward(grad_rows, n, r, mgain)
        grad_hidden = top + part
        dh_ref[s] = grad_hidden
        branch = grad_hidden.astype(BF)
        outacc_ref[...] += mm_nt(attended, branch)
        gains_ref[:, 1:2] += gain_part
        datt_ref[s] = mm(out_ref[...], branch).astype(BF).reshape(HEADS, HEAD_DIM, length)

    def store_result(s):
        return pltpu.make_async_copy(result_ref.at[s], result_hbm.at[s, 0], local_sem.at[s])

    def store_igrad(s):
        return pltpu.make_async_copy(igrad_ref.at[s], igrad_hbm.at[s, 0], local_sem.at[series + s])

    for s in range(series):
        store_result(s).start()

    share = ffout_ref.shape[1]
    for t in range(n_t):
        staged = ffacc_ref[t].astype(BF).reshape(pairs, 2, share, hidden_local)
        for c in range(2):
            ffstage_ref[c, t] = staged[:, c]
    peers = pairs * n_t
    place = pair * n_t + my_t

    def ff_pair():
        return remote(ffstage_ref.at[1 - core], ffpair_ref, ff_sem.at[0], ff_sem.at[1], partner)

    ff_pair().start()

    def ff_send():
        ff_pair().wait()
        ffhalf_ref[...] = (ffstage_ref[core].astype(F32) + ffpair_ref[...].astype(F32)).astype(BF)

        def part(k):
            peer = lax.rem(place + k, peers)
            peer_pair, peer_t = peer // n_t, lax.rem(peer, n_t)
            piece = ffhalf_ref.at[lax.rem(my_t - peer_t + n_t, n_t), peer_pair]
            remote(piece, ffrecv_ref.at[k - 1], ff_sem.at[2], ff_sem.at[3], (2 * peer_pair + core, peer_t)).start()

        each(1, peers, part)

    def ff_parts():
        return remote(ffrecv_ref, ffrecv_ref, ff_sem.at[2], ff_sem.at[3], to(index))

    def ff_reduce():
        ff_parts().wait_recv()
        total = ffhalf_ref[0, pair].astype(F32) + jnp.sum(ffrecv_ref[...].astype(F32), axis=0)
        ffout_ref[my_dp] = total.astype(BF)

        def whole(k):
            device = (lax.rem(my_dp + k, n_dp), my_t)
            remote(ffout_ref.at[my_dp], ffout_ref.at[my_dp], ff_sem.at[4], ff_sem.at[5], device).start()

        each(1, n_dp, whole)

    def ff_finish():
        ff_parts().wait_send()
        others = ffout_ref.at[pl.ds(0, n_dp - 1)]
        remote(others, others, ff_sem.at[4], ff_sem.at[5], to(index)).wait()
        sums = ffout_ref[...].astype(F32).reshape(-1, hidden_local)
        gateg_ref[...] = sums[:D]
        upg_ref[...] = sums[D : 2 * D]
        downg_ref[...] = sums[2 * D : 3 * D]

    sum1 = GroupSum(index, count, to, stage1, recv1, out1, sems1)
    sum2 = GroupSum(index, count, to, stage2, recv2, out2, sems2)
    sum3 = GroupSum(index, count, to, stage3, recv3, out3, sems3)

    def head_grads(parts):
        total = None
        for s in range(series):
            grads = jnp.concatenate([dproj_ref[s, c * HEADS + h] for c, h in parts], axis=0)
            piece = mm_nt(rows_ref[s], grads)
            total = piece if total is None else total + piece
        return total

    def put(stage, grads):
        for t in range(grads.shape[1] // LANES):
            tile = grads[:, t * LANES : (t + 1) * LANES].astype(BF)
            stage[t * GROUPS : (t + 1) * GROUPS] = tile.reshape(GROUPS, 16, LANES)

    @pl.loop(0, HEADS)
    def _(h):
        @pl.loop(0, series)
        def _(s):
            grad = (datt_ref[s, h].astype(F32) * linv_ref[s, h]).astype(BF)
            delta = -jnp.sum(grad.astype(F32) * o_ref[s, h], axis=0, keepdims=True)
            high = delta.astype(BF).astype(F32)
            tail = jnp.where(tail_rows == 0, high, jnp.where(tail_rows == 1, delta - high, 0.0))
            grad_all = jnp.concatenate([grad, tail.astype(BF)], axis=0)
            values = v_ref[s, h]
            queries, keys = q_ref[s, h], k_ref[s, h]
            for j in range(nblk):
                lo, hi = j * BLK, (j + 1) * BLK
                weights = e_ref[s * HEADS + h, offset(j) : offset(j) + hi]
                centred = mm_tn(values[:, :hi], grad_all[:, lo:hi])
                ds_ref[offset(j) : offset(j) + hi] = centred.astype(BF) * weights
            value_grads, key_grads, query_grads = [], [], []
            for j in range(nblk):
                lo, hi = j * BLK, (j + 1) * BLK
                query_grads.append(mm(keys[:, :hi], ds_ref[offset(j) : offset(j) + hi]))
            for i in range(nblk):
                value_grad = key_grad = None
                for j in range(i, nblk):
                    at = offset(j) + i * BLK
                    cols = slice(j * BLK, (j + 1) * BLK)
                    piece = mm_nt(grad[:, cols], e_ref[s * HEADS + h, at : at + BLK])
                    value_grad = piece if value_grad is None else value_grad + piece
                    piece = mm_nt(queries[:, cols], ds_ref[at : at + BLK])
                    key_grad = piece if key_grad is None else key_grad + piece
                value_grads.append(value_grad)
                key_grads.append(key_grad)

            def unrotate(g):
                a, b = g[:8], g[8:]
                return jnp.concatenate([a * cosine + b * sine, b * cosine - a * sine], axis=0)

            query_grad = jnp.concatenate(query_grads, axis=1) * 0.25
            key_grad = jnp.concatenate(key_grads, axis=1) * 0.25
            dproj_ref[s, h] = unrotate(query_grad).astype(BF)
            dproj_ref[s, HEADS + h] = unrotate(key_grad).astype(BF)
            dproj_ref[s, 2 * HEADS + h] = jnp.concatenate(value_grads, axis=1).astype(BF)

        @pl.when(h == 0)
        def _():
            ff_send()

        @pl.when(h == 4)
        def _():
            ff_reduce()
            put(stage1, jnp.concatenate([head_grads(STAGE1), outacc_ref[...]], axis=1))
            sum1.go()

        @pl.when(h == 6)
        def _():
            sum1.reduce()

        @pl.when(h == 7)
        def _():
            put(stage2, head_grads(STAGE2))
            sum2.go()

    @pl.loop(0, series)
    def _(s):
        grad = dproj_ref[s].reshape(3 * D, length)
        grad_rows = mm(qkv_ref[...], grad)
        n, r = norm_stats(scaled_ref[s])
        part, gain_part = norm_backward(grad_rows, n, r, again)
        igrad_ref[s] = (dh_ref[s] + part) * spread_inverse(s)
        gains_ref[:, 0:1] += gain_part

    last = head_grads(STAGE3)
    put(stage3, jnp.concatenate([last, gains_ref[:, : LANES - GAIN_AT]], axis=1))
    sum3.go()
    for s in range(series):
        store_igrad(s).start()
    sum2.reduce()
    ff_finish()
    sum1.finish()
    place_of = jnp.where(
        lax.broadcasted_iota(jnp.int32, (sum(TILES) * LANES, source_ref.shape[1]), 0) == source_ref[...], 1.0, 0.0
    ).astype(BF)
    sum3.reduce()
    sum2.finish()
    for s in range(series):
        store_result(s).wait()
        store_igrad(s).wait()
    sum3.finish()
    tiles = []
    for out, n in zip((out1, out2, out3), TILES, strict=True):
        tiles += [out[t * GROUPS : (t + 1) * GROUPS].reshape(D, LANES) for t in range(n)]
    sums = mm(jnp.concatenate(tiles, axis=1), place_of)
    qkvg_ref[...] = sums[:, : 3 * D]
    outg_ref[...] = sums[:, 4 * LANES : 4 * LANES + D]
    againg_ref[...] = to_row(tiles[-1][:, GAIN_AT : GAIN_AT + 1].astype(F32))
    mgaing_ref[...] = to_row(tiles[-1][:, GAIN_AT + 1 : GAIN_AT + 2].astype(F32))


def rope_tables(length):
    half = HEAD_DIM // 2
    frequency = np.float32(10000.0) ** (-(np.arange(half, dtype=np.float32) * np.float32(2.0) / np.float32(HEAD_DIM)))
    angles = np.arange(length, dtype=np.float32)[None, :] * frequency.astype(np.float32)[:, None]
    return np.cos(angles).astype(np.float32), np.sin(angles).astype(np.float32)


def column_sources():
    source = np.full((1, 4 * LANES + D), -1, np.int32)
    first = 0
    for parts, tiles in zip((STAGE1, STAGE2, STAGE3), TILES, strict=True):
        for place, (c, h) in enumerate(parts):
            at = c * D + h * HEAD_DIM
            source[0, at : at + HEAD_DIM] = first + place * HEAD_DIM + np.arange(HEAD_DIM)
        first += tiles * LANES
    source[0, 4 * LANES :] = OUT_AT + np.arange(D)
    return source


def copy_kernel(n, *refs):
    sources, results, held, sems = refs[:n], refs[n : 2 * n], refs[2 * n : 3 * n], refs[3 * n]
    takes = [pltpu.make_async_copy(sources[i], held[i], sems.at[0, i]) for i in range(n)]
    gives = [pltpu.make_async_copy(held[i], results[i], sems.at[1, i]) for i in range(n)]
    for copy in takes:
        copy.start()
    for take, give in zip(takes, gives, strict=True):
        take.wait()
        give.start()
    for copy in gives:
        copy.wait()


def hand_over(arrays):
    n = len(arrays)
    place = pl.BlockSpec(memory_space=pltpu.HBM)
    return pl.pallas_call(
        functools.partial(copy_kernel, n),
        out_shape=[jax.ShapeDtypeStruct(a.shape, a.dtype) for a in arrays],
        in_specs=[place] * n,
        out_specs=[place] * n,
        scratch_shapes=[pltpu.VMEM(a.shape, a.dtype) for a in arrays] + [pltpu.SemaphoreType.DMA((2, n))],
    )(*arrays)


def layer(n_dp, n_t, median_code, scale_code, raw, cot, qkv, out, again, gate, up, down, mgain):
    series, _, width, length = raw.shape
    cosine, sine = rope_tables(length)
    source = column_sources()
    blocks = length // BLK
    packed = BLK * blocks * (blocks + 1) // 2
    vmem = pl.BlockSpec(memory_space=pltpu.VMEM)
    smem = pl.BlockSpec(memory_space=pltpu.SMEM)
    anywhere = pl.BlockSpec(memory_space=pl.ANY)
    per_head = (series, HEADS, HEAD_DIM, length)
    rows = (series, width, length)
    count = n_dp * n_t
    pairs = n_dp // 2
    hidden = gate.shape[1]
    share = -(-3 * width // (16 * n_dp)) * 16
    dma = pltpu.SemaphoreType.DMA
    stages = []
    for n in TILES:
        stages += [
            pltpu.VMEM((n * GROUPS, 16, LANES), BF), pltpu.VMEM((count - 1, 16, LANES), BF), pltpu.VMEM((n * GROUPS, 16, LANES), BF),
        ]
    return pl.pallas_call(
        functools.partial(kernel, n_dp, n_t),
        out_shape=[
            jax.ShapeDtypeStruct(raw.shape, BF),
            jax.ShapeDtypeStruct(raw.shape, F32),
            jax.ShapeDtypeStruct((width, 3 * width), F32),
            jax.ShapeDtypeStruct((width, width), F32),
            jax.ShapeDtypeStruct((1, width), F32),
            jax.ShapeDtypeStruct((width, hidden), F32),
            jax.ShapeDtypeStruct((width, hidden), F32),
            jax.ShapeDtypeStruct((width, hidden), F32),
            jax.ShapeDtypeStruct((1, width), F32),
        ],
        in_specs=[smem, smem, anywhere, anywhere] + [vmem] * 10,
        out_specs=[anywhere, anywhere] + [vmem] * 7,
        scratch_shapes=[
            pltpu.VMEM(rows, BF),
            pltpu.VMEM(rows, BF),
            pltpu.VMEM(rows, BF),
            pltpu.VMEM(rows, F32),
            pltpu.VMEM((series * HEADS, packed, BLK), BF),
            pltpu.VMEM((packed, BLK), BF),
            pltpu.VMEM((series, HEADS, 2 * HEAD_DIM, length), BF),
            pltpu.VMEM(per_head, BF),
            pltpu.VMEM(per_head, BF),
            pltpu.VMEM((series, HEADS, 2 * HEAD_DIM, length), BF),
            pltpu.VMEM(per_head, F32),
            pltpu.VMEM((series, HEADS, 1, length), F32),
            pltpu.VMEM(per_head, BF),
            pltpu.VMEM(per_head, BF),
            pltpu.VMEM((series, 3 * HEADS, HEAD_DIM, length), BF),
            pltpu.VMEM(rows, BF),
            pltpu.VMEM(rows, F32),
            pltpu.VMEM(rows, F32),
            pltpu.VMEM((n_t, width, 3 * hidden), BF),
            pltpu.VMEM((n_t, n_dp * share, hidden), F32),
            pltpu.VMEM((2, n_t, pairs, share, hidden), BF),
            pltpu.VMEM((n_t, pairs, share, hidden), BF),
            pltpu.VMEM((n_t, pairs, share, hidden), BF),
            pltpu.VMEM((pairs * n_t - 1, share, hidden), BF),
            pltpu.VMEM((n_dp, share, hidden), BF),
            pltpu.VMEM((width, width), F32),
            pltpu.VMEM((width, LANES), F32),
            *stages,
            dma((2 * series,)), dma((n_t,)), dma((n_t,)), dma((n_t,)), dma((n_t,)), dma((6,)), dma((4,)), dma((4,)), dma((4,)),
        ],
        compiler_params=pltpu.CompilerParams(vmem_limit_bytes=60 * 2**20, collective_id=0, has_side_effects=True),
    )(
        median_code, scale_code, raw, cot, qkv, out, again.reshape(1, -1), gate, up, down, mgain.reshape(1, -1), cosine, sine, source
    )


def local(
    n_dp, n_t, raw_series, median_code, scale_code, qkv_weight, out_weight, attn_gain, gate_weight, up_weight, down_weight,
    mlp_gain, cotangent,
):
    result, input_grad, qkv_grad, out_grad, again_grad, gate_grad, up_grad, down_grad, mgain_grad = hand_over(layer(
        n_dp, n_t, median_code.T, scale_code.T, raw_series.transpose(0, 1, 3, 2), cotangent.transpose(0, 1, 3, 2), qkv_weight,
        out_weight, attn_gain, gate_weight, up_weight, down_weight.T, mlp_gain,
    ))
    return (
        result.transpose(0, 1, 3, 2), input_grad.transpose(0, 1, 3, 2), qkv_grad, out_grad, again_grad[0], gate_grad, up_grad,
        down_grad.T, mgain_grad[0],
    )


def solution(mesh):
    placed = (
        P(None, ("dp", "tensor"), None, None), P(None, ("dp", "tensor")), P(None, ("dp", "tensor")), P(), P(), P(),
        P(None, "tensor"), P(None, "tensor"), P("tensor", None), P(), P(None, ("dp", "tensor"), None, None),
    )
    return jax.shard_map(
        functools.partial(local, mesh.shape["dp"], mesh.shape["tensor"]), mesh=mesh, in_specs=placed,
        out_specs=(
            P(None, ("dp", "tensor"), None, None), P(None, ("dp", "tensor"), None, None), P(), P(), P(),
            P(None, "tensor"), P(None, "tensor"), P("tensor", None), P(),
        ),
        check_vma=False,
    )
```

```python
import functools

import jax
import jax.numpy as jnp
import numpy as np
from jax import lax
from jax.experimental import pallas as pl
from jax.experimental.pallas import tpu as pltpu
from jax.sharding import PartitionSpec as P

BF = jnp.bfloat16
F32 = jnp.float32
MESH = pl.DeviceIdType.MESH
HEADS = 9
HEAD_DIM = 16
D = HEADS * HEAD_DIM
LANES = 128
GROUPS = D // 16
BLK = 256
EPS = 1e-05
MASKED = -1e30
LOG2E_SCALED = 0.25 * 1.4426950408889634

FIRST = [(c, h) for c in range(3) for h in range(6)]
STAGE1 = FIRST[:16]
STAGE2 = FIRST[16:] + [(c, h) for c in range(3) for h in (6, 7)]
LAST = HEADS - 1
TILES = (2, 2, 1)


def mm(a, b):
    return lax.dot_general(a, b, (((1,), (0,)), ((), ())), preferred_element_type=F32)


def mm_tn(a, b):
    return lax.dot_general(a, b, (((0,), (0,)), ((), ())), preferred_element_type=F32)


def mm_nt(a, b):
    return lax.dot_general(a, b, (((1,), (1,)), ((), ())), preferred_element_type=F32)


def eye(n):
    same = lax.broadcasted_iota(jnp.int32, (n, n), 0) == lax.broadcasted_iota(jnp.int32, (n, n), 1)
    return jnp.where(same, 1.0, 0.0)


def to_column(row):
    return jnp.sum(eye(row.shape[1]) * row, axis=1, keepdims=True)


def to_row(column):
    return jnp.sum(eye(column.shape[0]) * column, axis=0, keepdims=True)


def norm_stats(rows):
    r = lax.rsqrt(jnp.mean(rows * rows, axis=0, keepdims=True) + EPS)
    return rows * r, r


def norm_backward(e, n, r, gain):
    weighted = e * gain
    mean = jnp.mean(weighted * n, axis=0, keepdims=True)
    return r * (weighted - n * mean), jnp.sum(e * n, axis=1, keepdims=True)


def rope(x, cosine, sine):
    length = x.shape[1]
    x = x.reshape(HEADS, 2, 8, length)
    a, b = x[:, 0], x[:, 1]
    first = a * cosine - b * sine
    second = a * sine + b * cosine
    return jnp.concatenate([first[:, None], second[:, None]], axis=1).reshape(HEADS, HEAD_DIM, length)


def each(first, last, body):
    if last - first <= 40:
        for k in range(first, last):
            body(k)
    else:
        pl.loop(first, last)(body)


def remote(src, dst, send_sem, recv_sem, device):
    return pltpu.make_async_remote_copy(
        src_ref=src, dst_ref=dst, send_sem=send_sem, recv_sem=recv_sem, device_id=device, device_id_type=MESH
    )


class GroupSum:
    def __init__(self, index, count, to, first, stage, recv, out, sems):
        self.index, self.count, self.to, self.first = index, count, to, first
        self.stage, self.recv, self.out = stage, recv, out
        self.send, self.land, self.spread, self.gather = (sems.at[i] for i in range(4))
        self.groups = stage.shape[0]
        self.stride = max(count // self.groups, 1)
        place = lax.rem(index + count - first, count)
        self.mine = place // self.stride
        self.owner = (lax.rem(place, self.stride) == 0) & (self.mine < self.groups)

    def go(self):
        def part(g):
            owner = lax.rem(g * self.stride + self.first, self.count)

            @pl.when(owner != self.index)
            def _():
                slot = lax.rem(owner - self.index + self.count, self.count) - 1
                remote(self.stage.at[g], self.recv.at[slot], self.send, self.land, self.to(owner)).start()

        each(0, self.groups, part)

    def _all_parts(self):
        return remote(self.recv, self.recv, self.spread, self.land, self.to(self.index))

    def reduce(self):
        @pl.when(self.owner)
        def _():
            self._all_parts().wait_recv()
            total = self.stage[self.mine].astype(F32) + jnp.sum(self.recv[...].astype(F32), axis=0)
            self.out[self.mine] = total.astype(BF)

            def whole(k):
                device = self.to(lax.rem(self.index + k, self.count))
                remote(self.out.at[self.mine], self.out.at[self.mine], self.spread, self.gather, device).start()

            each(1, self.count, whole)

    def finish(self):
        def landed(n):
            stage, out = self.stage.at[pl.ds(0, n)], self.out.at[pl.ds(0, n)]
            both = remote(stage, out, self.send, self.gather, self.to(self.index))
            both.wait_recv()
            both.wait_send()

        @pl.when(self.owner)
        def _():
            if self.groups > 1:
                landed(self.groups - 1)
            self._all_parts().wait_send()

        @pl.when(jnp.logical_not(self.owner))
        def _():
            landed(self.groups)


class HeadSum:
    def __init__(self, own, pair, half, recv, total, sems, core, partner, device_of, peers):
        self.own, self.pair, self.half, self.recv, self.total = own, pair, half, recv, total
        self.sems, self.core, self.partner, self.device_of, self.peers = sems, core, partner, device_of, peers

    def _exchange(self):
        return remote(self.own.at[1 - self.core], self.pair, self.sems.at[0], self.sems.at[1], self.partner)

    def go(self, main, rest):
        main = main.astype(BF).reshape(3, 16, LANES)
        self.own[0] = main[:2]
        self.own[1, 0] = main[2]
        self.own[1, 1] = jnp.concatenate([rest, jnp.zeros((16, LANES - rest.shape[1]), F32)], axis=1).astype(BF)
        self._exchange().start()

    def send(self):
        self._exchange().wait()
        self.half[...] = (self.own[self.core].astype(F32) + self.pair[...].astype(F32)).astype(BF)
        for_peer = lambda k: remote(self.half, self.recv.at[k - 1], self.sems.at[2], self.sems.at[3], self.device_of(k)).start()
        each(1, self.peers, for_peer)

    def _back(self):
        piece = self.total.at[self.core]
        return remote(piece, piece, self.sems.at[4], self.sems.at[5], self.partner)

    def reduce(self):
        remote(self.recv, self.recv, self.sems.at[2], self.sems.at[3], self.partner).wait()
        self.total[self.core] = (self.half[...].astype(F32) + jnp.sum(self.recv[...].astype(F32), axis=0)).astype(BF)
        self._back().start()

    def finish(self):
        self._back().wait()
        turn = jnp.where(
            lax.broadcasted_iota(jnp.int32, (48, LANES), 0) == lax.broadcasted_iota(jnp.int32, (48, LANES), 1), 1.0, 0.0
        ).astype(BF)
        total = self.total[...].reshape(4, 16, LANES)
        return jnp.concatenate([mm_tn(total[:3].reshape(48, LANES), turn).astype(BF), total[3]], axis=0)


def kernel(
    n_dp, n_t,
    median_ref, scale_ref, raw_hbm, cot_hbm, qkv_ref, out_ref, again_ref, gate_ref, up_ref, down_ref, mgain_ref, cos_ref, sin_ref,
    source_ref,
    result_hbm, igrad_hbm, qkvg_ref, outg_ref, againg_ref, gateg_ref, upg_ref, downg_ref, mgaing_ref,
    raw_ref, cot_ref, result_ref, igrad_ref,
    e_ref, ds_ref, ds2_ref, ga_ref, ga2_ref, qa_ref, q_ref, k_ref, v_ref, o_ref, linv_ref, att_ref, datt_ref, dproj_ref, rows_ref, scaled_ref, dh_ref,
    w_ref, ffacc_ref, ffstage_ref, ffpair_ref, ffhalf_ref, ffrecv_ref, ffout_ref, outacc_ref, gains_ref,
    stage0, recv0, out0, stage1, recv1, out1, stage2, recv2, out2, *rest,
):
    local_sem, w_send, w_recv, w_send2, w_recv2, ff_sem, sems0, sems1, sems2, sems3 = rest[5:]
    series, _, _, length = raw_hbm.shape
    nblk = length // BLK
    hidden_local = gate_ref.shape[1]
    count = n_dp * n_t
    my_dp, my_t = lax.axis_index("dp"), lax.axis_index("tensor")
    index = my_dp * n_t + my_t
    core = lax.rem(my_dp, 2)
    pair = my_dp // 2
    partner = (my_dp + 1 - 2 * core, my_t)
    pairs = n_dp // 2

    def to(device):
        return (device // n_t, lax.rem(device, n_t))

    loads = [pltpu.make_async_copy(raw_hbm.at[s, 0], raw_ref.at[s], local_sem.at[s]) for s in range(series)]
    loads += [pltpu.make_async_copy(cot_hbm.at[s, 0], cot_ref.at[s], local_sem.at[series + s]) for s in range(series)]
    for copy in loads:
        copy.start()

    barrier = pltpu.get_barrier_semaphore()

    def greet(k):
        pl.semaphore_signal(barrier, inc=1, device_id=to(lax.rem(index + k, count)), device_id_type=MESH)

    each(1, count, greet)

    cosine, sine = cos_ref[...], sin_ref[...]
    again, mgain = to_column(again_ref[...]), to_column(mgain_ref[...])

    def spread_inverse(s):
        return 1.0 / jnp.full((1, length), scale_ref[0, s].astype(F32) * 0.25, F32)

    tail_rows = lax.broadcasted_iota(jnp.int32, (HEAD_DIM, length), 0)
    w_ref[0, :, :hidden_local] = gate_ref[...]
    w_ref[0, :, hidden_local : 2 * hidden_local] = up_ref[...]
    w_ref[0, :, 2 * hidden_local :] = down_ref[...]
    for copy in loads:
        copy.wait()

    @pl.loop(0, series)
    def _(s):
        shift = median_ref[0, s].astype(F32) * 0.05
        scaled = (raw_ref[s].astype(F32) - shift) * spread_inverse(s)
        scaled_ref[s] = scaled
        n, _ = norm_stats(scaled)
        rows = (n * again).astype(BF)
        rows_ref[s] = rows
        projected = mm_tn(qkv_ref[...], rows)
        queries = rope(projected[:D], cosine, sine).astype(BF)
        keys = rope(projected[D : 2 * D], cosine, sine).astype(BF)
        values = projected[2 * D :].reshape(HEADS, HEAD_DIM, length).astype(BF)
        q_ref[s] = queries
        k_ref[s] = keys
        wide = queries.astype(F32) * LOG2E_SCALED
        high = wide.astype(BF)
        qa_ref[s, :, :HEAD_DIM] = high
        qa_ref[s, :, HEAD_DIM:] = (wide - high.astype(F32)).astype(BF)
        v_ref[s, :, :HEAD_DIM] = values
        ones = jnp.where(tail_rows < 2, 1.0, 0.0).astype(BF)
        v_ref[s, :, HEAD_DIM:] = jnp.broadcast_to(ones[None], (HEADS, HEAD_DIM, length))

    cut = 16 * ((GROUPS + 1) // 2)

    def half_rows(which, body):
        for c, (lo, hi) in enumerate(((0, cut), (cut, D))):
            @pl.when(core == (c if which == 0 else 1 - c))
            def _():
                body(pl.ds(lo, hi - lo))

    def over_links(k, rows):
        device = (my_dp, lax.rem(my_t + k, n_t))
        return remote(w_ref.at[0, rows], w_ref.at[k, rows], w_send.at[k], w_recv.at[k], device)

    def within_pair(k, rows):
        return remote(w_ref.at[k, rows], w_ref.at[k, rows], w_send2.at[k], w_recv2.at[k], partner)

    def send_weights():
        pl.semaphore_wait(barrier, count - 1)

        def start(rows):
            for k in range(1, n_t):
                over_links(k, rows).start()

        half_rows(0, start)

    def exchange_weights():
        def forward(rows):
            for k in range(1, n_t):
                over_links(k, rows).wait()
                within_pair(k, rows).start()

        half_rows(0, forward)

    def finish_weights():
        def sent(rows):
            for k in range(1, n_t):
                within_pair(k, rows).wait_send()

        def landed(rows):
            for k in range(1, n_t):
                within_pair(k, rows).wait_recv()

        half_rows(0, sent)
        half_rows(1, landed)

    causal = lax.broadcasted_iota(jnp.int32, (BLK, BLK), 0) <= lax.broadcasted_iota(jnp.int32, (BLK, BLK), 1)

    def offset(j):
        return BLK * (j * (j + 1) // 2)


    heads_total = series * HEADS

    def score(i, j, target):
        s, h = i // HEADS, lax.rem(i, HEADS)
        keys = k_ref[s, h]
        lo, hi = j * BLK, (j + 1) * BLK
        scores = mm_tn(jnp.concatenate([keys, keys], axis=0)[:, :hi], qa_ref[s, h, :, lo:hi])
        diagonal = jnp.where(causal, scores[lo:], MASKED)
        scores = jnp.concatenate([scores[:lo], diagonal], axis=0) if j else diagonal
        largest = jnp.max(scores, axis=0, keepdims=True)
        e = jnp.exp2(scores - largest).astype(BF)
        e_ref[i, offset(j) : offset(j) + hi] = e
        if target is not None:
            target[offset(j) : offset(j) + hi] = e

    def mix(i, j, source):
        s, h = i // HEADS, lax.rem(i, HEADS)
        lo, hi = j * BLK, (j + 1) * BLK
        e = e_ref[i, offset(j) : offset(j) + hi] if source is None else source[offset(j) : offset(j) + hi]
        mixed = mm(v_ref[s, h, :, :hi], e)
        inverse = 1.0 / mixed[HEAD_DIM : HEAD_DIM + 1]
        attended = mixed[:HEAD_DIM] * inverse
        linv_ref[s, h, :, lo:hi] = inverse
        o_ref[s, h, :, lo:hi] = attended
        att_ref[s, h, :, lo:hi] = attended.astype(BF)


    for j in range(nblk):
        score(0, j, ds_ref)

    @pl.loop(1, heads_total, step=2)
    def _(i):
        for j in range(nblk):
            score(i, j, ds2_ref)
            mix(i - 1, j, ds_ref)
        for j in range(nblk):
            score(lax.min(i + 1, heads_total - 1), j, ds_ref)
            mix(i, j, ds2_ref)

        @pl.when(i == 3)
        def _():
            send_weights()

        @pl.when(i == 11)
        def _():
            exchange_weights()

    finish_weights()

    ffacc_ref[...] = jnp.zeros_like(ffacc_ref)
    outacc_ref[...] = jnp.zeros_like(outacc_ref)
    gains_ref[...] = jnp.zeros_like(gains_ref)

    @pl.loop(0, series)
    def _(s):
        attended = att_ref[s].reshape(D, length)
        hidden = scaled_ref[s] + mm_tn(out_ref[...], attended)
        n, r = norm_stats(hidden)
        rows = (n * mgain).astype(BF)
        low = cot_ref[s]
        top = low.astype(F32)
        result = hidden
        grad_rows = jnp.zeros((D, length), F32)
        for t in range(n_t):
            gu = w_ref[t, :, : 2 * hidden_local]
            down = w_ref[t, :, 2 * hidden_local :]
            both = mm_tn(gu, rows)
            gate, up = both[:hidden_local], both[hidden_local:]
            grad_inner = mm_tn(down, low)
            sigma = 1.0 / (1.0 + jnp.exp(-gate))
            act = gate * sigma
            inner = (act * up).astype(BF)
            grad_gate = (grad_inner * up * (sigma + act * (1.0 - sigma))).astype(BF)
            grad_up = (grad_inner * act).astype(BF)
            grad_both = jnp.concatenate([grad_gate, grad_up], axis=0)
            result = result + mm(down, inner)
            grad_rows = grad_rows + mm(gu, grad_both)
            gu_piece = mm_nt(rows, grad_both)
            ffacc_ref[t, :D] += gu_piece[:, :hidden_local]
            ffacc_ref[t, D : 2 * D] += gu_piece[:, hidden_local:]
            ffacc_ref[t, 2 * D : 3 * D] += mm_nt(low, inner)

        result_ref[s] = result.astype(BF)
        part, gain_part = norm_backward(grad_rows, n, r, mgain)
        grad_hidden = top + part
        dh_ref[s] = grad_hidden
        branch = grad_hidden.astype(BF)
        outacc_ref[...] += mm_nt(attended, branch)
        gains_ref[:, 0:1] += gain_part
        datt_ref[s] = mm(out_ref[...], branch).astype(BF).reshape(HEADS, HEAD_DIM, length)

    def store_result(s):
        return pltpu.make_async_copy(result_ref.at[s], result_hbm.at[s, 0], local_sem.at[s])

    def store_igrad(s):
        return pltpu.make_async_copy(igrad_ref.at[s], igrad_hbm.at[s, 0], local_sem.at[series + s])

    for s in range(series):
        store_result(s).start()

    share = ffout_ref.shape[1]
    for t in range(n_t):
        staged = ffacc_ref[t].astype(BF).reshape(pairs, 2, share, hidden_local)
        for c in range(2):
            ffstage_ref[c, t] = staged[:, c]
    peers = pairs * n_t
    place = pair * n_t + my_t

    def ff_pair():
        return remote(ffstage_ref.at[1 - core], ffpair_ref, ff_sem.at[0], ff_sem.at[1], partner)

    ff_pair().start()

    def ff_send():
        ff_pair().wait()
        ffhalf_ref[...] = (ffstage_ref[core].astype(F32) + ffpair_ref[...].astype(F32)).astype(BF)

        def part(k):
            peer = lax.rem(place + k, peers)
            peer_pair, peer_t = peer // n_t, lax.rem(peer, n_t)
            piece = ffhalf_ref.at[lax.rem(my_t - peer_t + n_t, n_t), peer_pair]
            remote(piece, ffrecv_ref.at[k - 1], ff_sem.at[2], ff_sem.at[3], (2 * peer_pair + core, peer_t)).start()

        each(1, peers, part)

    def ff_parts():
        return remote(ffrecv_ref, ffrecv_ref, ff_sem.at[2], ff_sem.at[3], to(index))

    def ff_reduce():
        ff_parts().wait_recv()
        total = ffhalf_ref[0, pair].astype(F32) + jnp.sum(ffrecv_ref[...].astype(F32), axis=0)
        ffout_ref[my_dp] = total.astype(BF)

        def whole(k):
            device = (lax.rem(my_dp + k, n_dp), my_t)
            remote(ffout_ref.at[my_dp], ffout_ref.at[my_dp], ff_sem.at[4], ff_sem.at[5], device).start()

        each(1, n_dp, whole)

    def ff_finish():
        ff_parts().wait_send()
        others = ffout_ref.at[pl.ds(0, n_dp - 1)]
        remote(others, others, ff_sem.at[4], ff_sem.at[5], to(index)).wait()
        sums = ffout_ref[...].astype(F32).reshape(-1, hidden_local)
        gateg_ref[...] = sums[:D]
        upg_ref[...] = sums[D : 2 * D]
        downg_ref[...] = sums[2 * D : 3 * D]

    sum0 = GroupSum(index, count, to, 0, stage0, recv0, out0, sems0)
    sum1 = GroupSum(index, count, to, count - 18, stage1, recv1, out1, sems1)
    sum2 = GroupSum(index, count, to, 1, stage2, recv2, out2, sems2)

    def head_grads(parts):
        total = None
        for s in range(series):
            grads = jnp.concatenate([dproj_ref[s, c * HEADS + h] for c, h in parts], axis=0)
            piece = mm_nt(rows_ref[s], grads)
            total = piece if total is None else total + piece
        return total

    def put(stage, grads):
        for t in range(grads.shape[1] // LANES):
            tile = grads[:, t * LANES : (t + 1) * LANES].astype(BF)
            stage[t * GROUPS : (t + 1) * GROUPS] = tile.reshape(GROUPS, 16, LANES)


    def place_of_head(i):
        return lax.rem(i, series), i // series

    def prepare(i, grad_all_ref):
        s, h = place_of_head(i)
        grad = (datt_ref[s, h].astype(F32) * linv_ref[s, h]).astype(BF)
        delta = -jnp.sum(grad.astype(F32) * o_ref[s, h], axis=0, keepdims=True)
        high = delta.astype(BF).astype(F32)
        tail = jnp.where(tail_rows == 0, high, jnp.where(tail_rows == 1, delta - high, 0.0))
        grad_all_ref[:HEAD_DIM] = grad
        grad_all_ref[HEAD_DIM:] = tail.astype(BF)

    def center(i, j, grad_all_ref, target):
        s, h = place_of_head(i)
        lo, hi = j * BLK, (j + 1) * BLK
        weights = e_ref[s * HEADS + h, offset(j) : offset(j) + hi]
        centred = mm_tn(v_ref[s, h, :, :hi], grad_all_ref[:, lo:hi])
        target[offset(j) : offset(j) + hi] = centred.astype(BF) * weights

    def unrotate(g, lo, hi):
        a, b = g[:8], g[8:]
        c, d = cosine[:, lo:hi], sine[:, lo:hi]
        return jnp.concatenate([a * c + b * d, b * c - a * d], axis=0)

    def grad_query(i, j, source):
        s, h = place_of_head(i)
        lo, hi = j * BLK, (j + 1) * BLK
        g = mm(k_ref[s, h, :, :hi], source[offset(j) : offset(j) + hi]) * 0.25
        dproj_ref[s, h, :, lo:hi] = unrotate(g, lo, hi).astype(BF)

    def grad_key(i, j, source):
        s, h = place_of_head(i)
        lo, hi = j * BLK, (j + 1) * BLK
        total = None
        for q in range(j, nblk):
            at = offset(q) + lo
            piece = mm_nt(q_ref[s, h, :, q * BLK : (q + 1) * BLK], source[at : at + BLK])
            total = piece if total is None else total + piece
        dproj_ref[s, HEADS + h, :, lo:hi] = unrotate(total * 0.25, lo, hi).astype(BF)

    def grad_value(i, j, grad_all_ref):
        s, h = place_of_head(i)
        lo, hi = j * BLK, (j + 1) * BLK
        total = None
        for q in range(j, nblk):
            at = offset(q) + lo
            piece = mm_nt(grad_all_ref[:HEAD_DIM, q * BLK : (q + 1) * BLK], e_ref[s * HEADS + h, at : at + BLK])
            total = piece if total is None else total + piece
        dproj_ref[s, 2 * HEADS + h, :, lo:hi] = total.astype(BF)

    def device_of(k):
        peer = lax.rem(place + k, peers)
        return (2 * (peer // n_t) + core, lax.rem(peer, n_t))

    sum3 = HeadSum(*rest[:5], sems3, core, partner, device_of, peers)

    def one_head_grads(h):
        main, rest = None, None
        for s in range(series):
            grads = jnp.concatenate([dproj_ref[s, c * HEADS + h] for c in range(3)], axis=0)
            one, two = mm_nt(grads, rows_ref[s, :LANES]), mm_nt(rows_ref[s, LANES:], grads)
            main, rest = (one, two) if main is None else (main + one, rest + two)
        return main, rest

    put(stage0, jnp.concatenate([outacc_ref[...], gains_ref[:, : 2 * LANES - D]], axis=1))
    sum0.go()

    def products(i, j, source, grad_all_ref):
        grad_query(i, j, source)
        grad_value(i, j, grad_all_ref)
        grad_key(i, j, source)

    prepare(0, ga_ref)
    for j in range(nblk):
        center(0, j, ga_ref, ds_ref)

    @pl.loop(0, heads_total - series, step=2)
    def _(i):
        prepare(i + 1, ga2_ref)
        for j in range(nblk):
            center(i + 1, j, ga2_ref, ds2_ref)
            products(i, j, ds_ref, ga_ref)
        prepare(i + 2, ga_ref)
        for j in range(nblk):
            center(i + 2, j, ga_ref, ds_ref)
            products(i + 1, j, ds2_ref, ga2_ref)

        @pl.when(i == 0)
        def _():
            ff_send()

        @pl.when(i == 3 * series)
        def _():
            ff_reduce()
            sum0.reduce()

        @pl.when(i == 5 * series)
        def _():
            put(stage1, head_grads(STAGE1))
            sum1.go()

        @pl.when(i == 7 * series)
        def _():
            sum1.reduce()
            put(stage2, head_grads(STAGE2))
            sum2.go()

    i = heads_total - 2
    prepare(i + 1, ga2_ref)
    for j in range(nblk):
        center(i + 1, j, ga2_ref, ds2_ref)
        products(i, j, ds_ref, ga_ref)
    for j in range(nblk):
        products(i + 1, j, ds2_ref, ga2_ref)
    sum3.go(*one_head_grads(LAST))

    def back(s):
        grad = dproj_ref[s].reshape(3 * D, length)
        grad_rows = mm(qkv_ref[...], grad)
        n, r = norm_stats(scaled_ref[s])
        part, _ = norm_backward(grad_rows, n, r, again)
        igrad_ref[s] = (dh_ref[s] + part) * spread_inverse(s)

    for s in range(series):
        back(s)
        if s == 0:
            sum3.send()
        store_igrad(s).start()

    ff_finish()
    sum0.finish()
    sum1.finish()
    sum2.reduce()
    fixed = sum(TILES) * LANES
    place_of = jnp.where(
        lax.broadcasted_iota(jnp.int32, (fixed + LANES, source_ref.shape[1]), 0) == source_ref[...], 1.0, 0.0
    ).astype(BF)

    def tiles_of(out, n):
        return [out[t * GROUPS : (t + 1) * GROUPS].reshape(D, LANES) for t in range(n)]

    tiles = tiles_of(out0, TILES[0]) + tiles_of(out1, TILES[1])
    mgaing_ref[...] = to_row(tiles[1][:, D - LANES : D - LANES + 1].astype(F32))
    sums = mm(jnp.concatenate(tiles, axis=1), place_of[: fixed - LANES])
    outg_ref[...] = sums[:, 4 * LANES : 4 * LANES + D]
    for s in range(series):
        store_result(s).wait()
        store_igrad(s).wait()
    sum3.reduce()
    sum2.finish()
    sums = sums[:, : 3 * D] + mm(tiles_of(out2, 1)[0], place_of[fixed - LANES : fixed, : 3 * D])
    sums = sums + mm(sum3.finish(), place_of[fixed:, : 3 * D])
    qkvg_ref[...] = sums
    againg_ref[...] = to_row(jnp.sum(sums * qkv_ref[...].astype(F32), axis=1, keepdims=True) / again)


def rope_tables(length):
    half = HEAD_DIM // 2
    frequency = np.float32(10000.0) ** (-(np.arange(half, dtype=np.float32) * np.float32(2.0) / np.float32(HEAD_DIM)))
    angles = np.arange(length, dtype=np.float32)[None, :] * frequency.astype(np.float32)[:, None]
    return np.cos(angles).astype(np.float32), np.sin(angles).astype(np.float32)


def column_sources():
    source = np.full((1, 4 * LANES + D), -1, np.int32)
    source[0, 4 * LANES :] = np.arange(D)
    first = TILES[0] * LANES
    last = [(c, LAST) for c in range(3)]
    for parts, tiles in zip((STAGE1, STAGE2, last), TILES[1:] + (1,), strict=True):
        for place, (c, h) in enumerate(parts):
            at = c * D + h * HEAD_DIM
            source[0, at : at + HEAD_DIM] = first + place * HEAD_DIM + np.arange(HEAD_DIM)
        first += tiles * LANES
    return source


def copy_kernel(n, *refs):
    sources, results, held, sems = refs[:n], refs[n : 2 * n], refs[2 * n : 3 * n], refs[3 * n]
    takes = [pltpu.make_async_copy(sources[i], held[i], sems.at[0, i]) for i in range(n)]
    gives = [pltpu.make_async_copy(held[i], results[i], sems.at[1, i]) for i in range(n)]
    for copy in takes:
        copy.start()
    for take, give in zip(takes, gives, strict=True):
        take.wait()
        give.start()
    for copy in gives:
        copy.wait()


def hand_over(arrays):
    n = len(arrays)
    place = pl.BlockSpec(memory_space=pltpu.HBM)
    return pl.pallas_call(
        functools.partial(copy_kernel, n),
        out_shape=[jax.ShapeDtypeStruct(a.shape, a.dtype) for a in arrays],
        in_specs=[place] * n,
        out_specs=[place] * n,
        scratch_shapes=[pltpu.VMEM(a.shape, a.dtype) for a in arrays] + [pltpu.SemaphoreType.DMA((2, n))],
    )(*arrays)


def layer(n_dp, n_t, median_code, scale_code, raw, cot, qkv, out, again, gate, up, down, mgain):
    series, _, width, length = raw.shape
    cosine, sine = rope_tables(length)
    source = column_sources()
    blocks = length // BLK
    packed = BLK * blocks * (blocks + 1) // 2
    vmem = pl.BlockSpec(memory_space=pltpu.VMEM)
    smem = pl.BlockSpec(memory_space=pltpu.SMEM)
    anywhere = pl.BlockSpec(memory_space=pl.ANY)
    per_head = (series, HEADS, HEAD_DIM, length)
    rows = (series, width, length)
    count = n_dp * n_t
    pairs = n_dp // 2
    hidden = gate.shape[1]
    share = -(-3 * width // (16 * n_dp)) * 16
    dma = pltpu.SemaphoreType.DMA
    stages = []
    for n in TILES:
        stages += [
            pltpu.VMEM((n * GROUPS, 16, LANES), BF), pltpu.VMEM((count - 1, 16, LANES), BF), pltpu.VMEM((n * GROUPS, 16, LANES), BF),
        ]
    half = (2, 16, LANES)
    one_head = [pltpu.VMEM(shape, BF) for shape in ((2,) + half, half, half, (pairs * n_t - 1,) + half, (2,) + half)]
    return pl.pallas_call(
        functools.partial(kernel, n_dp, n_t),
        out_shape=[
            jax.ShapeDtypeStruct(raw.shape, BF),
            jax.ShapeDtypeStruct(raw.shape, F32),
            jax.ShapeDtypeStruct((width, 3 * width), F32),
            jax.ShapeDtypeStruct((width, width), F32),
            jax.ShapeDtypeStruct((1, width), F32),
            jax.ShapeDtypeStruct((width, hidden), F32),
            jax.ShapeDtypeStruct((width, hidden), F32),
            jax.ShapeDtypeStruct((width, hidden), F32),
            jax.ShapeDtypeStruct((1, width), F32),
        ],
        in_specs=[smem, smem, anywhere, anywhere] + [vmem] * 10,
        out_specs=[anywhere, anywhere] + [vmem] * 7,
        scratch_shapes=[
            pltpu.VMEM(rows, BF),
            pltpu.VMEM(rows, BF),
            pltpu.VMEM(rows, BF),
            pltpu.VMEM(rows, F32),
            pltpu.VMEM((series * HEADS, packed, BLK), BF),
            pltpu.VMEM((packed, BLK), BF),
            pltpu.VMEM((packed, BLK), BF),
            pltpu.VMEM((2 * HEAD_DIM, length), BF),
            pltpu.VMEM((2 * HEAD_DIM, length), BF),
            pltpu.VMEM((series, HEADS, 2 * HEAD_DIM, length), BF),
            pltpu.VMEM(per_head, BF),
            pltpu.VMEM(per_head, BF),
            pltpu.VMEM((series, HEADS, 2 * HEAD_DIM, length), BF),
            pltpu.VMEM(per_head, F32),
            pltpu.VMEM((series, HEADS, 1, length), F32),
            pltpu.VMEM(per_head, BF),
            pltpu.VMEM(per_head, BF),
            pltpu.VMEM((series, 3 * HEADS, HEAD_DIM, length), BF),
            pltpu.VMEM(rows, BF),
            pltpu.VMEM(rows, F32),
            pltpu.VMEM(rows, F32),
            pltpu.VMEM((n_t, width, 3 * hidden), BF),
            pltpu.VMEM((n_t, n_dp * share, hidden), F32),
            pltpu.VMEM((2, n_t, pairs, share, hidden), BF),
            pltpu.VMEM((n_t, pairs, share, hidden), BF),
            pltpu.VMEM((n_t, pairs, share, hidden), BF),
            pltpu.VMEM((pairs * n_t - 1, share, hidden), BF),
            pltpu.VMEM((n_dp, share, hidden), BF),
            pltpu.VMEM((width, width), F32),
            pltpu.VMEM((width, LANES), F32),
            *stages,
            *one_head,
            dma((2 * series,)), dma((n_t,)), dma((n_t,)), dma((n_t,)), dma((n_t,)), dma((6,)), dma((4,)), dma((4,)), dma((4,)), dma((6,)),
        ],
        compiler_params=pltpu.CompilerParams(vmem_limit_bytes=60 * 2**20, collective_id=0, has_side_effects=True),
    )(
        median_code, scale_code, raw, cot, qkv, out, again.reshape(1, -1), gate, up, down, mgain.reshape(1, -1), cosine, sine, source
    )


def local(
    n_dp, n_t, raw_series, median_code, scale_code, qkv_weight, out_weight, attn_gain, gate_weight, up_weight, down_weight,
    mlp_gain, cotangent,
):
    result, input_grad, qkv_grad, out_grad, again_grad, gate_grad, up_grad, down_grad, mgain_grad = hand_over(layer(
        n_dp, n_t, median_code.T, scale_code.T, raw_series.transpose(0, 1, 3, 2), cotangent.transpose(0, 1, 3, 2), qkv_weight,
        out_weight, attn_gain, gate_weight, up_weight, down_weight.T, mlp_gain,
    ))
    return (
        result.transpose(0, 1, 3, 2), input_grad.transpose(0, 1, 3, 2), qkv_grad, out_grad, again_grad[0], gate_grad, up_grad,
        down_grad.T, mgain_grad[0],
    )


def solution(mesh):
    placed = (
        P(None, ("dp", "tensor"), None, None), P(None, ("dp", "tensor")), P(None, ("dp", "tensor")), P(), P(), P(),
        P(None, "tensor"), P(None, "tensor"), P("tensor", None), P(), P(None, ("dp", "tensor"), None, None),
    )
    return jax.shard_map(
        functools.partial(local, mesh.shape["dp"], mesh.shape["tensor"]), mesh=mesh, in_specs=placed,
        out_specs=(
            P(None, ("dp", "tensor"), None, None), P(None, ("dp", "tensor"), None, None), P(), P(), P(),
            P(None, "tensor"), P(None, "tensor"), P("tensor", None), P(),
        ),
        check_vma=False,
    )
```

```python
import functools

import jax
import jax.numpy as jnp
import numpy as np
from jax import lax
from jax.experimental import pallas as pl
from jax.experimental.pallas import tpu as pltpu
from jax.sharding import PartitionSpec as P

BF = jnp.bfloat16
F32 = jnp.float32
MESH = pl.DeviceIdType.MESH
HEADS = 9
HEAD_DIM = 16
D = HEADS * HEAD_DIM
LANES = 128
GROUPS = D // 16
BLK = 256
HALF = BLK // 2
EPS = 1e-05
MASKED = -1e30
LOG2E_SCALED = 0.25 * 1.4426950408889634

STAGE1 = [(c, h) for c in range(3) for h in range(4)]
STAGE2 = [(c, h) for c in range(3) for h in range(4, 8)]
LAST = HEADS - 1
TILES = (2, 2, 2)


def mm(a, b):
    return lax.dot_general(a, b, (((1,), (0,)), ((), ())), preferred_element_type=F32)


def mm_tn(a, b):
    return lax.dot_general(a, b, (((0,), (0,)), ((), ())), preferred_element_type=F32)


def mm_nt(a, b):
    return lax.dot_general(a, b, (((1,), (1,)), ((), ())), preferred_element_type=F32)


def eye(n):
    same = lax.broadcasted_iota(jnp.int32, (n, n), 0) == lax.broadcasted_iota(jnp.int32, (n, n), 1)
    return jnp.where(same, 1.0, 0.0)


def to_column(row):
    return jnp.sum(eye(row.shape[1]) * row, axis=1, keepdims=True)


def to_row(column):
    return jnp.sum(eye(column.shape[0]) * column, axis=0, keepdims=True)


def norm_stats(rows):
    r = lax.rsqrt(jnp.mean(rows * rows, axis=0, keepdims=True) + EPS)
    return rows * r, r


def norm_backward(e, n, r, gain):
    weighted = e * gain
    mean = jnp.mean(weighted * n, axis=0, keepdims=True)
    return r * (weighted - n * mean), jnp.sum(e * n, axis=1, keepdims=True)


def rope(x, cosine, sine):
    length = x.shape[1]
    x = x.reshape(HEADS, 2, 8, length)
    a, b = x[:, 0], x[:, 1]
    first = a * cosine - b * sine
    second = a * sine + b * cosine
    return jnp.concatenate([first[:, None], second[:, None]], axis=1).reshape(HEADS, HEAD_DIM, length)


def each(first, last, body):
    if last - first <= 40:
        for k in range(first, last):
            body(k)
    else:
        pl.loop(first, last)(body)


def remote(src, dst, send_sem, recv_sem, device):
    return pltpu.make_async_remote_copy(
        src_ref=src, dst_ref=dst, send_sem=send_sem, recv_sem=recv_sem, device_id=device, device_id_type=MESH
    )


class GroupSum:
    def __init__(self, index, count, to, first, stage, recv, out, sems):
        self.index, self.count, self.to, self.first = index, count, to, first
        self.stage, self.recv, self.out = stage, recv, out
        self.send, self.land, self.spread, self.gather = (sems.at[i] for i in range(4))
        self.groups = stage.shape[0]
        self.stride = max(count // self.groups, 1)
        place = lax.rem(index + count - first, count)
        self.mine = place // self.stride
        self.owner = (lax.rem(place, self.stride) == 0) & (self.mine < self.groups)

    def go(self):
        def part(g):
            owner = lax.rem(g * self.stride + self.first, self.count)

            @pl.when(owner != self.index)
            def _():
                slot = lax.rem(owner - self.index + self.count, self.count) - 1
                remote(self.stage.at[g], self.recv.at[slot], self.send, self.land, self.to(owner)).start()

        each(0, self.groups, part)

    def _all_parts(self):
        return remote(self.recv, self.recv, self.spread, self.land, self.to(self.index))

    def reduce(self):
        @pl.when(self.owner)
        def _():
            self._all_parts().wait_recv()
            total = self.stage[self.mine].astype(F32) + jnp.sum(self.recv[...].astype(F32), axis=0)
            self.out[self.mine] = total.astype(BF)

            def whole(k):
                device = self.to(lax.rem(self.index + k, self.count))
                remote(self.out.at[self.mine], self.out.at[self.mine], self.spread, self.gather, device).start()

            each(1, self.count, whole)

    def finish(self):
        def landed(n):
            stage, out = self.stage.at[pl.ds(0, n)], self.out.at[pl.ds(0, n)]
            both = remote(stage, out, self.send, self.gather, self.to(self.index))
            both.wait_recv()
            both.wait_send()

        @pl.when(self.owner)
        def _():
            if self.groups > 1:
                landed(self.groups - 1)
            self._all_parts().wait_send()

        @pl.when(jnp.logical_not(self.owner))
        def _():
            landed(self.groups)


class HeadSum:
    def __init__(self, own, pair, half, recv, total, sems, core, partner, device_of, peers):
        self.own, self.pair, self.half, self.recv, self.total = own, pair, half, recv, total
        self.sems, self.core, self.partner, self.device_of, self.peers = sems, core, partner, device_of, peers

    def _exchange(self):
        return remote(self.own.at[1 - self.core], self.pair, self.sems.at[0], self.sems.at[1], self.partner)

    def go(self, main, rest):
        main = main.astype(BF).reshape(3, 16, LANES)
        self.own[0] = main[:2]
        self.own[1, 0] = main[2]
        self.own[1, 1] = jnp.concatenate([rest, jnp.zeros((16, LANES - rest.shape[1]), F32)], axis=1).astype(BF)
        self._exchange().start()

    def send(self):
        self._exchange().wait()
        self.half[...] = (self.own[self.core].astype(F32) + self.pair[...].astype(F32)).astype(BF)
        for_peer = lambda k: remote(self.half, self.recv.at[k - 1], self.sems.at[2], self.sems.at[3], self.device_of(k)).start()
        each(1, self.peers, for_peer)

    def _back(self):
        piece = self.total.at[self.core]
        return remote(piece, piece, self.sems.at[4], self.sems.at[5], self.partner)

    def reduce(self):
        remote(self.recv, self.recv, self.sems.at[2], self.sems.at[3], self.partner).wait()
        self.total[self.core] = (self.half[...].astype(F32) + jnp.sum(self.recv[...].astype(F32), axis=0)).astype(BF)
        self._back().start()

    def finish(self):
        self._back().wait()
        turn = jnp.where(
            lax.broadcasted_iota(jnp.int32, (48, LANES), 0) == lax.broadcasted_iota(jnp.int32, (48, LANES), 1), 1.0, 0.0
        ).astype(BF)
        total = self.total[...].reshape(4, 16, LANES)
        return jnp.concatenate([mm_tn(total[:3].reshape(48, LANES), turn).astype(BF), total[3]], axis=0)


def kernel(
    n_dp, n_t,
    median_ref, scale_ref, raw_hbm, cot_hbm, qkv_ref, out_ref, again_ref, gate_ref, up_ref, down_ref, mgain_ref, cos_ref, sin_ref,
    source_ref,
    result_ref, igrad_ref, qkvg_ref, outg_ref, againg_ref, gateg_ref, upg_ref, downg_ref, mgaing_ref,
    raw_ref, cot_ref,
    e_ref, held0_ref, held1_ref, largest_ref, ds_ref, ds2_ref, dt_ref, dt2_ref, ga_ref, ga2_ref, qa_ref, q_ref, k_ref, v_ref, o_ref, linv_ref, att_ref, dproj_ref, rows_ref, scaled_ref,
    w_ref, inner_ref, ffacc_ref, ffstage_ref, ffpair_ref, ffhalf_ref, ffrecv_ref, ffout_ref, outacc_ref, gains_ref,
    stage0, recv0, out0, stage1, recv1, out1, stage2, recv2, out2, *rest,
):
    local_sem, w_send, w_recv, w_send2, w_recv2, ff_sem, sems0, sems1, sems2, sems3 = rest[5:]
    held_refs = (held0_ref, held1_ref)
    series, _, _, length = raw_hbm.shape
    nblk = length // BLK
    hidden_local = gate_ref.shape[1]
    count = n_dp * n_t
    my_dp, my_t = lax.axis_index("dp"), lax.axis_index("tensor")
    index = my_dp * n_t + my_t
    core = lax.rem(my_dp, 2)
    pair = my_dp // 2
    partner = (my_dp + 1 - 2 * core, my_t)
    pairs = n_dp // 2

    def to(device):
        return (device // n_t, lax.rem(device, n_t))

    loads = [pltpu.make_async_copy(raw_hbm.at[s, 0], raw_ref.at[s], local_sem.at[s]) for s in range(series)]
    loads += [pltpu.make_async_copy(cot_hbm.at[s, 0], cot_ref.at[s], local_sem.at[series + s]) for s in range(series)]
    for copy in loads:
        copy.start()

    barrier = pltpu.get_barrier_semaphore()

    def greet(k):
        pl.semaphore_signal(barrier, inc=1, device_id=to(lax.rem(index + k, count)), device_id_type=MESH)

    each(1, count, greet)

    cosine, sine = cos_ref[...], sin_ref[...]
    again, mgain = to_column(again_ref[...]), to_column(mgain_ref[...])

    def spread_inverse(s):
        return 1.0 / jnp.full((1, length), scale_ref[0, s].astype(F32) * 0.25, F32)

    def scaled_series(s):
        return (raw_ref[s].astype(F32) - median_ref[0, s].astype(F32) * 0.05) * spread_inverse(s)

    tail_rows = lax.broadcasted_iota(jnp.int32, (HEAD_DIM, length), 0)
    w_ref[0, :, :hidden_local] = gate_ref[...]
    w_ref[0, :, hidden_local : 2 * hidden_local] = up_ref[...]
    w_ref[0, :, 2 * hidden_local :] = down_ref[...]
    for copy in loads:
        copy.wait()

    @pl.loop(0, series)
    def _(s):
        scaled = scaled_series(s)
        scaled_ref[s] = scaled
        n, _ = norm_stats(scaled)
        rows = (n * again).astype(BF)
        rows_ref[s] = rows
        projected = mm_tn(qkv_ref[...], rows)
        queries = rope(projected[:D], cosine, sine).astype(BF)
        keys = rope(projected[D : 2 * D], cosine, sine).astype(BF)
        values = projected[2 * D :].reshape(HEADS, HEAD_DIM, length).astype(BF)
        q_ref[s] = queries
        k_ref[s] = keys
        wide = queries.astype(F32) * LOG2E_SCALED
        high = wide.astype(BF)
        qa_ref[s, :, :HEAD_DIM] = high
        qa_ref[s, :, HEAD_DIM:] = (wide - high.astype(F32)).astype(BF)
        v_ref[s, :, :HEAD_DIM] = values
        ones = jnp.where(tail_rows < 2, 1.0, 0.0).astype(BF)
        v_ref[s, :, HEAD_DIM:] = jnp.broadcast_to(ones[None], (HEADS, HEAD_DIM, length))

    cut = 16 * ((GROUPS + 1) // 2)

    def half_rows(which, body):
        for c, (lo, hi) in enumerate(((0, cut), (cut, D))):
            @pl.when(core == (c if which == 0 else 1 - c))
            def _():
                body(pl.ds(lo, hi - lo))

    def over_links(k, rows):
        device = (my_dp, lax.rem(my_t + k, n_t))
        return remote(w_ref.at[0, rows], w_ref.at[k, rows], w_send.at[k], w_recv.at[k], device)

    def within_pair(k, rows):
        return remote(w_ref.at[k, rows], w_ref.at[k, rows], w_send2.at[k], w_recv2.at[k], partner)

    def send_weights():
        pl.semaphore_wait(barrier, count - 1)

        def start(rows):
            for k in range(1, n_t):
                over_links(k, rows).start()

        half_rows(0, start)

    def exchange_weights():
        def forward(rows):
            for k in range(1, n_t):
                over_links(k, rows).wait()
                within_pair(k, rows).start()

        half_rows(0, forward)

    def finish_weights():
        def sent(rows):
            for k in range(1, n_t):
                within_pair(k, rows).wait_send()

        def landed(rows):
            for k in range(1, n_t):
                within_pair(k, rows).wait_recv()

        half_rows(0, sent)
        half_rows(1, landed)

    up_allowed = lax.broadcasted_iota(jnp.int32, (HALF, BLK), 0) <= lax.broadcasted_iota(jnp.int32, (HALF, BLK), 1)
    side = lax.broadcasted_iota(jnp.int32, (HALF, BLK), 1)
    side = jnp.where(side < HALF, side, side - HALF)
    side_allowed = lax.broadcasted_iota(jnp.int32, (HALF, BLK), 0) <= side

    def bounds(j):
        return j * BLK, j * BLK + HALF, (j + 1) * BLK

    def segments(j):
        _, mid, _ = bounds(j)
        at = BLK * j * (j - 1) + (BLK + HALF) * j
        return slice(at, at + mid), slice(at + mid, at + 2 * mid), slice(at + 2 * mid, at + 2 * mid + HALF)

    def key_segments(i):
        rest = length - bounds(i)[1]
        at = sum(2 * (length - bounds(k)[1]) + HALF for k in range(i))
        return slice(at, at + rest), slice(at + rest, at + 2 * rest), slice(at + 2 * rest, at + 2 * rest + HALF)

    def turn_to_keys(j, own, shared, target):
        lo, mid, _ = bounds(j)
        main = key_segments(j)
        for s in range(2):
            for i in range(j):
                at = key_segments(i)[s].start + lo - bounds(i)[1]
                target[at : at + BLK] = own[s][i * BLK : (i + 1) * BLK].T
            turned = own[s][lo:mid].T
            target[main[2], halves(s)] = turned[:HALF]
            at = main[s].start
            target[at : at + HALF, halves(0)] = turned[HALF:]
            target[at : at + HALF, halves(1)] = shared[:, halves(s)].T

    def turn_to_queries(i, own, shared, target):
        lo, mid, hi = bounds(i)
        main = segments(i)
        for s in range(2):
            turned = own[s][:HALF].T
            at = main[s].start + lo
            target[at : at + HALF, halves(1)] = turned[:HALF]
            target[main[2], halves(s)] = turned[HALF:]
            target[at : at + HALF, halves(0)] = shared[:, halves(s)].T
            for j in range(i + 1, nblk):
                at = segments(j)[s].start + lo
                first = bounds(j)[0] - mid
                target[at : at + BLK] = own[s][first : first + BLK].T

    def halves(s):
        return slice(s * HALF, (s + 1) * HALF)

    def side_by_side(a, b):
        zero = jnp.zeros_like(a)
        return jnp.concatenate([jnp.concatenate([a, zero], axis=1), jnp.concatenate([zero, b], axis=1)], axis=0)

    def score(h, j):
        lo, mid, hi = bounds(j)
        held = held_refs[j % 2]
        keys = [jnp.concatenate([k_ref[s, h], k_ref[s, h]], axis=0) for s in range(2)]
        queries = [qa_ref[s, h, :, lo:hi] for s in range(2)]
        shared = mm_tn(
            jnp.concatenate([keys[s][:, mid:hi] for s in range(2)], axis=0),
            side_by_side(queries[0][:, HALF:], queries[1][:, HALF:]),
        )
        shared = jnp.where(side_allowed, shared, MASKED)
        held[2 * mid : 2 * mid + HALF] = shared
        shared_largest = jnp.max(shared, axis=0, keepdims=True)
        for s in range(2):
            scores = mm_tn(keys[s][:, :mid], queries[s])
            diagonal = jnp.where(up_allowed, scores[lo:], MASKED)
            scores = jnp.concatenate([scores[:lo], diagonal], axis=0) if j else diagonal
            held[s * mid : (s + 1) * mid] = scores
            top = jnp.max(scores, axis=0, keepdims=True)
            right = jnp.maximum(top[:, HALF:], shared_largest[:, halves(s)])
            largest_ref[j % 2, s : s + 1] = jnp.concatenate([top[:, :HALF], right], axis=1)

    def softmax(h, j, target):
        lo, mid, hi = bounds(j)
        held = held_refs[j % 2]
        largest = [largest_ref[j % 2, s : s + 1] for s in range(2)]
        weights = [jnp.exp2(held[s * mid : (s + 1) * mid] - largest[s]) for s in range(2)]
        side_largest = jnp.concatenate([largest[0][:, HALF:], largest[1][:, HALF:]], axis=1)
        weights.append(jnp.exp2(held[2 * mid : 2 * mid + HALF] - side_largest))
        shared_total = jnp.sum(weights[2], axis=0, keepdims=True)
        for s in range(2):
            total = jnp.sum(weights[s], axis=0, keepdims=True)
            total = jnp.concatenate([total[:, :HALF], total[:, HALF:] + shared_total[:, halves(s)]], axis=1)
            linv_ref[s, h, :, lo:hi] = 1.0 / total
        weights = [e.astype(BF) for e in weights]
        for rows, e in zip(segments(j), weights, strict=True):
            target[rows] = e
        turn_to_keys(j, weights[:2], weights[2], e_ref.at[h])

    def from_segments(j, left, source):
        _, mid, hi = bounds(j)
        segs = segments(j)
        shared = mm(jnp.concatenate([left[s][:, mid:hi] for s in range(2)], axis=0), source[segs[2]])
        out = []
        for s in range(2):
            own = mm(left[s][:, :mid], source[segs[s]])
            right = own[:, HALF:] + shared[s * HEAD_DIM : (s + 1) * HEAD_DIM, halves(s)]
            out.append(jnp.concatenate([own[:, :HALF], right], axis=1))
        return out

    def mix(h, j, source):
        lo, _, hi = bounds(j)
        mixed = from_segments(j, [v_ref[s, h, :HEAD_DIM] for s in range(2)], source)
        for s in range(2):
            attended = mixed[s] * linv_ref[s, h, :, lo:hi]
            o_ref[s, h, :, lo:hi] = attended
            att_ref[s, h, :, lo:hi] = attended.astype(BF)

    score(0, 0)
    for j in range(1, nblk):
        score(0, j)
        softmax(0, j - 1, ds_ref)

    def step(h, now, before):
        for j in range(nblk):
            score(h, j)
            if j:
                softmax(h, j - 1, now)
            else:
                softmax(h - 1, nblk - 1, before)
            mix(h - 1, j, before)

    @pl.loop(1, HEADS, step=2)
    def _(h):
        step(h, ds2_ref, ds_ref)
        step(h + 1, ds_ref, ds2_ref)

        @pl.when(h == 1)
        def _():
            send_weights()

        @pl.when(h == 5)
        def _():
            exchange_weights()

    softmax(HEADS - 1, nblk - 1, ds_ref)
    for j in range(nblk):
        mix(HEADS - 1, j, ds_ref)

    finish_weights()

    ffacc_ref[...] = jnp.zeros_like(ffacc_ref)
    outacc_ref[...] = jnp.zeros_like(outacc_ref)
    gains_ref[...] = jnp.zeros_like(gains_ref)

    @pl.loop(0, series)
    def _(s):
        attended = att_ref[s].reshape(D, length)
        hidden = scaled_ref[s] + mm_tn(out_ref[...], attended)
        n, r = norm_stats(hidden)
        rows = (n * mgain).astype(BF)
        low = cot_ref[s]
        top = low.astype(F32)
        scaled_ref[s] = hidden
        grad_rows = jnp.zeros((D, length), F32)
        for t in range(n_t):
            gu = w_ref[t, :, : 2 * hidden_local]
            down = w_ref[t, :, 2 * hidden_local :]
            both = mm_tn(gu, rows)
            gate, up = both[:hidden_local], both[hidden_local:]
            grad_inner = mm_tn(down, low)
            sigma = 1.0 / (1.0 + jnp.exp(-gate))
            act = gate * sigma
            inner = (act * up).astype(BF)
            inner_ref[s, t * hidden_local : (t + 1) * hidden_local] = inner
            grad_gate = (grad_inner * up * (sigma + act * (1.0 - sigma))).astype(BF)
            grad_up = (grad_inner * act).astype(BF)
            grad_both = jnp.concatenate([grad_gate, grad_up], axis=0)
            grad_rows = grad_rows + mm(gu, grad_both)
            gu_piece = mm_nt(rows, grad_both)
            ffacc_ref[t, :D] += gu_piece[:, :hidden_local]
            ffacc_ref[t, D : 2 * D] += gu_piece[:, hidden_local:]
            ffacc_ref[t, 2 * D : 3 * D] += mm_nt(low, inner)

        part, gain_part = norm_backward(grad_rows, n, r, mgain)
        grad_hidden = top + part
        igrad_ref[s, 0] = grad_hidden
        branch = grad_hidden.astype(BF)
        outacc_ref[...] += mm_nt(attended, branch)
        gains_ref[:, 0:1] += gain_part
        att_ref[s] = mm(out_ref[...], branch).astype(BF).reshape(HEADS, HEAD_DIM, length)

    share = ffout_ref.shape[1]
    for t in range(n_t):
        staged = ffacc_ref[t].astype(BF).reshape(pairs, 2, share, hidden_local)
        for c in range(2):
            ffstage_ref[c, t] = staged[:, c]
    peers = pairs * n_t
    place = pair * n_t + my_t

    def ff_pair():
        return remote(ffstage_ref.at[1 - core], ffpair_ref, ff_sem.at[0], ff_sem.at[1], partner)

    ff_pair().start()

    def ff_send():
        ff_pair().wait()
        ffhalf_ref[...] = (ffstage_ref[core].astype(F32) + ffpair_ref[...].astype(F32)).astype(BF)

        def part(k):
            peer = lax.rem(place + k, peers)
            peer_pair, peer_t = peer // n_t, lax.rem(peer, n_t)
            piece = ffhalf_ref.at[lax.rem(my_t - peer_t + n_t, n_t), peer_pair]
            remote(piece, ffrecv_ref.at[k - 1], ff_sem.at[2], ff_sem.at[3], (2 * peer_pair + core, peer_t)).start()

        each(1, peers, part)

    def ff_parts():
        return remote(ffrecv_ref, ffrecv_ref, ff_sem.at[2], ff_sem.at[3], to(index))

    def ff_reduce():
        ff_parts().wait_recv()
        total = ffhalf_ref[0, pair].astype(F32) + jnp.sum(ffrecv_ref[...].astype(F32), axis=0)
        ffout_ref[my_dp] = total.astype(BF)

        def whole(k):
            device = (lax.rem(my_dp + k, n_dp), my_t)
            remote(ffout_ref.at[my_dp], ffout_ref.at[my_dp], ff_sem.at[4], ff_sem.at[5], device).start()

        each(1, n_dp, whole)

    def ff_finish():
        ff_parts().wait_send()
        others = ffout_ref.at[pl.ds(0, n_dp - 1)]
        remote(others, others, ff_sem.at[4], ff_sem.at[5], to(index)).wait()
        sums = ffout_ref[...].astype(F32).reshape(-1, hidden_local)
        gateg_ref[...] = sums[:D]
        upg_ref[...] = sums[D : 2 * D]
        downg_ref[...] = sums[2 * D : 3 * D]

    sum0 = GroupSum(index, count, to, 0, stage0, recv0, out0, sems0)
    sum1 = GroupSum(index, count, to, count - 18, stage1, recv1, out1, sems1)
    sum2 = GroupSum(index, count, to, 7, stage2, recv2, out2, sems2)

    def head_grads(parts):
        total = None
        for s in range(series):
            grads = jnp.concatenate([dproj_ref[s, c * HEADS + h] for c, h in parts], axis=0)
            piece = mm_nt(rows_ref[s], grads)
            total = piece if total is None else total + piece
        spare = -total.shape[1] % LANES
        return jnp.concatenate([total, jnp.zeros((D, spare), F32)], axis=1)

    def put(stage, grads):
        for t in range(grads.shape[1] // LANES):
            tile = grads[:, t * LANES : (t + 1) * LANES].astype(BF)
            stage[t * GROUPS : (t + 1) * GROUPS] = tile.reshape(GROUPS, 16, LANES)


    def device_of(k):
        peer = lax.rem(place + k, peers)
        return (2 * (peer // n_t) + core, lax.rem(peer, n_t))

    sum3 = HeadSum(*rest[:5], sems3, core, partner, device_of, peers)

    def one_head_grads(h):
        main, rest = None, None
        for s in range(series):
            grads = jnp.concatenate([dproj_ref[s, c * HEADS + h] for c in range(3)], axis=0)
            one, two = mm_nt(grads, rows_ref[s, :LANES]), mm_nt(rows_ref[s, LANES:], grads)
            main, rest = (one, two) if main is None else (main + one, rest + two)
        return main, rest

    put(stage0, jnp.concatenate([outacc_ref[...], gains_ref[:, : 2 * LANES - D]], axis=1))
    sum0.go()

    def prepare(h, grad_ref):
        for s in range(2):
            grad = (att_ref[s, h].astype(F32) * linv_ref[s, h]).astype(BF)
            delta = -jnp.sum(grad.astype(F32) * o_ref[s, h], axis=0, keepdims=True)
            high = delta.astype(BF).astype(F32)
            tail = jnp.where(tail_rows == 0, high, jnp.where(tail_rows == 1, delta - high, 0.0))
            grad_ref[s, :HEAD_DIM] = grad
            grad_ref[s, HEAD_DIM:] = tail.astype(BF)

    def center(h, i, grad_ref, target, turned):
        lo, mid, hi = bounds(i)
        segs = key_segments(i)
        values = [v_ref[s, h] for s in range(2)]
        shared = mm_tn(
            jnp.concatenate([grad_ref[s, :, lo:mid] for s in range(2)], axis=0),
            side_by_side(values[0][:, lo:mid], values[1][:, lo:mid]),
        )
        shared = shared.astype(BF) * e_ref[h, segs[2]]
        target[segs[2]] = shared
        own = []
        for s in range(2):
            centred = mm_tn(grad_ref[s, :, mid:], values[s][:, lo:hi])
            own.append(centred.astype(BF) * e_ref[h, segs[s]])
            target[segs[s]] = own[s]
        turn_to_queries(i, own, shared, turned)

    def from_key_segments(i, left, source):
        lo, mid, _ = bounds(i)
        segs = key_segments(i)
        shared = mm(jnp.concatenate([left[s][:, lo:mid] for s in range(2)], axis=0), source[segs[2]])
        out = []
        for s in range(2):
            own = mm(left[s][:, mid:], source[segs[s]])
            first = own[:, :HALF] + shared[s * HEAD_DIM : (s + 1) * HEAD_DIM, halves(s)]
            out.append(jnp.concatenate([first, own[:, HALF:]], axis=1))
        return out

    def unrotate(g, lo, hi):
        a, b = g[:8], g[8:]
        c, d = cosine[:, lo:hi], sine[:, lo:hi]
        return jnp.concatenate([a * c + b * d, b * c - a * d], axis=0)

    def products(h, source, turned, grad_ref, between):
        queries = [q_ref[s, h] for s in range(2)]
        grads = [grad_ref[s, :HEAD_DIM] for s in range(2)]
        keys = [k_ref[s, h] for s in range(2)]
        for j in range(nblk):
            between(j)
            lo, _, hi = bounds(j)
            for s, g in enumerate(from_key_segments(j, grads, e_ref.at[h])):
                dproj_ref[s, 2 * HEADS + h, :, lo:hi] = g.astype(BF)
            for s, g in enumerate(from_key_segments(j, queries, source)):
                dproj_ref[s, HEADS + h, :, lo:hi] = unrotate(g * 0.25, lo, hi).astype(BF)
            for s, g in enumerate(from_segments(nblk - 1 - j, keys, turned)):
                lo, _, hi = bounds(nblk - 1 - j)
                dproj_ref[s, h, :, lo:hi] = unrotate(g * 0.25, lo, hi).astype(BF)

    prepare(0, ga_ref)
    for j in range(nblk):
        center(0, j, ga_ref, ds_ref, dt_ref)
    ff_send()

    def step_back(h, source, turned, grad_ref, next_source, next_turned, next_grad_ref):
        prepare(h + 1, next_grad_ref)
        products(h, source, turned, grad_ref, lambda j: center(h + 1, j, next_grad_ref, next_source, next_turned))

    even, odd = (ds_ref, dt_ref, ga_ref), (ds2_ref, dt2_ref, ga2_ref)

    @pl.loop(0, HEADS - 3, step=2)
    def _(h):
        step_back(h, *even, *odd)
        step_back(h + 1, *odd, *even)

        @pl.when(h == 2)
        def _():
            put(stage1, head_grads(STAGE1))
            sum1.go()

        @pl.when(h == 4)
        def _():
            ff_reduce()
            sum0.reduce()

    step_back(HEADS - 3, *even, *odd)
    sum1.reduce()
    step_back(HEADS - 2, *odd, *even)
    put(stage2, head_grads(STAGE2))
    sum2.go()
    products(HEADS - 1, *even, lambda j: None)
    sum3.go(*one_head_grads(LAST))

    def back(s):
        grad = dproj_ref[s].reshape(3 * D, length)
        grad_rows = mm(qkv_ref[...], grad)
        n, r = norm_stats(scaled_series(s))
        part, _ = norm_backward(grad_rows, n, r, again)
        igrad_ref[s, 0] = (igrad_ref[s, 0] + part) * spread_inverse(s)

    for s in range(series):
        back(s)
        if s == 0:
            sum3.send()
    down_wide = jnp.concatenate([w_ref[t, :, 2 * hidden_local :] for t in range(n_t)], axis=1)
    for s in range(series):
        result_ref[s, 0] = (scaled_ref[s] + mm(down_wide, inner_ref[s])).astype(BF)

    sum2.reduce()
    ff_finish()
    sum0.finish()
    sum1.finish()
    fixed = sum(TILES) * LANES
    place_of = jnp.where(
        lax.broadcasted_iota(jnp.int32, (fixed + LANES, source_ref.shape[1]), 0) == source_ref[...], 1.0, 0.0
    ).astype(BF)

    def tiles_of(out, n):
        return [out[t * GROUPS : (t + 1) * GROUPS].reshape(D, LANES) for t in range(n)]

    tiles = tiles_of(out0, TILES[0]) + tiles_of(out1, TILES[1])
    mgaing_ref[...] = to_row(tiles[1][:, D - LANES : D - LANES + 1].astype(F32))
    before = sum(TILES[:2]) * LANES
    sums = mm(jnp.concatenate(tiles, axis=1), place_of[:before])
    outg_ref[...] = sums[:, 4 * LANES : 4 * LANES + D]
    sum3.reduce()
    sum2.finish()
    sums = sums[:, : 3 * D] + mm(jnp.concatenate(tiles_of(out2, TILES[2]), axis=1), place_of[before:fixed, : 3 * D])
    sums = sums + mm(sum3.finish(), place_of[fixed:, : 3 * D])
    qkvg_ref[...] = sums
    againg_ref[...] = to_row(jnp.sum(sums * qkv_ref[...].astype(F32), axis=1, keepdims=True) / again)


def rope_tables(length):
    half = HEAD_DIM // 2
    frequency = np.float32(10000.0) ** (-(np.arange(half, dtype=np.float32) * np.float32(2.0) / np.float32(HEAD_DIM)))
    angles = np.arange(length, dtype=np.float32)[None, :] * frequency.astype(np.float32)[:, None]
    return np.cos(angles).astype(np.float32), np.sin(angles).astype(np.float32)


def column_sources():
    source = np.full((1, 4 * LANES + D), -1, np.int32)
    source[0, 4 * LANES :] = np.arange(D)
    first = TILES[0] * LANES
    last = [(c, LAST) for c in range(3)]
    for parts, tiles in zip((STAGE1, STAGE2, last), TILES[1:] + (1,), strict=True):
        for place, (c, h) in enumerate(parts):
            at = c * D + h * HEAD_DIM
            source[0, at : at + HEAD_DIM] = first + place * HEAD_DIM + np.arange(HEAD_DIM)
        first += tiles * LANES
    return source


def copy_kernel(n, *refs):
    sems = refs[2 * n]
    copies = [pltpu.make_async_copy(refs[i], refs[n + i], sems.at[i]) for i in range(n)]
    for copy in copies:
        copy.start()
    for copy in copies:
        copy.wait()


def hand_over(arrays):
    n = len(arrays)
    return pl.pallas_call(
        functools.partial(copy_kernel, n),
        out_shape=[jax.ShapeDtypeStruct(a.shape, a.dtype) for a in arrays],
        in_specs=[pl.BlockSpec(memory_space=pltpu.VMEM)] * n,
        out_specs=[pl.BlockSpec(memory_space=pltpu.HBM)] * n,
        scratch_shapes=[pltpu.SemaphoreType.DMA((n,))],
    )(*[pltpu.with_memory_space_constraint(a, pltpu.VMEM) for a in arrays])


def layer(n_dp, n_t, median_code, scale_code, raw, cot, qkv, out, again, gate, up, down, mgain):
    series, _, width, length = raw.shape
    cosine, sine = rope_tables(length)
    source = column_sources()
    blocks = length // BLK
    packed = BLK * blocks * (blocks - 1) + (BLK + HALF) * blocks
    vmem = pl.BlockSpec(memory_space=pltpu.VMEM)
    smem = pl.BlockSpec(memory_space=pltpu.SMEM)
    anywhere = pl.BlockSpec(memory_space=pl.ANY)
    per_head = (series, HEADS, HEAD_DIM, length)
    rows = (series, width, length)
    count = n_dp * n_t
    pairs = n_dp // 2
    hidden = gate.shape[1]
    share = -(-3 * width // (16 * n_dp)) * 16
    dma = pltpu.SemaphoreType.DMA
    landing = 2 * LANES * (len(TILES) * (count - 1) * 16 + (pairs * n_t - 1) * (share + 32))
    stages = []
    for n in TILES:
        stages += [
            pltpu.VMEM((n * GROUPS, 16, LANES), BF), pltpu.VMEM((count - 1, 16, LANES), BF), pltpu.VMEM((n * GROUPS, 16, LANES), BF),
        ]
    half = (2, 16, LANES)
    one_head = [pltpu.VMEM(shape, BF) for shape in ((2,) + half, half, half, (pairs * n_t - 1,) + half, (2,) + half)]
    return pl.pallas_call(
        functools.partial(kernel, n_dp, n_t),
        out_shape=[
            pltpu.VMEM(raw.shape, BF),
            pltpu.VMEM(raw.shape, F32),
            pltpu.VMEM((width, 3 * width), F32),
            pltpu.VMEM((width, width), F32),
            pltpu.VMEM((1, width), F32),
            pltpu.VMEM((width, hidden), F32),
            pltpu.VMEM((width, hidden), F32),
            pltpu.VMEM((width, hidden), F32),
            pltpu.VMEM((1, width), F32),
        ],
        in_specs=[smem, smem, anywhere, anywhere] + [vmem] * 10,
        out_specs=[vmem] * 9,
        scratch_shapes=[
            pltpu.VMEM(rows, BF),
            pltpu.VMEM(rows, BF),
            pltpu.VMEM((HEADS, packed, BLK), BF),
            pltpu.VMEM((2 * length - 2 * BLK - HALF, BLK), F32),
            pltpu.VMEM((2 * length - HALF, BLK), F32),
            pltpu.VMEM((2, 2, BLK), F32),
            pltpu.VMEM((packed, BLK), BF),
            pltpu.VMEM((packed, BLK), BF),
            pltpu.VMEM((packed, BLK), BF),
            pltpu.VMEM((packed, BLK), BF),
            pltpu.VMEM((series, 2 * HEAD_DIM, length), BF),
            pltpu.VMEM((series, 2 * HEAD_DIM, length), BF),
            pltpu.VMEM((series, HEADS, 2 * HEAD_DIM, length), BF),
            pltpu.VMEM(per_head, BF),
            pltpu.VMEM(per_head, BF),
            pltpu.VMEM((series, HEADS, 2 * HEAD_DIM, length), BF),
            pltpu.VMEM(per_head, F32),
            pltpu.VMEM((series, HEADS, 1, length), F32),
            pltpu.VMEM(per_head, BF),
            pltpu.VMEM((series, 3 * HEADS, HEAD_DIM, length), BF),
            pltpu.VMEM(rows, BF),
            pltpu.VMEM(rows, F32),
            pltpu.VMEM((n_t, width, 3 * hidden), BF),
            pltpu.VMEM((series, n_t * hidden, length), BF),
            pltpu.VMEM((n_t, n_dp * share, hidden), F32),
            pltpu.VMEM((2, n_t, pairs, share, hidden), BF),
            pltpu.VMEM((n_t, pairs, share, hidden), BF),
            pltpu.VMEM((n_t, pairs, share, hidden), BF),
            pltpu.VMEM((pairs * n_t - 1, share, hidden), BF),
            pltpu.VMEM((n_dp, share, hidden), BF),
            pltpu.VMEM((width, width), F32),
            pltpu.VMEM((width, LANES), F32),
            *stages,
            *one_head,
            dma((2 * series,)), dma((n_t,)), dma((n_t,)), dma((n_t,)), dma((n_t,)), dma((6,)), dma((4,)), dma((4,)), dma((4,)), dma((6,)),
        ],
        compiler_params=pltpu.CompilerParams(vmem_limit_bytes=56 * 2**20 + landing, collective_id=0, has_side_effects=True),
    )(
        median_code, scale_code, raw, cot, qkv, out, again.reshape(1, -1), gate, up, down, mgain.reshape(1, -1), cosine, sine, source
    )


def local(
    n_dp, n_t, raw_series, median_code, scale_code, qkv_weight, out_weight, attn_gain, gate_weight, up_weight, down_weight,
    mlp_gain, cotangent,
):
    result, input_grad, qkv_grad, out_grad, again_grad, gate_grad, up_grad, down_grad, mgain_grad = hand_over(layer(
        n_dp, n_t, median_code.T, scale_code.T, raw_series.transpose(0, 1, 3, 2), cotangent.transpose(0, 1, 3, 2), qkv_weight,
        out_weight, attn_gain, gate_weight, up_weight, down_weight.T, mlp_gain,
    ))
    return (
        result.transpose(0, 1, 3, 2), input_grad.transpose(0, 1, 3, 2), qkv_grad, out_grad, again_grad[0], gate_grad, up_grad,
        down_grad.T, mgain_grad[0],
    )


def solution(mesh):
    placed = (
        P(None, ("dp", "tensor"), None, None), P(None, ("dp", "tensor")), P(None, ("dp", "tensor")), P(), P(), P(),
        P(None, "tensor"), P(None, "tensor"), P("tensor", None), P(), P(None, ("dp", "tensor"), None, None),
    )
    return jax.shard_map(
        functools.partial(local, mesh.shape["dp"], mesh.shape["tensor"]), mesh=mesh, in_specs=placed,
        out_specs=(
            P(None, ("dp", "tensor"), None, None), P(None, ("dp", "tensor"), None, None), P(), P(), P(),
            P(None, "tensor"), P(None, "tensor"), P("tensor", None), P(),
        ),
        check_vma=False,
    )
```

```python
import functools

import jax
import jax.numpy as jnp
import numpy as np
from jax import lax
from jax.experimental import pallas as pl
from jax.experimental.pallas import tpu as pltpu
from jax.sharding import PartitionSpec as P

BF = jnp.bfloat16
F32 = jnp.float32
MESH = pl.DeviceIdType.MESH
HEADS = 9
HEAD_DIM = 16
D = HEADS * HEAD_DIM
LANES = 128
GROUPS = D // 16
BLK = 256
HALF = BLK // 2
EPS = 1e-05
MASKED = -1e30
LOG2E_SCALED = 0.25 * 1.4426950408889634

STAGE1 = [(c, h) for c in range(3) for h in range(4)]
STAGE2 = [(c, h) for c in range(3) for h in range(4, 8)]
LAST = HEADS - 1
TILES = (2, 2, 2)


def mm(a, b):
    return lax.dot_general(a, b, (((1,), (0,)), ((), ())), preferred_element_type=F32)


def mm_tn(a, b):
    return lax.dot_general(a, b, (((0,), (0,)), ((), ())), preferred_element_type=F32)


def mm_nt(a, b):
    return lax.dot_general(a, b, (((1,), (1,)), ((), ())), preferred_element_type=F32)


def eye(n):
    same = lax.broadcasted_iota(jnp.int32, (n, n), 0) == lax.broadcasted_iota(jnp.int32, (n, n), 1)
    return jnp.where(same, 1.0, 0.0)


def to_column(row):
    return jnp.sum(eye(row.shape[1]) * row, axis=1, keepdims=True)


def to_row(column):
    return jnp.sum(eye(column.shape[0]) * column, axis=0, keepdims=True)


def norm_stats(rows):
    r = lax.rsqrt(jnp.mean(rows * rows, axis=0, keepdims=True) + EPS)
    return rows * r, r


def norm_backward(e, n, r, gain):
    weighted = e * gain
    mean = jnp.mean(weighted * n, axis=0, keepdims=True)
    return r * (weighted - n * mean), jnp.sum(e * n, axis=1, keepdims=True)


def rope(x, cosine, sine):
    length = x.shape[1]
    x = x.reshape(HEADS, 2, 8, length)
    a, b = x[:, 0], x[:, 1]
    first = a * cosine - b * sine
    second = a * sine + b * cosine
    return jnp.concatenate([first[:, None], second[:, None]], axis=1).reshape(HEADS, HEAD_DIM, length)


def each(first, last, body):
    if last - first <= 40:
        for k in range(first, last):
            body(k)
    else:
        pl.loop(first, last)(body)


def split(k, n):
    return divmod(k, n) if isinstance(k, int) else (k // n, lax.rem(k, n))


def ring(size, mine):
    known = [mine] + [lax.rem(mine + k, size) for k in range(1, size)] if size <= 40 else None
    return lambda k: known[k] if known and isinstance(k, int) else lax.rem(mine + k, size)


def remote(src, dst, send_sem, recv_sem, device):
    return pltpu.make_async_remote_copy(
        src_ref=src, dst_ref=dst, send_sem=send_sem, recv_sem=recv_sem, device_id=device, device_id_type=MESH
    )


class GroupSum:
    def __init__(self, index, count, to, here, other, first, stage, recv, out, sems):
        self.index, self.count, self.to, self.here, self.other, self.first = index, count, to, here, other, first
        self.stage, self.recv, self.out = stage, recv, out
        self.send, self.land, self.spread, self.gather = (sems.at[i] for i in range(4))
        self.groups = stage.shape[0]
        self.stride = max(count // self.groups, 1)
        place = lax.rem(index + count - first, count)
        self.mine = place // self.stride
        self.owner = (lax.rem(place, self.stride) == 0) & (self.mine < self.groups)

    def go(self):
        def part(g):
            owner = split(g * self.stride + self.first, self.count)[1]

            @pl.when(owner != self.index)
            def _():
                remote(self.stage.at[g], self.recv.at[self.index], self.send, self.land, self.to(owner)).start()

        each(0, self.groups, part)

    def _all_parts(self):
        others = self.recv.at[pl.ds(0, self.count - 1)]
        return remote(others, others, self.spread, self.land, self.here)

    def reduce(self):
        @pl.when(self.owner)
        def _():
            self._all_parts().wait_recv()
            self.recv[self.index] = self.stage[self.mine]
            self.out[self.mine] = jnp.sum(self.recv[...].astype(F32), axis=0).astype(BF)

            def whole(k):
                remote(self.out.at[self.mine], self.out.at[self.mine], self.spread, self.gather, self.other(k)).start()

            each(1, self.count, whole)

    def finish(self):
        def landed(n):
            stage, out = self.stage.at[pl.ds(0, n)], self.out.at[pl.ds(0, n)]
            both = remote(stage, out, self.send, self.gather, self.here)
            both.wait_recv()
            both.wait_send()

        @pl.when(self.owner)
        def _():
            if self.groups > 1:
                landed(self.groups - 1)
            self._all_parts().wait_send()

        @pl.when(jnp.logical_not(self.owner))
        def _():
            landed(self.groups)


class HeadSum:
    def __init__(self, own, pair, half, recv, total, sems, core, partner, device_of, peers):
        self.own, self.pair, self.half, self.recv, self.total = own, pair, half, recv, total
        self.sems, self.core, self.partner, self.device_of, self.peers = sems, core, partner, device_of, peers

    def _exchange(self):
        return remote(self.own.at[1 - self.core], self.pair, self.sems.at[0], self.sems.at[1], self.partner)

    def go(self, main, rest):
        main = main.astype(BF).reshape(3, 16, LANES)
        self.own[0] = main[:2]
        self.own[1, 0] = main[2]
        self.own[1, 1] = jnp.concatenate([rest, jnp.zeros((16, LANES - rest.shape[1]), F32)], axis=1).astype(BF)
        self._exchange().start()

    def send(self):
        self._exchange().wait()
        self.half[...] = (self.own[self.core].astype(F32) + self.pair[...].astype(F32)).astype(BF)
        for_peer = lambda k: remote(self.half, self.recv.at[k - 1], self.sems.at[2], self.sems.at[3], self.device_of(k)).start()
        each(1, self.peers, for_peer)

    def _back(self):
        piece = self.total.at[self.core]
        return remote(piece, piece, self.sems.at[4], self.sems.at[5], self.partner)

    def reduce(self):
        remote(self.recv, self.recv, self.sems.at[2], self.sems.at[3], self.partner).wait()
        self.total[self.core] = (self.half[...].astype(F32) + jnp.sum(self.recv[...].astype(F32), axis=0)).astype(BF)
        self._back().start()

    def finish(self):
        self._back().wait()
        turn = jnp.where(
            lax.broadcasted_iota(jnp.int32, (48, LANES), 0) == lax.broadcasted_iota(jnp.int32, (48, LANES), 1), 1.0, 0.0
        ).astype(BF)
        total = self.total[...].reshape(4, 16, LANES)
        return jnp.concatenate([mm_tn(total[:3].reshape(48, LANES), turn).astype(BF), total[3]], axis=0)


def kernel(
    n_dp, n_t,
    median_ref, scale_ref, raw_ref, cot_ref, qkv_ref, out_ref, again_ref, gate_ref, up_ref, down_ref, mgain_ref, cos_ref, sin_ref,
    source_ref,
    result_ref, igrad_ref, qkvg_ref, outg_ref, againg_ref, gateg_ref, upg_ref, downg_ref, mgaing_ref,
    e_ref, held0_ref, held1_ref, largest_ref, ds_ref, ds2_ref, dt_ref, dt2_ref, ga_ref, ga2_ref, qa_ref, q_ref, k_ref, v_ref, o_ref, linv_ref, att_ref, dproj_ref, rows_ref, scaled_ref,
    w_ref, inner_ref, ffacc_ref, ffstage_ref, ffpair_ref, ffhalf_ref, ffrecv_ref, ffout_ref, outacc_ref, gains_ref,
    stage0, recv0, out0, stage1, recv1, out1, stage2, recv2, out2, *rest,
):
    w_send, w_recv, w_send2, w_recv2, ff_sem, sems0, sems1, sems2, sems3 = rest[5:]
    held_refs = (held0_ref, held1_ref)
    series, _, _, length = raw_ref.shape
    nblk = length // BLK
    hidden_local = gate_ref.shape[1]
    count = n_dp * n_t
    my_dp, my_t = lax.axis_index("dp"), lax.axis_index("tensor")
    index = my_dp * n_t + my_t
    core = lax.rem(my_dp, 2)
    pair = my_dp // 2
    partner = (my_dp + 1 - 2 * core, my_t)
    pairs = n_dp // 2

    here = (my_dp, my_t)
    on_dp, on_t, on_pair = ring(n_dp, my_dp), ring(n_t, my_t), ring(pairs, pair)

    def to(device):
        return split(device, n_t)

    def other(k):
        along_dp, along_t = split(k, n_t)
        return on_dp(along_dp), on_t(along_t)

    barrier = pltpu.get_barrier_semaphore()

    def greet(k):
        pl.semaphore_signal(barrier, inc=1, device_id=other(k), device_id_type=MESH)

    each(1, count, greet)

    cosine, sine = cos_ref[...], sin_ref[...]
    again, mgain = to_column(again_ref[...]), to_column(mgain_ref[...])

    def spread_inverse(s):
        return 1.0 / jnp.full((1, length), scale_ref[0, s].astype(F32) * 0.25, F32)

    def scaled_series(s):
        return (raw_ref[s, 0].astype(F32) - median_ref[0, s].astype(F32) * 0.05) * spread_inverse(s)

    tail_rows = lax.broadcasted_iota(jnp.int32, (HEAD_DIM, length), 0)
    w_ref[0, :, :hidden_local] = gate_ref[...]
    w_ref[0, :, hidden_local : 2 * hidden_local] = up_ref[...]
    w_ref[0, :, 2 * hidden_local :] = down_ref[...]

    @pl.loop(0, series)
    def _(s):
        scaled = scaled_series(s)
        scaled_ref[s] = scaled
        n, _ = norm_stats(scaled)
        rows = (n * again).astype(BF)
        rows_ref[s] = rows
        projected = mm_tn(qkv_ref[...], rows)
        queries = rope(projected[:D], cosine, sine).astype(BF)
        keys = rope(projected[D : 2 * D], cosine, sine).astype(BF)
        values = projected[2 * D :].reshape(HEADS, HEAD_DIM, length).astype(BF)
        q_ref[s] = queries
        k_ref[s] = keys
        wide = queries.astype(F32) * LOG2E_SCALED
        high = wide.astype(BF)
        qa_ref[s, :, :HEAD_DIM] = high
        qa_ref[s, :, HEAD_DIM:] = (wide - high.astype(F32)).astype(BF)
        v_ref[s, :, :HEAD_DIM] = values
        ones = jnp.where(tail_rows < 2, 1.0, 0.0).astype(BF)
        v_ref[s, :, HEAD_DIM:] = jnp.broadcast_to(ones[None], (HEADS, HEAD_DIM, length))

    cut = 16 * ((GROUPS + 1) // 2)

    def half_rows(which, body):
        for c, (lo, hi) in enumerate(((0, cut), (cut, D))):
            @pl.when(core == (c if which == 0 else 1 - c))
            def _():
                body(pl.ds(lo, hi - lo))

    def over_links(k, rows):
        device = (my_dp, on_t(k))
        return remote(w_ref.at[0, rows], w_ref.at[k, rows], w_send.at[k], w_recv.at[k], device)

    def within_pair(k, rows):
        return remote(w_ref.at[k, rows], w_ref.at[k, rows], w_send2.at[k], w_recv2.at[k], partner)

    def send_weights():
        pl.semaphore_wait(barrier, count - 1)

        def start(rows):
            for k in range(1, n_t):
                over_links(k, rows).start()

        half_rows(0, start)

    def exchange_weights():
        def forward(rows):
            for k in range(1, n_t):
                over_links(k, rows).wait()
                within_pair(k, rows).start()

        half_rows(0, forward)

    def finish_weights():
        def sent(rows):
            for k in range(1, n_t):
                within_pair(k, rows).wait_send()

        def landed(rows):
            for k in range(1, n_t):
                within_pair(k, rows).wait_recv()

        half_rows(0, sent)
        half_rows(1, landed)

    up_allowed = lax.broadcasted_iota(jnp.int32, (HALF, BLK), 0) <= lax.broadcasted_iota(jnp.int32, (HALF, BLK), 1)
    side = lax.broadcasted_iota(jnp.int32, (HALF, BLK), 1)
    side = jnp.where(side < HALF, side, side - HALF)
    side_allowed = lax.broadcasted_iota(jnp.int32, (HALF, BLK), 0) <= side

    def bounds(j):
        return j * BLK, j * BLK + HALF, (j + 1) * BLK

    def segments(j):
        _, mid, _ = bounds(j)
        at = BLK * j * (j - 1) + (BLK + HALF) * j
        return slice(at, at + mid), slice(at + mid, at + 2 * mid), slice(at + 2 * mid, at + 2 * mid + HALF)

    def key_segments(i):
        rest = length - bounds(i)[1]
        at = sum(2 * (length - bounds(k)[1]) + HALF for k in range(i))
        return slice(at, at + rest), slice(at + rest, at + 2 * rest), slice(at + 2 * rest, at + 2 * rest + HALF)

    def turn_to_keys(j, own, shared, target):
        lo, mid, _ = bounds(j)
        main = key_segments(j)
        for s in range(2):
            for i in range(j):
                at = key_segments(i)[s].start + lo - bounds(i)[1]
                target[at : at + BLK] = own[s][i * BLK : (i + 1) * BLK].T
            turned = own[s][lo:mid].T
            target[main[2], halves(s)] = turned[:HALF]
            at = main[s].start
            target[at : at + HALF, halves(0)] = turned[HALF:]
            target[at : at + HALF, halves(1)] = shared[:, halves(s)].T

    def turn_to_queries(i, own, shared, target):
        lo, mid, hi = bounds(i)
        main = segments(i)
        for s in range(2):
            turned = own[s][:HALF].T
            at = main[s].start + lo
            target[at : at + HALF, halves(1)] = turned[:HALF]
            target[main[2], halves(s)] = turned[HALF:]
            target[at : at + HALF, halves(0)] = shared[:, halves(s)].T
            for j in range(i + 1, nblk):
                at = segments(j)[s].start + lo
                first = bounds(j)[0] - mid
                target[at : at + BLK] = own[s][first : first + BLK].T

    def halves(s):
        return slice(s * HALF, (s + 1) * HALF)

    def side_by_side(a, b):
        zero = jnp.zeros_like(a)
        return jnp.concatenate([jnp.concatenate([a, zero], axis=1), jnp.concatenate([zero, b], axis=1)], axis=0)

    def score(h, j):
        lo, mid, hi = bounds(j)
        held = held_refs[j % 2]
        keys = [jnp.concatenate([k_ref[s, h], k_ref[s, h]], axis=0) for s in range(2)]
        queries = [qa_ref[s, h, :, lo:hi] for s in range(2)]
        shared = mm_tn(
            jnp.concatenate([keys[s][:, mid:hi] for s in range(2)], axis=0),
            side_by_side(queries[0][:, HALF:], queries[1][:, HALF:]),
        )
        shared = jnp.where(side_allowed, shared, MASKED)
        held[2 * mid : 2 * mid + HALF] = shared
        shared_largest = jnp.max(shared, axis=0, keepdims=True)
        for s in range(2):
            scores = mm_tn(keys[s][:, :mid], queries[s])
            diagonal = jnp.where(up_allowed, scores[lo:], MASKED)
            scores = jnp.concatenate([scores[:lo], diagonal], axis=0) if j else diagonal
            held[s * mid : (s + 1) * mid] = scores
            top = jnp.max(scores, axis=0, keepdims=True)
            right = jnp.maximum(top[:, HALF:], shared_largest[:, halves(s)])
            largest_ref[j % 2, s : s + 1] = jnp.concatenate([top[:, :HALF], right], axis=1)

    def softmax(h, j, target):
        lo, mid, hi = bounds(j)
        held = held_refs[j % 2]
        largest = [largest_ref[j % 2, s : s + 1] for s in range(2)]
        weights = [jnp.exp2(held[s * mid : (s + 1) * mid] - largest[s]) for s in range(2)]
        side_largest = jnp.concatenate([largest[0][:, HALF:], largest[1][:, HALF:]], axis=1)
        weights.append(jnp.exp2(held[2 * mid : 2 * mid + HALF] - side_largest))
        shared_total = jnp.sum(weights[2], axis=0, keepdims=True)
        for s in range(2):
            total = jnp.sum(weights[s], axis=0, keepdims=True)
            total = jnp.concatenate([total[:, :HALF], total[:, HALF:] + shared_total[:, halves(s)]], axis=1)
            linv_ref[s, h, :, lo:hi] = 1.0 / total
        weights = [e.astype(BF) for e in weights]
        for rows, e in zip(segments(j), weights, strict=True):
            target[rows] = e
        turn_to_keys(j, weights[:2], weights[2], e_ref.at[h])

    def from_segments(j, left, source):
        _, mid, hi = bounds(j)
        segs = segments(j)
        shared = mm(jnp.concatenate([left[s][:, mid:hi] for s in range(2)], axis=0), source[segs[2]])
        out = []
        for s in range(2):
            own = mm(left[s][:, :mid], source[segs[s]])
            right = own[:, HALF:] + shared[s * HEAD_DIM : (s + 1) * HEAD_DIM, halves(s)]
            out.append(jnp.concatenate([own[:, :HALF], right], axis=1))
        return out

    def mix(h, j, source):
        lo, _, hi = bounds(j)
        mixed = from_segments(j, [v_ref[s, h, :HEAD_DIM] for s in range(2)], source)
        for s in range(2):
            attended = mixed[s] * linv_ref[s, h, :, lo:hi]
            o_ref[s, h, :, lo:hi] = attended
            att_ref[s, h, :, lo:hi] = attended.astype(BF)

    score(0, 0)
    for j in range(1, nblk):
        score(0, j)
        softmax(0, j - 1, ds_ref)

    def step(h, now, before):
        for j in range(nblk):
            score(h, j)
            if j:
                softmax(h, j - 1, now)
            else:
                softmax(h - 1, nblk - 1, before)
            mix(h - 1, j, before)

    @pl.loop(1, HEADS, step=2)
    def _(h):
        step(h, ds2_ref, ds_ref)
        step(h + 1, ds_ref, ds2_ref)

        @pl.when(h == 1)
        def _():
            send_weights()

        @pl.when(h == 5)
        def _():
            exchange_weights()

    finish_weights()
    softmax(HEADS - 1, nblk - 1, ds_ref)
    for j in range(nblk):
        mix(HEADS - 1, j, ds_ref)

    ffacc_ref[...] = jnp.zeros_like(ffacc_ref)
    outacc_ref[...] = jnp.zeros_like(outacc_ref)
    gains_ref[...] = jnp.zeros_like(gains_ref)

    def feed_forward(s):
        attended = att_ref[s].reshape(D, length)
        hidden = scaled_ref[s] + mm_tn(out_ref[...], attended)
        n, r = norm_stats(hidden)
        rows = (n * mgain).astype(BF)
        low = cot_ref[s, 0]
        top = low.astype(F32)
        scaled_ref[s] = hidden
        grad_rows = jnp.zeros((D, length), F32)
        for t in range(n_t):
            gu = w_ref[t, :, : 2 * hidden_local]
            down = w_ref[t, :, 2 * hidden_local :]
            both = mm_tn(gu, rows)
            gate, up = both[:hidden_local], both[hidden_local:]
            grad_inner = mm_tn(down, low)
            sigma = 1.0 / (1.0 + jnp.exp(-gate))
            act = gate * sigma
            inner = (act * up).astype(BF)
            inner_ref[s, t * hidden_local : (t + 1) * hidden_local] = inner
            grad_gate = (grad_inner * up * (sigma + act * (1.0 - sigma))).astype(BF)
            grad_up = (grad_inner * act).astype(BF)
            grad_both = jnp.concatenate([grad_gate, grad_up], axis=0)
            grad_rows = grad_rows + mm(gu, grad_both)
            gu_piece = mm_nt(rows, grad_both)
            ffacc_ref[t, :D] += gu_piece[:, :hidden_local]
            ffacc_ref[t, D : 2 * D] += gu_piece[:, hidden_local:]

        down_piece = mm_nt(low, inner_ref[s])
        for t in range(n_t):
            ffacc_ref[t, 2 * D : 3 * D] += down_piece[:, t * hidden_local : (t + 1) * hidden_local]
        part, gain_part = norm_backward(grad_rows, n, r, mgain)
        grad_hidden = top + part
        igrad_ref[s, 0] = grad_hidden
        branch = grad_hidden.astype(BF)
        outacc_ref[...] += mm_nt(attended, branch)
        gains_ref[:, 0:1] += gain_part
        att_ref[s] = mm(out_ref[...], branch).astype(BF).reshape(HEADS, HEAD_DIM, length)

    for s in range(series):
        feed_forward(s)

    share = ffout_ref.shape[1]
    for t in range(n_t):
        staged = ffacc_ref[t].astype(BF).reshape(pairs, 2, share, hidden_local)
        for c in range(2):
            ffstage_ref[c, t] = staged[:, c]
    peers = pairs * n_t

    def ff_pair():
        return remote(ffstage_ref.at[1 - core], ffpair_ref, ff_sem.at[0], ff_sem.at[1], partner)

    ff_pair().start()

    def ff_send():
        ff_pair().wait()
        ffhalf_ref[...] = (ffstage_ref[core].astype(F32) + ffpair_ref[...].astype(F32)).astype(BF)

        def part(k):
            along_pair, along_t = split(k, n_t)
            peer_pair = on_pair(along_pair)
            piece = ffhalf_ref.at[split(n_t - along_t, n_t)[1], peer_pair]
            remote(piece, ffrecv_ref.at[k - 1], ff_sem.at[2], ff_sem.at[3], (2 * peer_pair + core, on_t(along_t))).start()

        each(1, peers, part)

    def ff_parts():
        return remote(ffrecv_ref, ffrecv_ref, ff_sem.at[2], ff_sem.at[3], here)

    def ff_reduce():
        ff_parts().wait_recv()
        total = ffhalf_ref[0, pair].astype(F32) + jnp.sum(ffrecv_ref[...].astype(F32), axis=0)
        ffout_ref[my_dp] = total.astype(BF)

        def whole(k):
            device = (on_dp(k), my_t)
            remote(ffout_ref.at[my_dp], ffout_ref.at[my_dp], ff_sem.at[4], ff_sem.at[5], device).start()

        each(1, n_dp, whole)

    def ff_finish():
        ff_parts().wait_send()
        others = ffout_ref.at[pl.ds(0, n_dp - 1)]
        remote(others, others, ff_sem.at[4], ff_sem.at[5], here).wait()
        sums = ffout_ref[...].astype(F32).reshape(-1, hidden_local)
        gateg_ref[...] = sums[:D]
        upg_ref[...] = sums[D : 2 * D]
        downg_ref[...] = sums[2 * D : 3 * D]

    sum0 = GroupSum(index, count, to, here, other, 0, stage0, recv0, out0, sems0)
    sum1 = GroupSum(index, count, to, here, other, count - 18, stage1, recv1, out1, sems1)
    sum2 = GroupSum(index, count, to, here, other, 7, stage2, recv2, out2, sems2)

    def head_grads(parts):
        total = None
        for s in range(series):
            grads = jnp.concatenate([dproj_ref[s, c * HEADS + h] for c, h in parts], axis=0)
            piece = mm_nt(rows_ref[s], grads)
            total = piece if total is None else total + piece
        spare = -total.shape[1] % LANES
        return jnp.concatenate([total, jnp.zeros((D, spare), F32)], axis=1)

    def put(stage, grads):
        for t in range(grads.shape[1] // LANES):
            tile = grads[:, t * LANES : (t + 1) * LANES].astype(BF)
            stage[t * GROUPS : (t + 1) * GROUPS] = tile.reshape(GROUPS, 16, LANES)


    def device_of(k):
        along_pair, along_t = split(k, n_t)
        return (2 * on_pair(along_pair) + core, on_t(along_t))

    sum3 = HeadSum(*rest[:5], sems3, core, partner, device_of, peers)

    def one_head_grads(h):
        main, rest = None, None
        for s in range(series):
            grads = jnp.concatenate([dproj_ref[s, c * HEADS + h] for c in range(3)], axis=0)
            one, two = mm_nt(grads, rows_ref[s, :LANES]), mm_nt(rows_ref[s, LANES:], grads)
            main, rest = (one, two) if main is None else (main + one, rest + two)
        return main, rest

    put(stage0, jnp.concatenate([outacc_ref[...], gains_ref[:, : 2 * LANES - D]], axis=1))
    sum0.go()

    def prepare(h, grad_ref):
        for s in range(2):
            grad = (att_ref[s, h].astype(F32) * linv_ref[s, h]).astype(BF)
            delta = -jnp.sum(grad.astype(F32) * o_ref[s, h], axis=0, keepdims=True)
            high = delta.astype(BF).astype(F32)
            tail = jnp.where(tail_rows == 0, high, jnp.where(tail_rows == 1, delta - high, 0.0))
            grad_ref[s, :HEAD_DIM] = grad
            grad_ref[s, HEAD_DIM:] = tail.astype(BF)

    def center(h, i, grad_ref, target, turned):
        lo, mid, hi = bounds(i)
        segs = key_segments(i)
        values = [v_ref[s, h] for s in range(2)]
        shared = mm_tn(
            jnp.concatenate([grad_ref[s, :, lo:mid] for s in range(2)], axis=0),
            side_by_side(values[0][:, lo:mid], values[1][:, lo:mid]),
        )
        shared = shared.astype(BF) * e_ref[h, segs[2]]
        target[segs[2]] = shared
        own = []
        for s in range(2):
            centred = mm_tn(grad_ref[s, :, mid:], values[s][:, lo:hi])
            own.append(centred.astype(BF) * e_ref[h, segs[s]])
            target[segs[s]] = own[s]
        turn_to_queries(i, own, shared, turned)

    def from_key_segments(i, left, source):
        lo, mid, _ = bounds(i)
        segs = key_segments(i)
        shared = mm(jnp.concatenate([left[s][:, lo:mid] for s in range(2)], axis=0), source[segs[2]])
        out = []
        for s in range(2):
            own = mm(left[s][:, mid:], source[segs[s]])
            first = own[:, :HALF] + shared[s * HEAD_DIM : (s + 1) * HEAD_DIM, halves(s)]
            out.append(jnp.concatenate([first, own[:, HALF:]], axis=1))
        return out

    def unrotate(g, lo, hi):
        a, b = g[:8], g[8:]
        c, d = cosine[:, lo:hi], sine[:, lo:hi]
        return jnp.concatenate([a * c + b * d, b * c - a * d], axis=0)

    def products(h, source, turned, grad_ref, between):
        queries = [q_ref[s, h] for s in range(2)]
        grads = [grad_ref[s, :HEAD_DIM] for s in range(2)]
        keys = [k_ref[s, h] for s in range(2)]
        for j in range(nblk):
            between(j)
            lo, _, hi = bounds(j)
            for s, g in enumerate(from_key_segments(j, grads, e_ref.at[h])):
                dproj_ref[s, 2 * HEADS + h, :, lo:hi] = g.astype(BF)
            for s, g in enumerate(from_key_segments(j, queries, source)):
                dproj_ref[s, HEADS + h, :, lo:hi] = unrotate(g * 0.25, lo, hi).astype(BF)
            for s, g in enumerate(from_segments(nblk - 1 - j, keys, turned)):
                lo, _, hi = bounds(nblk - 1 - j)
                dproj_ref[s, h, :, lo:hi] = unrotate(g * 0.25, lo, hi).astype(BF)

    prepare(0, ga_ref)
    for j in range(nblk):
        center(0, j, ga_ref, ds_ref, dt_ref)
    ff_send()

    def step_back(h, source, turned, grad_ref, next_source, next_turned, next_grad_ref):
        prepare(h + 1, next_grad_ref)
        products(h, source, turned, grad_ref, lambda j: center(h + 1, j, next_grad_ref, next_source, next_turned))

    even, odd = (ds_ref, dt_ref, ga_ref), (ds2_ref, dt2_ref, ga2_ref)

    @pl.loop(0, HEADS - 3, step=2)
    def _(h):
        step_back(h, *even, *odd)
        step_back(h + 1, *odd, *even)

        @pl.when(h == 2)
        def _():
            put(stage1, head_grads(STAGE1))
            sum1.go()

        @pl.when(h == 4)
        def _():
            ff_reduce()
            sum0.reduce()

    step_back(HEADS - 3, *even, *odd)
    sum1.reduce()
    prepare(HEADS - 1, ga_ref)
    products(HEADS - 2, *odd, lambda j: center(HEADS - 1, j, ga_ref, ds_ref, dt_ref) if j >= 2 else None)
    put(stage2, head_grads(STAGE2))
    sum2.go()
    for j in range(2):
        center(HEADS - 1, j, ga_ref, ds_ref, dt_ref)
    products(HEADS - 1, *even, lambda j: None)
    sum3.go(*one_head_grads(LAST))

    def back(s):
        grad = dproj_ref[s].reshape(3 * D, length)
        grad_rows = mm(qkv_ref[...], grad)
        n, r = norm_stats(scaled_series(s))
        part, _ = norm_backward(grad_rows, n, r, again)
        igrad_ref[s, 0] = (igrad_ref[s, 0] + part) * spread_inverse(s)

    for s in range(series):
        back(s)
        if s == 0:
            sum3.send()
    down_wide = jnp.concatenate([w_ref[t, :, 2 * hidden_local :] for t in range(n_t)], axis=1)
    for s in range(series):
        result_ref[s, 0] = (scaled_ref[s] + mm(down_wide, inner_ref[s])).astype(BF)

    sum2.reduce()
    ff_finish()
    sum0.finish()
    sum1.finish()
    fixed = sum(TILES) * LANES
    place_of = jnp.where(
        lax.broadcasted_iota(jnp.int32, (fixed + LANES, source_ref.shape[1]), 0) == source_ref[...], 1.0, 0.0
    ).astype(BF)

    def tiles_of(out, n):
        return [out[t * GROUPS : (t + 1) * GROUPS].reshape(D, LANES) for t in range(n)]

    tiles = tiles_of(out0, TILES[0]) + tiles_of(out1, TILES[1])
    mgaing_ref[...] = to_row(tiles[1][:, D - LANES : D - LANES + 1].astype(F32))
    before = sum(TILES[:2]) * LANES
    sums = mm(jnp.concatenate(tiles, axis=1), place_of[:before])
    outg_ref[...] = sums[:, 4 * LANES : 4 * LANES + D]
    sum3.reduce()
    sum2.finish()
    sums = sums[:, : 3 * D] + mm(jnp.concatenate(tiles_of(out2, TILES[2]), axis=1), place_of[before:fixed, : 3 * D])
    sums = sums + mm(sum3.finish(), place_of[fixed:, : 3 * D])
    qkvg_ref[...] = sums
    againg_ref[...] = to_row(jnp.sum(sums * qkv_ref[...].astype(F32), axis=1, keepdims=True) / again)


def rope_tables(length):
    half = HEAD_DIM // 2
    frequency = np.float32(10000.0) ** (-(np.arange(half, dtype=np.float32) * np.float32(2.0) / np.float32(HEAD_DIM)))
    angles = np.arange(length, dtype=np.float32)[None, :] * frequency.astype(np.float32)[:, None]
    return np.cos(angles).astype(np.float32), np.sin(angles).astype(np.float32)


def column_sources():
    source = np.full((1, 4 * LANES + D), -1, np.int32)
    source[0, 4 * LANES :] = np.arange(D)
    first = TILES[0] * LANES
    last = [(c, LAST) for c in range(3)]
    for parts, tiles in zip((STAGE1, STAGE2, last), TILES[1:] + (1,), strict=True):
        for place, (c, h) in enumerate(parts):
            at = c * D + h * HEAD_DIM
            source[0, at : at + HEAD_DIM] = first + place * HEAD_DIM + np.arange(HEAD_DIM)
        first += tiles * LANES
    return source


def copy_kernel(n, *refs):
    sems = refs[2 * n]
    copies = [pltpu.make_async_copy(refs[i], refs[n + i], sems.at[i]) for i in range(n)]
    for copy in copies:
        copy.start()
    for copy in copies:
        copy.wait()


def hand_over(arrays):
    n = len(arrays)
    return pl.pallas_call(
        functools.partial(copy_kernel, n),
        out_shape=[jax.ShapeDtypeStruct(a.shape, a.dtype) for a in arrays],
        in_specs=[pl.BlockSpec(memory_space=pltpu.VMEM)] * n,
        out_specs=[pl.BlockSpec(memory_space=pltpu.HBM)] * n,
        scratch_shapes=[pltpu.SemaphoreType.DMA((n,))],
    )(*[pltpu.with_memory_space_constraint(a, pltpu.VMEM) for a in arrays])


def layer(n_dp, n_t, median_code, scale_code, raw, cot, qkv, out, again, gate, up, down, mgain):
    series, _, width, length = raw.shape
    cosine, sine = rope_tables(length)
    source = column_sources()
    blocks = length // BLK
    packed = BLK * blocks * (blocks - 1) + (BLK + HALF) * blocks
    vmem = pl.BlockSpec(memory_space=pltpu.VMEM)
    smem = pl.BlockSpec(memory_space=pltpu.SMEM)
    per_head = (series, HEADS, HEAD_DIM, length)
    rows = (series, width, length)
    count = n_dp * n_t
    pairs = n_dp // 2
    hidden = gate.shape[1]
    share = -(-3 * width // (16 * n_dp)) * 16
    dma = pltpu.SemaphoreType.DMA
    landing = 2 * LANES * (len(TILES) * count * 16 + (pairs * n_t - 1) * (share + 32))
    stages = []
    for n in TILES:
        stages += [
            pltpu.VMEM((n * GROUPS, 16, LANES), BF), pltpu.VMEM((count, 16, LANES), BF), pltpu.VMEM((n * GROUPS, 16, LANES), BF),
        ]
    half = (2, 16, LANES)
    one_head = [pltpu.VMEM(shape, BF) for shape in ((2,) + half, half, half, (pairs * n_t - 1,) + half, (2,) + half)]
    return pl.pallas_call(
        functools.partial(kernel, n_dp, n_t),
        out_shape=[
            pltpu.VMEM(raw.shape, BF),
            pltpu.VMEM(raw.shape, F32),
            pltpu.VMEM((width, 3 * width), F32),
            pltpu.VMEM((width, width), F32),
            pltpu.VMEM((1, width), F32),
            pltpu.VMEM((width, hidden), F32),
            pltpu.VMEM((width, hidden), F32),
            pltpu.VMEM((width, hidden), F32),
            pltpu.VMEM((1, width), F32),
        ],
        in_specs=[smem, smem] + [vmem] * 12,
        out_specs=[vmem] * 9,
        scratch_shapes=[
            pltpu.VMEM((HEADS, packed, BLK), BF),
            pltpu.VMEM((2 * length - 2 * BLK - HALF, BLK), F32),
            pltpu.VMEM((2 * length - HALF, BLK), F32),
            pltpu.VMEM((2, 2, BLK), F32),
            pltpu.VMEM((packed, BLK), BF),
            pltpu.VMEM((packed, BLK), BF),
            pltpu.VMEM((packed, BLK), BF),
            pltpu.VMEM((packed, BLK), BF),
            pltpu.VMEM((series, 2 * HEAD_DIM, length), BF),
            pltpu.VMEM((series, 2 * HEAD_DIM, length), BF),
            pltpu.VMEM((series, HEADS, 2 * HEAD_DIM, length), BF),
            pltpu.VMEM(per_head, BF),
            pltpu.VMEM(per_head, BF),
            pltpu.VMEM((series, HEADS, 2 * HEAD_DIM, length), BF),
            pltpu.VMEM(per_head, F32),
            pltpu.VMEM((series, HEADS, 1, length), F32),
            pltpu.VMEM(per_head, BF),
            pltpu.VMEM((series, 3 * HEADS, HEAD_DIM, length), BF),
            pltpu.VMEM(rows, BF),
            pltpu.VMEM(rows, F32),
            pltpu.VMEM((n_t, width, 3 * hidden), BF),
            pltpu.VMEM((series, n_t * hidden, length), BF),
            pltpu.VMEM((n_t, n_dp * share, hidden), F32),
            pltpu.VMEM((2, n_t, pairs, share, hidden), BF),
            pltpu.VMEM((n_t, pairs, share, hidden), BF),
            pltpu.VMEM((n_t, pairs, share, hidden), BF),
            pltpu.VMEM((pairs * n_t - 1, share, hidden), BF),
            pltpu.VMEM((n_dp, share, hidden), BF),
            pltpu.VMEM((width, width), F32),
            pltpu.VMEM((width, LANES), F32),
            *stages,
            *one_head,
            dma((n_t,)), dma((n_t,)), dma((n_t,)), dma((n_t,)), dma((6,)), dma((4,)), dma((4,)), dma((4,)), dma((6,)),
        ],
        compiler_params=pltpu.CompilerParams(vmem_limit_bytes=57 * 2**20 + landing, collective_id=0, has_side_effects=True),
    )(
        median_code, scale_code, raw, cot, qkv, out, again.reshape(1, -1), gate, up, down, mgain.reshape(1, -1), cosine, sine, source
    )


def local(
    n_dp, n_t, raw_series, median_code, scale_code, qkv_weight, out_weight, attn_gain, gate_weight, up_weight, down_weight,
    mlp_gain, cotangent,
):
    result, input_grad, qkv_grad, out_grad, again_grad, gate_grad, up_grad, down_grad, mgain_grad = hand_over(layer(
        n_dp, n_t, median_code.T, scale_code.T, raw_series.transpose(0, 1, 3, 2), cotangent.transpose(0, 1, 3, 2), qkv_weight,
        out_weight, attn_gain, gate_weight, up_weight, down_weight.T, mlp_gain,
    ))
    return (
        result.transpose(0, 1, 3, 2), input_grad.transpose(0, 1, 3, 2), qkv_grad, out_grad, again_grad[0], gate_grad, up_grad,
        down_grad.T, mgain_grad[0],
    )


def solution(mesh):
    placed = (
        P(None, ("dp", "tensor"), None, None), P(None, ("dp", "tensor")), P(None, ("dp", "tensor")), P(), P(), P(),
        P(None, "tensor"), P(None, "tensor"), P("tensor", None), P(), P(None, ("dp", "tensor"), None, None),
    )
    return jax.shard_map(
        functools.partial(local, mesh.shape["dp"], mesh.shape["tensor"]), mesh=mesh, in_specs=placed,
        out_specs=(
            P(None, ("dp", "tensor"), None, None), P(None, ("dp", "tensor"), None, None), P(), P(), P(),
            P(None, "tensor"), P(None, "tensor"), P("tensor", None), P(),
        ),
        check_vma=False,
    )
```

```python
import functools

import jax
import jax.numpy as jnp
import numpy as np
from jax import lax
from jax.experimental import pallas as pl
from jax.experimental.pallas import tpu as pltpu
from jax.sharding import PartitionSpec as P

BF = jnp.bfloat16
F32 = jnp.float32
MESH = pl.DeviceIdType.MESH
HEADS = 9
HEAD_DIM = 16
D = HEADS * HEAD_DIM
LANES = 128
GROUPS = D // 16
BLK = 256
HALF = BLK // 2
EPS = 1e-05
MASKED = -1e30
LOG2E_SCALED = 0.25 * 1.4426950408889634

STAGE1 = [(c, h) for c in range(3) for h in range(4)]
STAGE2 = [(c, h) for c in range(3) for h in range(4, 8)]
LAST = HEADS - 1
TILES = (2, 2, 2)


def mm(a, b):
    return lax.dot_general(a, b, (((1,), (0,)), ((), ())), preferred_element_type=F32)


def mm_tn(a, b):
    return lax.dot_general(a, b, (((0,), (0,)), ((), ())), preferred_element_type=F32)


def mm_nt(a, b):
    return lax.dot_general(a, b, (((1,), (1,)), ((), ())), preferred_element_type=F32)


def eye(n):
    same = lax.broadcasted_iota(jnp.int32, (n, n), 0) == lax.broadcasted_iota(jnp.int32, (n, n), 1)
    return jnp.where(same, 1.0, 0.0)


def to_column(row):
    return jnp.sum(eye(row.shape[1]) * row, axis=1, keepdims=True)


def to_row(column):
    return jnp.sum(eye(column.shape[0]) * column, axis=0, keepdims=True)


def norm_stats(rows):
    r = lax.rsqrt(jnp.mean(rows * rows, axis=0, keepdims=True) + EPS)
    return rows * r, r


def norm_backward(e, n, r, gain):
    weighted = e * gain
    mean = jnp.mean(weighted * n, axis=0, keepdims=True)
    return r * (weighted - n * mean), jnp.sum(e * n, axis=1, keepdims=True)


def rope(x, cosine, sine):
    length = x.shape[1]
    x = x.reshape(HEADS, 2, 8, length)
    a, b = x[:, 0], x[:, 1]
    first = a * cosine - b * sine
    second = a * sine + b * cosine
    return jnp.concatenate([first[:, None], second[:, None]], axis=1).reshape(HEADS, HEAD_DIM, length)


def each(first, last, body):
    if last - first <= 40:
        for k in range(first, last):
            body(k)
    else:
        pl.loop(first, last)(body)


def split(k, n):
    return divmod(k, n) if isinstance(k, int) else (k // n, lax.rem(k, n))


def ring(size, mine):
    known = [mine] + [lax.rem(mine + k, size) for k in range(1, size)] if size <= 40 else None
    return lambda k: known[k] if known and isinstance(k, int) else lax.rem(mine + k, size)


def remote(src, dst, send_sem, recv_sem, device):
    return pltpu.make_async_remote_copy(
        src_ref=src, dst_ref=dst, send_sem=send_sem, recv_sem=recv_sem, device_id=device, device_id_type=MESH
    )


class GroupSum:
    def __init__(self, index, count, to, here, other, first, stage, recv, out, sems):
        self.index, self.count, self.to, self.here, self.other, self.first = index, count, to, here, other, first
        self.stage, self.recv, self.out = stage, recv, out
        self.send, self.land, self.spread, self.gather = (sems.at[i] for i in range(4))
        self.groups = stage.shape[0]
        self.stride = max(count // self.groups, 1)
        place = lax.rem(index + count - first, count)
        self.mine = place // self.stride
        self.owner = (lax.rem(place, self.stride) == 0) & (self.mine < self.groups)

    def go(self):
        def part(g):
            owner = split(g * self.stride + self.first, self.count)[1]

            @pl.when(owner != self.index)
            def _():
                remote(self.stage.at[g], self.recv.at[self.index], self.send, self.land, self.to(owner)).start()

        each(0, self.groups, part)

    def _all_parts(self):
        others = self.recv.at[pl.ds(0, self.count - 1)]
        return remote(others, others, self.spread, self.land, self.here)

    def reduce(self):
        @pl.when(self.owner)
        def _():
            self._all_parts().wait_recv()
            self.recv[self.index] = self.stage[self.mine]
            self.out[self.mine] = jnp.sum(self.recv[...].astype(F32), axis=0).astype(BF)

            def whole(k):
                remote(self.out.at[self.mine], self.out.at[self.mine], self.spread, self.gather, self.other(k)).start()

            each(1, self.count, whole)

    def finish(self):
        def landed(n):
            stage, out = self.stage.at[pl.ds(0, n)], self.out.at[pl.ds(0, n)]
            both = remote(stage, out, self.send, self.gather, self.here)
            both.wait_recv()
            both.wait_send()

        @pl.when(self.owner)
        def _():
            if self.groups > 1:
                landed(self.groups - 1)
            self._all_parts().wait_send()

        @pl.when(jnp.logical_not(self.owner))
        def _():
            landed(self.groups)


class HeadSum:
    def __init__(self, own, pair, half, recv, total, sems, core, partner, device_of, peers):
        self.own, self.pair, self.half, self.recv, self.total = own, pair, half, recv, total
        self.sems, self.core, self.partner, self.device_of, self.peers = sems, core, partner, device_of, peers

    def _exchange(self):
        return remote(self.own.at[1 - self.core], self.pair, self.sems.at[0], self.sems.at[1], self.partner)

    def go(self, main, rest):
        main = main.astype(BF).reshape(3, 16, LANES)
        self.own[0] = main[:2]
        self.own[1, 0] = main[2]
        self.own[1, 1] = jnp.concatenate([rest, jnp.zeros((16, LANES - rest.shape[1]), F32)], axis=1).astype(BF)
        self._exchange().start()

    def send(self):
        self._exchange().wait()
        self.half[...] = (self.own[self.core].astype(F32) + self.pair[...].astype(F32)).astype(BF)
        for_peer = lambda k: remote(self.half, self.recv.at[k - 1], self.sems.at[2], self.sems.at[3], self.device_of(k)).start()
        each(1, self.peers, for_peer)

    def _back(self):
        piece = self.total.at[self.core]
        return remote(piece, piece, self.sems.at[4], self.sems.at[5], self.partner)

    def reduce(self):
        remote(self.recv, self.recv, self.sems.at[2], self.sems.at[3], self.partner).wait()
        self.total[self.core] = (self.half[...].astype(F32) + jnp.sum(self.recv[...].astype(F32), axis=0)).astype(BF)
        self._back().start()

    def finish(self):
        self._back().wait()
        turn = jnp.where(
            lax.broadcasted_iota(jnp.int32, (48, LANES), 0) == lax.broadcasted_iota(jnp.int32, (48, LANES), 1), 1.0, 0.0
        ).astype(BF)
        total = self.total[...].reshape(4, 16, LANES)
        return jnp.concatenate([mm_tn(total[:3].reshape(48, LANES), turn).astype(BF), total[3]], axis=0)


def kernel(
    n_dp, n_t,
    median_ref, scale_ref, raw_ref, cot_ref, qkv_ref, out_ref, again_ref, gate_ref, up_ref, down_ref, mgain_ref, cos_ref, sin_ref,
    source_ref,
    result_ref, igrad_ref, qkvg_ref, outg_ref, againg_ref, gateg_ref, upg_ref, downg_ref, mgaing_ref,
    e_ref, held0_ref, held1_ref, largest_ref, ds_ref, ds2_ref, dt_ref, dt2_ref, ga_ref, ga2_ref, qa_ref, q_ref, k_ref, v_ref, o_ref, linv_ref, att_ref, dproj_ref, rows_ref, scaled_ref,
    w_ref, inner_ref, ffacc_ref, ffstage_ref, ffpair_ref, ffhalf_ref, ffrecv_ref, ffout_ref, outacc_ref, gains_ref,
    stage0, recv0, out0, stage1, recv1, out1, stage2, recv2, out2, *rest,
):
    w_send, w_recv, w_send2, w_recv2, ff_sem, sems0, sems1, sems2, sems3 = rest[5:]
    held_refs = (held0_ref, held1_ref)
    series, _, _, length = raw_ref.shape
    nblk = length // BLK
    hidden_local = gate_ref.shape[1]
    count = n_dp * n_t
    my_dp, my_t = lax.axis_index("dp"), lax.axis_index("tensor")
    index = my_dp * n_t + my_t
    core = lax.rem(my_dp, 2)
    pair = my_dp // 2
    partner = (my_dp + 1 - 2 * core, my_t)
    pairs = n_dp // 2

    here = (my_dp, my_t)
    on_dp, on_t, on_pair = ring(n_dp, my_dp), ring(n_t, my_t), ring(pairs, pair)

    def to(device):
        return split(device, n_t)

    def other(k):
        along_dp, along_t = split(k, n_t)
        return on_dp(along_dp), on_t(along_t)

    barrier = pltpu.get_barrier_semaphore()

    def greet(k):
        pl.semaphore_signal(barrier, inc=1, device_id=other(k), device_id_type=MESH)

    each(1, count, greet)

    cosine, sine = cos_ref[...], sin_ref[...]
    again, mgain = to_column(again_ref[...]), to_column(mgain_ref[...])

    def spread_inverse(s):
        return 1.0 / jnp.full((1, length), scale_ref[0, s].astype(F32) * 0.25, F32)

    def scaled_series(s):
        return (raw_ref[s, 0].astype(F32) - median_ref[0, s].astype(F32) * 0.05) * spread_inverse(s)

    tail_rows = lax.broadcasted_iota(jnp.int32, (HEAD_DIM, length), 0)
    w_ref[0, :, :hidden_local] = gate_ref[...]
    w_ref[0, :, hidden_local : 2 * hidden_local] = up_ref[...]
    w_ref[0, :, 2 * hidden_local :] = down_ref[...]

    def project(s):
        scaled = scaled_series(s)
        scaled_ref[s] = scaled
        n, _ = norm_stats(scaled)
        rows = (n * again).astype(BF)
        rows_ref[s] = rows
        projected = mm_tn(qkv_ref[...], rows)
        queries = rope(projected[:D], cosine, sine).astype(BF)
        keys = rope(projected[D : 2 * D], cosine, sine).astype(BF)
        values = projected[2 * D :].reshape(HEADS, HEAD_DIM, length).astype(BF)
        q_ref[s] = queries
        k_ref[s] = keys
        wide = queries.astype(F32) * LOG2E_SCALED
        high = wide.astype(BF)
        qa_ref[s, :, :HEAD_DIM] = high
        qa_ref[s, :, HEAD_DIM:] = (wide - high.astype(F32)).astype(BF)
        v_ref[s, :, :HEAD_DIM] = values
        ones = jnp.where(tail_rows < 2, 1.0, 0.0).astype(BF)
        v_ref[s, :, HEAD_DIM:] = jnp.broadcast_to(ones[None], (HEADS, HEAD_DIM, length))

    for s in range(series):
        project(s)

    cut = 16 * ((GROUPS + 1) // 2)

    def half_rows(which, body):
        for c, (lo, hi) in enumerate(((0, cut), (cut, D))):
            @pl.when(core == (c if which == 0 else 1 - c))
            def _():
                body(pl.ds(lo, hi - lo))

    def over_links(k, rows):
        device = (my_dp, on_t(k))
        return remote(w_ref.at[0, rows], w_ref.at[k, rows], w_send.at[k], w_recv.at[k], device)

    def within_pair(k, rows):
        return remote(w_ref.at[k, rows], w_ref.at[k, rows], w_send2.at[k], w_recv2.at[k], partner)

    def send_weights():
        pl.semaphore_wait(barrier, count - 1)

        def start(rows):
            for k in range(1, n_t):
                over_links(k, rows).start()

        half_rows(0, start)

    def exchange_weights():
        def forward(rows):
            for k in range(1, n_t):
                over_links(k, rows).wait()
                within_pair(k, rows).start()

        half_rows(0, forward)

    def finish_weights():
        def sent(rows):
            for k in range(1, n_t):
                within_pair(k, rows).wait_send()

        def landed(rows):
            for k in range(1, n_t):
                within_pair(k, rows).wait_recv()

        half_rows(0, sent)
        half_rows(1, landed)

    up_allowed = lax.broadcasted_iota(jnp.int32, (HALF, BLK), 0) <= lax.broadcasted_iota(jnp.int32, (HALF, BLK), 1)
    side = lax.broadcasted_iota(jnp.int32, (HALF, BLK), 1)
    side = jnp.where(side < HALF, side, side - HALF)
    side_allowed = lax.broadcasted_iota(jnp.int32, (HALF, BLK), 0) <= side

    def bounds(j):
        return j * BLK, j * BLK + HALF, (j + 1) * BLK

    def segments(j):
        _, mid, _ = bounds(j)
        at = BLK * j * (j - 1) + (BLK + HALF) * j
        return slice(at, at + mid), slice(at + mid, at + 2 * mid), slice(at + 2 * mid, at + 2 * mid + HALF)

    def key_segments(i):
        rest = length - bounds(i)[1]
        at = sum(2 * (length - bounds(k)[1]) + HALF for k in range(i))
        return slice(at, at + rest), slice(at + rest, at + 2 * rest), slice(at + 2 * rest, at + 2 * rest + HALF)

    def turn_to_keys(j, own, shared, target):
        lo, mid, _ = bounds(j)
        main = key_segments(j)
        for s in range(2):
            for i in range(j):
                at = key_segments(i)[s].start + lo - bounds(i)[1]
                target[at : at + BLK] = own[s][i * BLK : (i + 1) * BLK].T
            turned = own[s][lo:mid].T
            target[main[2], halves(s)] = turned[:HALF]
            at = main[s].start
            target[at : at + HALF, halves(0)] = turned[HALF:]
            target[at : at + HALF, halves(1)] = shared[:, halves(s)].T

    def turn_to_queries(i, own, shared, target):
        lo, mid, hi = bounds(i)
        main = segments(i)
        for s in range(2):
            turned = own[s][:HALF].T
            at = main[s].start + lo
            target[at : at + HALF, halves(1)] = turned[:HALF]
            target[main[2], halves(s)] = turned[HALF:]
            target[at : at + HALF, halves(0)] = shared[:, halves(s)].T
            for j in range(i + 1, nblk):
                at = segments(j)[s].start + lo
                first = bounds(j)[0] - mid
                target[at : at + BLK] = own[s][first : first + BLK].T

    def halves(s):
        return slice(s * HALF, (s + 1) * HALF)

    def side_by_side(a, b):
        zero = jnp.zeros_like(a)
        return jnp.concatenate([jnp.concatenate([a, zero], axis=1), jnp.concatenate([zero, b], axis=1)], axis=0)

    def score(h, j):
        lo, mid, hi = bounds(j)
        held = held_refs[j % 2]
        keys = [jnp.concatenate([k_ref[s, h], k_ref[s, h]], axis=0) for s in range(2)]
        queries = [qa_ref[s, h, :, lo:hi] for s in range(2)]
        shared = mm_tn(
            jnp.concatenate([keys[s][:, mid:hi] for s in range(2)], axis=0),
            side_by_side(queries[0][:, HALF:], queries[1][:, HALF:]),
        )
        shared = jnp.where(side_allowed, shared, MASKED)
        held[2 * mid : 2 * mid + HALF] = shared
        shared_largest = jnp.max(shared, axis=0, keepdims=True)
        for s in range(2):
            scores = mm_tn(keys[s][:, :mid], queries[s])
            diagonal = jnp.where(up_allowed, scores[lo:], MASKED)
            scores = jnp.concatenate([scores[:lo], diagonal], axis=0) if j else diagonal
            held[s * mid : (s + 1) * mid] = scores
            top = jnp.max(scores, axis=0, keepdims=True)
            right = jnp.maximum(top[:, HALF:], shared_largest[:, halves(s)])
            largest_ref[j % 2, s : s + 1] = jnp.concatenate([top[:, :HALF], right], axis=1)

    def softmax(h, j, target):
        lo, mid, hi = bounds(j)
        held = held_refs[j % 2]
        largest = [largest_ref[j % 2, s : s + 1] for s in range(2)]
        weights = [jnp.exp2(held[s * mid : (s + 1) * mid] - largest[s]) for s in range(2)]
        side_largest = jnp.concatenate([largest[0][:, HALF:], largest[1][:, HALF:]], axis=1)
        weights.append(jnp.exp2(held[2 * mid : 2 * mid + HALF] - side_largest))
        shared_total = jnp.sum(weights[2], axis=0, keepdims=True)
        for s in range(2):
            total = jnp.sum(weights[s], axis=0, keepdims=True)
            total = jnp.concatenate([total[:, :HALF], total[:, HALF:] + shared_total[:, halves(s)]], axis=1)
            linv_ref[s, h, :, lo:hi] = 1.0 / total
        weights = [e.astype(BF) for e in weights]
        for rows, e in zip(segments(j), weights, strict=True):
            target[rows] = e
        turn_to_keys(j, weights[:2], weights[2], e_ref.at[h])

    def from_segments(j, left, source):
        _, mid, hi = bounds(j)
        segs = segments(j)
        shared = mm(jnp.concatenate([left[s][:, mid:hi] for s in range(2)], axis=0), source[segs[2]])
        out = []
        for s in range(2):
            own = mm(left[s][:, :mid], source[segs[s]])
            right = own[:, HALF:] + shared[s * HEAD_DIM : (s + 1) * HEAD_DIM, halves(s)]
            out.append(jnp.concatenate([own[:, :HALF], right], axis=1))
        return out

    def mix(h, j, source):
        lo, _, hi = bounds(j)
        mixed = from_segments(j, [v_ref[s, h, :HEAD_DIM] for s in range(2)], source)
        for s in range(2):
            attended = mixed[s] * linv_ref[s, h, :, lo:hi]
            o_ref[s, h, :, lo:hi] = attended
            att_ref[s, h, :, lo:hi] = attended.astype(BF)

    score(0, 0)
    for j in range(1, nblk):
        score(0, j)
        softmax(0, j - 1, ds_ref)

    def step(h, now, before):
        for j in range(nblk):
            score(h, j)
            if j:
                softmax(h, j - 1, now)
            else:
                softmax(h - 1, nblk - 1, before)
            mix(h - 1, j, before)

    @pl.loop(1, HEADS, step=2)
    def _(h):
        step(h, ds2_ref, ds_ref)
        step(h + 1, ds_ref, ds2_ref)

        @pl.when(h == 1)
        def _():
            send_weights()

        @pl.when(h == 5)
        def _():
            exchange_weights()

    finish_weights()
    softmax(HEADS - 1, nblk - 1, ds_ref)
    for j in range(nblk):
        mix(HEADS - 1, j, ds_ref)

    ffacc_ref[...] = jnp.zeros_like(ffacc_ref)
    outacc_ref[...] = jnp.zeros_like(outacc_ref)
    gains_ref[...] = jnp.zeros_like(gains_ref)

    def feed_forward(s):
        attended = att_ref[s].reshape(D, length)
        hidden = scaled_ref[s] + mm_tn(out_ref[...], attended)
        n, r = norm_stats(hidden)
        rows = (n * mgain).astype(BF)
        low = cot_ref[s, 0]
        top = low.astype(F32)
        scaled_ref[s] = hidden
        grad_rows = jnp.zeros((D, length), F32)
        for t in range(n_t):
            gu = w_ref[t, :, : 2 * hidden_local]
            down = w_ref[t, :, 2 * hidden_local :]
            both = mm_tn(gu, rows)
            gate, up = both[:hidden_local], both[hidden_local:]
            grad_inner = mm_tn(down, low)
            sigma = 1.0 / (1.0 + jnp.exp(-gate))
            act = gate * sigma
            inner = (act * up).astype(BF)
            inner_ref[s, t * hidden_local : (t + 1) * hidden_local] = inner
            grad_gate = (grad_inner * up * (sigma + act * (1.0 - sigma))).astype(BF)
            grad_up = (grad_inner * act).astype(BF)
            grad_both = jnp.concatenate([grad_gate, grad_up], axis=0)
            grad_rows = grad_rows + mm(gu, grad_both)
            gu_piece = mm_nt(rows, grad_both)
            ffacc_ref[t, :D] += gu_piece[:, :hidden_local]
            ffacc_ref[t, D : 2 * D] += gu_piece[:, hidden_local:]

        down_piece = mm_nt(low, inner_ref[s])
        for t in range(n_t):
            ffacc_ref[t, 2 * D : 3 * D] += down_piece[:, t * hidden_local : (t + 1) * hidden_local]
        part, gain_part = norm_backward(grad_rows, n, r, mgain)
        grad_hidden = top + part
        igrad_ref[s, 0] = grad_hidden
        branch = grad_hidden.astype(BF)
        outacc_ref[...] += mm_nt(attended, branch)
        gains_ref[:, 0:1] += gain_part
        att_ref[s] = mm(out_ref[...], branch).astype(BF).reshape(HEADS, HEAD_DIM, length)

    for s in range(series):
        feed_forward(s)

    share = ffout_ref.shape[1]
    for t in range(n_t):
        staged = ffacc_ref[t].astype(BF).reshape(pairs, 2, share, hidden_local)
        for c in range(2):
            ffstage_ref[c, t] = staged[:, c]
    peers = pairs * n_t

    def ff_pair():
        return remote(ffstage_ref.at[1 - core], ffpair_ref, ff_sem.at[0], ff_sem.at[1], partner)

    ff_pair().start()

    def ff_send():
        ff_pair().wait()
        ffhalf_ref[...] = (ffstage_ref[core].astype(F32) + ffpair_ref[...].astype(F32)).astype(BF)

        def part(k):
            along_pair, along_t = split(k, n_t)
            peer_pair = on_pair(along_pair)
            piece = ffhalf_ref.at[split(n_t - along_t, n_t)[1], peer_pair]
            remote(piece, ffrecv_ref.at[k - 1], ff_sem.at[2], ff_sem.at[3], (2 * peer_pair + core, on_t(along_t))).start()

        each(1, peers, part)

    def ff_parts():
        return remote(ffrecv_ref, ffrecv_ref, ff_sem.at[2], ff_sem.at[3], here)

    def ff_reduce():
        ff_parts().wait_recv()
        total = ffhalf_ref[0, pair].astype(F32) + jnp.sum(ffrecv_ref[...].astype(F32), axis=0)
        ffout_ref[my_dp] = total.astype(BF)

        def whole(k):
            device = (on_dp(k), my_t)
            remote(ffout_ref.at[my_dp], ffout_ref.at[my_dp], ff_sem.at[4], ff_sem.at[5], device).start()

        each(1, n_dp, whole)

    def ff_finish():
        ff_parts().wait_send()
        others = ffout_ref.at[pl.ds(0, n_dp - 1)]
        remote(others, others, ff_sem.at[4], ff_sem.at[5], here).wait()
        sums = ffout_ref[...].astype(F32).reshape(-1, hidden_local)
        gateg_ref[...] = sums[:D]
        upg_ref[...] = sums[D : 2 * D]
        downg_ref[...] = sums[2 * D : 3 * D]

    sum0 = GroupSum(index, count, to, here, other, 0, stage0, recv0, out0, sems0)
    sum1 = GroupSum(index, count, to, here, other, count - 18, stage1, recv1, out1, sems1)
    sum2 = GroupSum(index, count, to, here, other, 7, stage2, recv2, out2, sems2)

    def head_grads(parts):
        total = None
        for s in range(series):
            grads = jnp.concatenate([dproj_ref[s, c * HEADS + h] for c, h in parts], axis=0)
            piece = mm_nt(rows_ref[s], grads)
            total = piece if total is None else total + piece
        spare = -total.shape[1] % LANES
        return jnp.concatenate([total, jnp.zeros((D, spare), F32)], axis=1)

    def put(stage, grads):
        for t in range(grads.shape[1] // LANES):
            tile = grads[:, t * LANES : (t + 1) * LANES].astype(BF)
            stage[t * GROUPS : (t + 1) * GROUPS] = tile.reshape(GROUPS, 16, LANES)


    def device_of(k):
        along_pair, along_t = split(k, n_t)
        return (2 * on_pair(along_pair) + core, on_t(along_t))

    sum3 = HeadSum(*rest[:5], sems3, core, partner, device_of, peers)

    def one_head_grads(h):
        main, rest = None, None
        for s in range(series):
            grads = jnp.concatenate([dproj_ref[s, c * HEADS + h] for c in range(3)], axis=0)
            one, two = mm_nt(grads, rows_ref[s, :LANES]), mm_nt(rows_ref[s, LANES:], grads)
            main, rest = (one, two) if main is None else (main + one, rest + two)
        return main, rest


    def prepare(h, grad_ref):
        for s in range(2):
            grad = (att_ref[s, h].astype(F32) * linv_ref[s, h]).astype(BF)
            delta = -jnp.sum(grad.astype(F32) * o_ref[s, h], axis=0, keepdims=True)
            high = delta.astype(BF).astype(F32)
            tail = jnp.where(tail_rows == 0, high, jnp.where(tail_rows == 1, delta - high, 0.0))
            grad_ref[s, :HEAD_DIM] = grad
            grad_ref[s, HEAD_DIM:] = tail.astype(BF)

    def center(h, i, grad_ref, target, turned):
        lo, mid, hi = bounds(i)
        segs = key_segments(i)
        values = [v_ref[s, h] for s in range(2)]
        shared = mm_tn(
            jnp.concatenate([grad_ref[s, :, lo:mid] for s in range(2)], axis=0),
            side_by_side(values[0][:, lo:mid], values[1][:, lo:mid]),
        )
        shared = shared.astype(BF) * e_ref[h, segs[2]]
        target[segs[2]] = shared
        own = []
        for s in range(2):
            centred = mm_tn(grad_ref[s, :, mid:], values[s][:, lo:hi])
            own.append(centred.astype(BF) * e_ref[h, segs[s]])
            target[segs[s]] = own[s]
        turn_to_queries(i, own, shared, turned)

    def from_key_segments(i, left, source):
        lo, mid, _ = bounds(i)
        segs = key_segments(i)
        shared = mm(jnp.concatenate([left[s][:, lo:mid] for s in range(2)], axis=0), source[segs[2]])
        out = []
        for s in range(2):
            own = mm(left[s][:, mid:], source[segs[s]])
            first = own[:, :HALF] + shared[s * HEAD_DIM : (s + 1) * HEAD_DIM, halves(s)]
            out.append(jnp.concatenate([first, own[:, HALF:]], axis=1))
        return out

    def unrotate(g, lo, hi):
        a, b = g[:8], g[8:]
        c, d = cosine[:, lo:hi], sine[:, lo:hi]
        return jnp.concatenate([a * c + b * d, b * c - a * d], axis=0)

    def products(h, source, turned, grad_ref, between):
        queries = [q_ref[s, h] for s in range(2)]
        grads = [grad_ref[s, :HEAD_DIM] for s in range(2)]
        keys = [k_ref[s, h] for s in range(2)]
        for j in range(nblk):
            between(j)
            lo, _, hi = bounds(j)
            for s, g in enumerate(from_key_segments(j, grads, e_ref.at[h])):
                dproj_ref[s, 2 * HEADS + h, :, lo:hi] = g.astype(BF)
            for s, g in enumerate(from_key_segments(j, queries, source)):
                dproj_ref[s, HEADS + h, :, lo:hi] = unrotate(g * 0.25, lo, hi).astype(BF)
            for s, g in enumerate(from_segments(nblk - 1 - j, keys, turned)):
                lo, _, hi = bounds(nblk - 1 - j)
                dproj_ref[s, h, :, lo:hi] = unrotate(g * 0.25, lo, hi).astype(BF)

    prepare(0, ga_ref)
    for j in range(nblk):
        center(0, j, ga_ref, ds_ref, dt_ref)
    put(stage0, jnp.concatenate([outacc_ref[...], gains_ref[:, : 2 * LANES - D]], axis=1))
    sum0.go()
    ff_send()

    def step_back(h, source, turned, grad_ref, next_source, next_turned, next_grad_ref):
        prepare(h + 1, next_grad_ref)
        products(h, source, turned, grad_ref, lambda j: center(h + 1, j, next_grad_ref, next_source, next_turned))

    even, odd = (ds_ref, dt_ref, ga_ref), (ds2_ref, dt2_ref, ga2_ref)

    @pl.loop(0, HEADS - 3, step=2)
    def _(h):
        step_back(h, *even, *odd)
        step_back(h + 1, *odd, *even)

        @pl.when(h == 2)
        def _():
            put(stage1, head_grads(STAGE1))
            sum1.go()

        @pl.when(h == 4)
        def _():
            ff_reduce()
            sum0.reduce()

    step_back(HEADS - 3, *even, *odd)
    sum1.reduce()
    prepare(HEADS - 1, ga_ref)
    products(HEADS - 2, *odd, lambda j: center(HEADS - 1, j, ga_ref, ds_ref, dt_ref) if j >= 2 else None)
    put(stage2, head_grads(STAGE2))
    sum2.go()
    for j in range(2):
        center(HEADS - 1, j, ga_ref, ds_ref, dt_ref)
    products(HEADS - 1, *even, lambda j: None)
    sum3.go(*one_head_grads(LAST))

    def back(s):
        grad = dproj_ref[s].reshape(3 * D, length)
        grad_rows = mm(qkv_ref[...], grad)
        n, r = norm_stats(scaled_series(s))
        part, _ = norm_backward(grad_rows, n, r, again)
        igrad_ref[s, 0] = (igrad_ref[s, 0] + part) * spread_inverse(s)

    for s in range(series):
        back(s)
        if s == 0:
            sum3.send()
    down_wide = jnp.concatenate([w_ref[t, :, 2 * hidden_local :] for t in range(n_t)], axis=1)
    for s in range(series):
        result_ref[s, 0] = (scaled_ref[s] + mm(down_wide, inner_ref[s])).astype(BF)

    sum2.reduce()
    ff_finish()
    sum0.finish()
    sum1.finish()
    fixed = sum(TILES) * LANES
    place_of = jnp.where(
        lax.broadcasted_iota(jnp.int32, (fixed + LANES, source_ref.shape[1]), 0) == source_ref[...], 1.0, 0.0
    ).astype(BF)

    def tiles_of(out, n):
        return [out[t * GROUPS : (t + 1) * GROUPS].reshape(D, LANES) for t in range(n)]

    tiles = tiles_of(out0, TILES[0]) + tiles_of(out1, TILES[1])
    mgaing_ref[...] = to_row(tiles[1][:, D - LANES : D - LANES + 1].astype(F32))
    before = sum(TILES[:2]) * LANES
    sums = mm(jnp.concatenate(tiles, axis=1), place_of[:before])
    outg_ref[...] = sums[:, 4 * LANES : 4 * LANES + D]
    sum3.reduce()
    sum2.finish()
    sums = sums[:, : 3 * D] + mm(jnp.concatenate(tiles_of(out2, TILES[2]), axis=1), place_of[before:fixed, : 3 * D])
    sums = sums + mm(sum3.finish(), place_of[fixed:, : 3 * D])
    qkvg_ref[...] = sums
    againg_ref[...] = to_row(jnp.sum(sums * qkv_ref[...].astype(F32), axis=1, keepdims=True) / again)


def rope_tables(length):
    half = HEAD_DIM // 2
    frequency = np.float32(10000.0) ** (-(np.arange(half, dtype=np.float32) * np.float32(2.0) / np.float32(HEAD_DIM)))
    angles = np.arange(length, dtype=np.float32)[None, :] * frequency.astype(np.float32)[:, None]
    return np.cos(angles).astype(np.float32), np.sin(angles).astype(np.float32)


def column_sources():
    source = np.full((1, 4 * LANES + D), -1, np.int32)
    source[0, 4 * LANES :] = np.arange(D)
    first = TILES[0] * LANES
    last = [(c, LAST) for c in range(3)]
    for parts, tiles in zip((STAGE1, STAGE2, last), TILES[1:] + (1,), strict=True):
        for place, (c, h) in enumerate(parts):
            at = c * D + h * HEAD_DIM
            source[0, at : at + HEAD_DIM] = first + place * HEAD_DIM + np.arange(HEAD_DIM)
        first += tiles * LANES
    return source


def copy_kernel(n, *refs):
    sems = refs[2 * n]
    copies = [pltpu.make_async_copy(refs[i], refs[n + i], sems.at[i]) for i in range(n)]
    for copy in copies:
        copy.start()
    for copy in copies:
        copy.wait()


def hand_over(arrays):
    n = len(arrays)
    return pl.pallas_call(
        functools.partial(copy_kernel, n),
        out_shape=[jax.ShapeDtypeStruct(a.shape, a.dtype) for a in arrays],
        in_specs=[pl.BlockSpec(memory_space=pltpu.VMEM)] * n,
        out_specs=[pl.BlockSpec(memory_space=pltpu.HBM)] * n,
        scratch_shapes=[pltpu.SemaphoreType.DMA((n,))],
    )(*[pltpu.with_memory_space_constraint(a, pltpu.VMEM) for a in arrays])


def layer(n_dp, n_t, median_code, scale_code, raw, cot, qkv, out, again, gate, up, down, mgain):
    series, _, width, length = raw.shape
    cosine, sine = rope_tables(length)
    source = column_sources()
    blocks = length // BLK
    packed = BLK * blocks * (blocks - 1) + (BLK + HALF) * blocks
    vmem = pl.BlockSpec(memory_space=pltpu.VMEM)
    smem = pl.BlockSpec(memory_space=pltpu.SMEM)
    per_head = (series, HEADS, HEAD_DIM, length)
    rows = (series, width, length)
    count = n_dp * n_t
    pairs = n_dp // 2
    hidden = gate.shape[1]
    share = -(-3 * width // (16 * n_dp)) * 16
    dma = pltpu.SemaphoreType.DMA
    landing = 2 * LANES * (len(TILES) * count * 16 + (pairs * n_t - 1) * (share + 32))
    stages = []
    for n in TILES:
        stages += [
            pltpu.VMEM((n * GROUPS, 16, LANES), BF), pltpu.VMEM((count, 16, LANES), BF), pltpu.VMEM((n * GROUPS, 16, LANES), BF),
        ]
    half = (2, 16, LANES)
    one_head = [pltpu.VMEM(shape, BF) for shape in ((2,) + half, half, half, (pairs * n_t - 1,) + half, (2,) + half)]
    return pl.pallas_call(
        functools.partial(kernel, n_dp, n_t),
        out_shape=[
            pltpu.VMEM(raw.shape, BF),
            pltpu.VMEM(raw.shape, F32),
            pltpu.VMEM((width, 3 * width), F32),
            pltpu.VMEM((width, width), F32),
            pltpu.VMEM((1, width), F32),
            pltpu.VMEM((width, hidden), F32),
            pltpu.VMEM((width, hidden), F32),
            pltpu.VMEM((width, hidden), F32),
            pltpu.VMEM((1, width), F32),
        ],
        in_specs=[smem, smem] + [vmem] * 12,
        out_specs=[vmem] * 9,
        scratch_shapes=[
            pltpu.VMEM((HEADS, packed, BLK), BF),
            pltpu.VMEM((2 * length - 2 * BLK - HALF, BLK), F32),
            pltpu.VMEM((2 * length - HALF, BLK), F32),
            pltpu.VMEM((2, 2, BLK), F32),
            pltpu.VMEM((packed, BLK), BF),
            pltpu.VMEM((packed, BLK), BF),
            pltpu.VMEM((packed, BLK), BF),
            pltpu.VMEM((packed, BLK), BF),
            pltpu.VMEM((series, 2 * HEAD_DIM, length), BF),
            pltpu.VMEM((series, 2 * HEAD_DIM, length), BF),
            pltpu.VMEM((series, HEADS, 2 * HEAD_DIM, length), BF),
            pltpu.VMEM(per_head, BF),
            pltpu.VMEM(per_head, BF),
            pltpu.VMEM((series, HEADS, 2 * HEAD_DIM, length), BF),
            pltpu.VMEM(per_head, F32),
            pltpu.VMEM((series, HEADS, 1, length), F32),
            pltpu.VMEM(per_head, BF),
            pltpu.VMEM((series, 3 * HEADS, HEAD_DIM, length), BF),
            pltpu.VMEM(rows, BF),
            pltpu.VMEM(rows, F32),
            pltpu.VMEM((n_t, width, 3 * hidden), BF),
            pltpu.VMEM((series, n_t * hidden, length), BF),
            pltpu.VMEM((n_t, n_dp * share, hidden), F32),
            pltpu.VMEM((2, n_t, pairs, share, hidden), BF),
            pltpu.VMEM((n_t, pairs, share, hidden), BF),
            pltpu.VMEM((n_t, pairs, share, hidden), BF),
            pltpu.VMEM((pairs * n_t - 1, share, hidden), BF),
            pltpu.VMEM((n_dp, share, hidden), BF),
            pltpu.VMEM((width, width), F32),
            pltpu.VMEM((width, LANES), F32),
            *stages,
            *one_head,
            dma((n_t,)), dma((n_t,)), dma((n_t,)), dma((n_t,)), dma((6,)), dma((4,)), dma((4,)), dma((4,)), dma((6,)),
        ],
        compiler_params=pltpu.CompilerParams(vmem_limit_bytes=57 * 2**20 + landing, collective_id=0, has_side_effects=True),
    )(
        median_code, scale_code, raw, cot, qkv, out, again.reshape(1, -1), gate, up, down, mgain.reshape(1, -1), cosine, sine, source
    )


def local(
    n_dp, n_t, raw_series, median_code, scale_code, qkv_weight, out_weight, attn_gain, gate_weight, up_weight, down_weight,
    mlp_gain, cotangent,
):
    result, input_grad, qkv_grad, out_grad, again_grad, gate_grad, up_grad, down_grad, mgain_grad = hand_over(layer(
        n_dp, n_t, median_code.T, scale_code.T, raw_series.transpose(0, 1, 3, 2), cotangent.transpose(0, 1, 3, 2), qkv_weight,
        out_weight, attn_gain, gate_weight, up_weight, down_weight.T, mlp_gain,
    ))
    return (
        result.transpose(0, 1, 3, 2), input_grad.transpose(0, 1, 3, 2), qkv_grad, out_grad, again_grad[0], gate_grad, up_grad,
        down_grad.T, mgain_grad[0],
    )


def solution(mesh):
    placed = (
        P(None, ("dp", "tensor"), None, None), P(None, ("dp", "tensor")), P(None, ("dp", "tensor")), P(), P(), P(),
        P(None, "tensor"), P(None, "tensor"), P("tensor", None), P(), P(None, ("dp", "tensor"), None, None),
    )
    return jax.shard_map(
        functools.partial(local, mesh.shape["dp"], mesh.shape["tensor"]), mesh=mesh, in_specs=placed,
        out_specs=(
            P(None, ("dp", "tensor"), None, None), P(None, ("dp", "tensor"), None, None), P(), P(), P(),
            P(None, "tensor"), P(None, "tensor"), P("tensor", None), P(),
        ),
        check_vma=False,
    )
```
